128 devices in a mesh: seg: 4 (over y), node: 32 (over x, z, core).
Axes of the slice: x: 4, y: 4, z: 4, core: 2. Of those that a mesh axis runs over, the one named last changes fastest.
Arguments:
- memory_base: bfloat16 [8192, 512], P('node'), may hold values from -1 to 1
- messages: bfloat16 [4, 8192, 512], P('seg', 'node'), may hold values from -6 to 6
- touched: int32 [4, 8192], P('seg', 'node'), may hold values 0 or 1
- gru_input: bfloat16 [512, 1536], replicated, may hold values from -0.25 to 0.25
- gru_state: bfloat16 [512, 1536], replicated, may hold values from -0.25 to 0.25
- attn_weights: bfloat16 [4, 512, 512], replicated, may hold values from -0.25 to 0.25
- frequency: float32 [512], replicated, may hold values from 0.001 to 1
- request_rows: int32 [4, 32, 256], P('seg', 'node'), may hold values from 0 to 255
- event_slots: int32 [4, 8192, 9], P('seg', 'node'), may hold values from 0 to 255
- delays: int32 [4, 8192, 8], P('seg', 'node'), may hold values from 0 to 999
- upstream: bfloat16 [4, 8192, 512], P('seg', 'node'), may hold values from -6 to 6
Outputs:
- embedded: bfloat16 [4, 8192, 512], P('seg', 'node')
- memory_out: bfloat16 [4, 8192, 512], P('seg', 'node')
- memory_grad: float32 [4, 8192, 512], P('seg', 'node')
- weight_grad: float32 [4, 512, 512], replicated
The draws below stay inside these ranges and needn't reach their ends.
Inputs may be any that keep to these rules, and one draw needn't show every extreme that they name: `request_rows`: a row within one owner. `event_slots`: a slot of the event's own block.
All inputs are finite; a program needn't handle non-finite values. No bound on the sum of `touched` on one device may be relied on, other than what follows from the above.
Results may differ from the reference program's by a relative error of at most 0.01.
Values may be sent and summed in bfloat16 or wider, within the bound.
No kernel may reach another device: no remote copies, remote signals or barrier semaphores. Data moves between devices by JAX's collectives and lax.ppermute only.
A program may use at most 128 MiB of HBM per device.

```python
import math
import jax
import jax.numpy as jnp
import numpy as np
from jax import lax

DM = 512
HEADS = 2
K = 8
E_DEV = 256
NODES_DEV = 256
CAP = 8
SEG = 4
NODES = 8192
EVENTS = 8192
SLOTS = 256
N_NODE = 32


def set_ends(array, own_key, low, high):
    dims = array.shape
    index_at = [jax.random.randint(jax.random.fold_in(own_key, axis), (), 0, dims[axis]) for axis in range(len(dims))]
    array = array.at[tuple(index_at)].set(low)
    longest = dims.index(max(dims))
    index_at[longest] = (index_at[longest] + 1) % dims[longest]
    return array.at[tuple(index_at)].set(high)


def level_of(own_key, dims, split, least, top_value):
    def one(position, parts):
        steps = jax.random.uniform(jax.random.fold_in(jax.random.fold_in(own_key, 6), position), (parts,), jnp.float32, least / len(split), top_value / len(split))
        return jnp.repeat(jnp.exp(steps), dims[position] // parts).reshape((-1,) + (1,) * (len(dims) - position - 1))

    factor_of = one(*split[0])
    for cut in split[1:]:
        factor_of = factor_of * one(*cut)
    return factor_of


def rank_table(amount, slope):
    portions = [(1 << 20) // math.isqrt(standing ** slope) + 1 for standing in range(1, amount + 1)]
    scale = 1 + sum(portions) // (1 << 30)
    return np.cumsum(np.array([max(1, weight // scale) for weight in portions]))


def skewed_ids(rng, dims, count, slope):
    grid = rank_table(count, slope)
    ticket = jax.random.randint(jax.random.fold_in(rng, 1), dims, 0, int(grid[count - 1]))
    standing = jnp.searchsorted(jnp.asarray(grid, jnp.int32), ticket, side="right")
    return jax.random.permutation(jax.random.fold_in(rng, 2), count)[standing].astype(jnp.int32)


def centred(rng, extent, deviation, limit, split=(), kind=jnp.bfloat16):
    values = jax.random.normal(rng, extent, jnp.float32) * deviation
    if len(split) > 0:
        values = level_of(rng, extent, split, -0.22, 0.18) * values
    return jnp.clip(values, min=-limit, max=limit).astype(kind)


def setup_inputs(seed: int = 0) -> dict:
    key_of = jax.random.split(jax.random.key(seed), 12)
    memory_base = jnp.clip(jax.random.uniform(key_of[0], (NODES, DM), jnp.float32, -1.0, 1.0) * level_of(key_of[0], (NODES, DM), ((0, 32),), -0.4, 0.0), -1.0, 1.0).astype(jnp.bfloat16)
    messages = centred(key_of[1], (SEG, NODES, DM), 1.0, 6.0, ((0, 4), (1, 32)))
    touched = set_ends((jax.random.randint(key_of[2], (SEG, NODES), 0, 2) < 1).astype(jnp.int32), jax.random.fold_in(key_of[2], 1), 0, 1)
    gru_input = centred(key_of[3], (DM, 3 * DM), DM ** -0.5, 0.25)
    gru_state = centred(key_of[4], (DM, 3 * DM), DM ** -0.5, 0.25)
    attn_weights = centred(key_of[5], (4, DM, DM), DM ** -0.5, 0.25)
    frequency = jnp.clip(jnp.exp(jax.random.uniform(key_of[6], (DM,), jnp.float32, math.log(0.001), math.log(1.0))), 0.001, 1.0)
    request_rows = set_ends(jax.random.randint(key_of[7], (SEG, N_NODE, SLOTS), 0, NODES_DEV), jax.random.fold_in(key_of[7], 1), 0, NODES_DEV - 1).astype(jnp.int32)
    event_slots = set_ends(skewed_ids(key_of[8], (SEG, EVENTS, K + 1), SLOTS, 2), jax.random.fold_in(key_of[8], 3), 0, SLOTS - 1).astype(jnp.int32)
    delays = set_ends(jax.random.randint(key_of[9], (SEG, EVENTS, K), 0, 1000), jax.random.fold_in(key_of[9], 1), 0, 999).astype(jnp.int32)
    upstream = centred(key_of[10], (SEG, EVENTS, DM), 1.0, 6.0, ((0, 4), (1, 32)))
    return dict(memory_base=memory_base, messages=messages, touched=touched, gru_input=gru_input, gru_state=gru_state, attn_weights=attn_weights, frequency=frequency, request_rows=request_rows, event_slots=event_slots, delays=delays, upstream=upstream)


def gru_update(message, state, w_input, w_state):
    width = state.shape[1]
    from_msg = jnp.dot(message, w_input, preferred_element_type=jnp.float32)
    from_state = jnp.dot(state, w_state, preferred_element_type=jnp.float32)
    update = jax.nn.sigmoid(from_msg[:, :width] + from_state[:, :width])
    reset = jax.nn.sigmoid(from_msg[:, width:2 * width] + from_state[:, width:2 * width])
    candidate = jnp.tanh(from_msg[:, 2 * width:] + reset * from_state[:, 2 * width:])
    return ((1.0 - update) * candidate + update * state.astype(jnp.float32)).astype(jnp.bfloat16)

def attend(source, neighbours, time_code, weights, upstream):
    count = source.shape[0]
    fanout = neighbours.shape[1]
    width = source.shape[1]
    head_size = width // HEADS
    w_query, w_key, w_value, w_out = (weights[0], weights[1], weights[2], weights[3])
    mixed = (neighbours.astype(jnp.float32) + time_code).astype(jnp.bfloat16).reshape(count * fanout, width)
    query = jnp.dot(source, w_query, preferred_element_type=jnp.float32).astype(jnp.bfloat16)
    keys = jnp.dot(mixed, w_key, preferred_element_type=jnp.float32).astype(jnp.bfloat16)
    values = jnp.dot(mixed, w_value, preferred_element_type=jnp.float32).astype(jnp.bfloat16)
    query_h = query.reshape(count, HEADS, head_size).astype(jnp.float32)
    keys_h = keys.reshape(count, fanout, HEADS, head_size).astype(jnp.float32)
    values_h = values.reshape(count, fanout, HEADS, head_size).astype(jnp.float32)
    scores = jnp.einsum('ehd,ekhd->ehk', query_h, keys_h) / jnp.sqrt(jnp.float32(head_size))
    powered = jnp.exp(scores)
    probs = powered / lax.optimization_barrier(jnp.sum(powered, axis=-1, keepdims=True))
    probs_b = probs.astype(jnp.bfloat16)
    attended = jnp.einsum('ehk,ekhd->ehd', probs_b.astype(jnp.float32), values_h)
    attended = attended.reshape(count, width).astype(jnp.bfloat16)
    output = jnp.dot(attended, w_out, preferred_element_type=jnp.float32) + source.astype(jnp.float32)
    embedded = output.astype(jnp.bfloat16)
    grad_out = jnp.dot(attended.T, upstream, preferred_element_type=jnp.float32)
    d_att = jnp.dot(upstream, w_out.T, preferred_element_type=jnp.float32).astype(jnp.bfloat16)
    d_att_h = d_att.reshape(count, HEADS, head_size).astype(jnp.float32)
    d_probs = jnp.einsum('ehd,ekhd->ehk', d_att_h, values_h)
    d_logits = probs * (d_probs - lax.optimization_barrier(jnp.sum(probs * d_probs, axis=-1, keepdims=True)))
    d_scores = (d_logits / jnp.sqrt(jnp.float32(head_size))).astype(jnp.bfloat16)
    d_scores_f = d_scores.astype(jnp.float32)
    d_values = jnp.einsum('ehk,ehd->ekhd', probs_b.astype(jnp.float32), d_att_h).astype(jnp.bfloat16).reshape(count * fanout, width)
    d_query = jnp.einsum('ehk,ekhd->ehd', d_scores_f, keys_h).astype(jnp.bfloat16).reshape(count, width)
    d_keys = jnp.einsum('ehk,ehd->ekhd', d_scores_f, query_h).astype(jnp.bfloat16).reshape(count * fanout, width)
    grad_query = jnp.dot(source.T, d_query, preferred_element_type=jnp.float32)
    grad_key = jnp.dot(mixed.T, d_keys, preferred_element_type=jnp.float32)
    grad_value = jnp.dot(mixed.T, d_values, preferred_element_type=jnp.float32)
    d_source = upstream.astype(jnp.float32) + jnp.dot(d_query, w_query.T, preferred_element_type=jnp.float32)
    d_neighbours = jnp.dot(d_keys, w_key.T, preferred_element_type=jnp.float32) + jnp.dot(d_values, w_value.T, preferred_element_type=jnp.float32)
    weight_terms = jnp.stack([grad_query, grad_key, grad_value, grad_out])
    return (embedded, d_source, d_neighbours.reshape(count, fanout, width), weight_terms)

def reference(memory_base, messages, touched, gru_input, gru_state, attn_weights, frequency, request_rows, event_slots, delays, upstream):
    width = memory_base.shape[1]
    current = memory_base
    embedded_all = []
    memory_all = []
    grad_all = []
    weight_total = jnp.zeros((4, width, width), jnp.float32)
    owners = (jnp.arange(SLOTS, dtype=jnp.int32) // CAP).astype(jnp.int32)
    for segment in range(SEG):
        start = current
        fresh = gru_update(messages[segment], memory_base, gru_input, gru_state)
        memory_now = jnp.where((touched[segment] > 0)[:, None], fresh, start)
        current = memory_now
        global_ids = (owners[None, :] * NODES_DEV + request_rows[segment]).astype(jnp.int32)
        slot_blocks = event_slots[segment].reshape(N_NODE, E_DEV, K + 1)
        node_ids = jax.vmap(lambda plan, chosen: plan[chosen])(global_ids, slot_blocks)
        delay_blocks = delays[segment].reshape(N_NODE, E_DEV, K)
        upstream_blocks = upstream[segment].reshape(N_NODE, E_DEV, width)

        def one_block(carry, inputs):
            grad_nodes, weight_sum = carry
            block_ids, block_delays, block_up = inputs
            gathered = start[block_ids]
            time_code = jnp.cos(block_delays[..., None].astype(jnp.float32) * frequency)
            emb, d_source, d_neighbours, weight_terms = attend(gathered[:, 0], gathered[:, 1:], time_code, attn_weights, block_up)
            event_grads = jnp.concatenate([d_source[:, None], d_neighbours], axis=1).reshape(-1, width)
            grad_nodes = grad_nodes.at[block_ids.reshape(-1)].add(event_grads)
            return ((grad_nodes, weight_sum + weight_terms), emb)
        init = (jnp.zeros((NODES, width), jnp.float32), jnp.zeros((4, width, width), jnp.float32))
        (grad_nodes, weight_sum), emb_blocks = lax.scan(one_block, init, (node_ids, delay_blocks, upstream_blocks))
        embedded_all.append(emb_blocks.reshape(EVENTS, width))
        memory_all.append(memory_now)
        grad_all.append(grad_nodes)
        weight_total = weight_total + weight_sum
    return (jnp.stack(embedded_all), jnp.stack(memory_all), jnp.stack(grad_all), weight_total)
```

```python
import functools
import math

import jax
import jax.numpy as jnp
from jax import lax
from jax.experimental import pallas as pl
from jax.experimental.pallas import tpu as pltpu
from jax.sharding import Mesh
from jax.sharding import PartitionSpec as P

SEG, X, Z, CORES = 4, 4, 4, 2
OWNERS = X * Z * CORES
PLANE = X * Z
DM = 512
HEADS = 2
HEAD = DM // HEADS
K = 8
E = 256
N = 256
CAP = 8
SLOTS = 256
PIECE = 64
HALF = PIECE // 2
CUT = DM // SEG
TILE = 128
TILES = E // TILE
ROWS = K * TILE
STEP = 32
ABSENT = 2.0
NODE = ("x", "z", "core")
FLAT = ("x", "z")
BF = jnp.bfloat16
F32 = jnp.float32

COS = (
    0.9999999698385398,
    -19.739198571306687,
    64.93882672218028,
    -85.44499716023202,
    60.126952745697146,
    -25.820504473745327,
    6.330480832160802,
)


def dot(a, b):
    return jnp.dot(a, b, preferred_element_type=F32)


def dot_tn(a, b):
    return lax.dot_general(a, b, (((0,), (0,)), ((), ())), preferred_element_type=F32)


def dot_nt(a, b):
    return lax.dot_general(a, b, (((1,), (1,)), ((), ())), preferred_element_type=F32)


def iota(shape, axis):
    return lax.broadcasted_iota(jnp.int32, shape, axis)


def column(row):
    n = row.shape[1]
    square = jnp.where(iota((n, n), 0) == iota((n, n), 1), row.astype(F32), 0.0)
    return jnp.sum(square, axis=1, keepdims=True)


def gru_kernel(touched, state, message, w_input, w_state, out, wi, ws, sem):
    copies = [
        pltpu.make_async_copy(w_state, ws, sem.at[0]),
        pltpu.make_async_copy(w_input, wi, sem.at[1]),
    ]
    for copy in copies:
        copy.start()
    keep = column(touched[...]) > 0.5
    m, s = message[...], state[...]
    copies[0].wait()
    from_state = [dot(s, ws[:, i * DM : (i + 1) * DM]) for i in range(3)]
    copies[1].wait()
    update = jax.nn.sigmoid(dot(m, wi[:, :DM]) + from_state[0])
    reset = jax.nn.sigmoid(dot(m, wi[:, DM : 2 * DM]) + from_state[1])
    candidate = jnp.tanh(dot(m, wi[:, 2 * DM :]) + reset * from_state[2])
    fresh = (1.0 - update) * candidate + update * s.astype(F32)
    out[...] = jnp.where(keep, fresh, ABSENT).astype(BF)


def gru(touched, state, message, w_input, w_state):
    whole = pl.BlockSpec(memory_space=pltpu.VMEM)
    far = pl.BlockSpec(memory_space=pl.ANY)
    return pl.pallas_call(
        gru_kernel,
        in_specs=[whole] * 3 + [far] * 2,
        out_specs=whole,
        out_shape=jax.ShapeDtypeStruct((N, DM), BF),
        scratch_shapes=[
            pltpu.VMEM((DM, 3 * DM), BF),
            pltpu.VMEM((DM, 3 * DM), BF),
            pltpu.SemaphoreType.DMA((2,)),
        ],
        compiler_params=pltpu.CompilerParams(vmem_limit_bytes=56 << 20),
        cost_estimate=pl.CostEstimate(
            flops=4 * N * DM * 3 * DM, bytes_accessed=4 << 20, transcendentals=3 * N * DM
        ),
        name="gru",
    )(touched, state, message, w_input, w_state)


def code_kernel(delays, frequency, code, code_t):
    k = pl.program_id(0)
    turns = frequency[...] * (1.0 / (2.0 * math.pi))
    high = jnp.round(turns * 16384.0) * (1.0 / 16384.0)
    low = turns - high
    lane = iota((E, K), 1)
    delay = jnp.sum(jnp.where(lane == k, delays[...].astype(F32), 0.0), axis=1, keepdims=True)
    coarse = delay * high
    part = (coarse - jnp.round(coarse)) + delay * low
    u = part * part
    wave = jnp.full_like(u, COS[-1])
    for c in COS[-2::-1]:
        wave = wave * u + c
    wave_b = wave.astype(BF)
    for i in range(TILES):
        code[i, 0] = wave_b[i * TILE : (i + 1) * TILE]
        code_t[i] = wave[i * TILE : (i + 1) * TILE].T.astype(BF)


def time_code(delays, frequency):
    return pl.pallas_call(
        code_kernel,
        grid=(K,),
        in_specs=[
            pl.BlockSpec((E, K), lambda k: (0, 0)),
            pl.BlockSpec((1, DM), lambda k: (0, 0)),
        ],
        out_specs=[
            pl.BlockSpec((TILES, 1, TILE, DM), lambda k: (0, k, 0, 0)),
            pl.BlockSpec((TILES, DM, TILE), lambda k: (0, 0, k)),
        ],
        out_shape=[
            jax.ShapeDtypeStruct((TILES, K, TILE, DM), BF),
            jax.ShapeDtypeStruct((TILES, DM, ROWS), BF),
        ],
        compiler_params=pltpu.CompilerParams(vmem_limit_bytes=16 << 20),
        cost_estimate=pl.CostEstimate(
            flops=20 * K * E * DM, bytes_accessed=4 << 20, transcendentals=K * E * DM
        ),
        name="time_code",
    )(delays, frequency)


def project_kernel(code, w, up, time_k, time_v, d_att):
    rows = code[0].reshape(K // 2 * TILE, DM)
    time_k[0] = dot(rows, w[1]).astype(BF).reshape(K // 2, TILE, DM)
    time_v[0] = dot(rows, w[2]).astype(BF).reshape(K // 2, TILE, DM)

    @pl.when((pl.program_id(0) == 0) & (pl.program_id(1) == 0))
    def _():
        d_att[...] = dot_nt(up[...], w[3]).astype(BF)


def project(code, weights, up):
    block = pl.BlockSpec((1, K // 2, TILE, DM), lambda i, j: (i, j, 0, 0))
    time = jax.ShapeDtypeStruct((TILES, K, TILE, DM), BF)
    whole = pl.BlockSpec((E, DM), lambda i, j: (0, 0))
    return pl.pallas_call(
        project_kernel,
        grid=(TILES, 2),
        in_specs=[block, pl.BlockSpec((4, DM, DM), lambda i, j: (0, 0, 0)), whole],
        out_specs=[block, block, whole],
        out_shape=[time, time, jax.ShapeDtypeStruct((E, DM), BF)],
        compiler_params=pltpu.CompilerParams(vmem_limit_bytes=16 << 20),
        cost_estimate=pl.CostEstimate(
            flops=4 * K * E * DM * DM, bytes_accessed=8 << 20, transcendentals=0
        ),
        name="time_projections",
    )(code, weights, up)


def owner_pick(asked):
    ids = jnp.concatenate([asked] * (N // 128), axis=1)
    return (ids == iota(ids.shape, 1)).astype(F32).astype(BF)


def start_kernel(seg, state, written, r1, r2, r3, asked, memory, rows):
    start = state[...]
    for back, r in ((3, r3), (2, r2), (1, r1)):
        row = r[...]
        start = jnp.where((row.astype(F32) < 1.5) & (seg[0] >= back), row, start)
    own = written[...]
    memory[...] = jnp.where(own.astype(F32) < 1.5, own, start)
    rows[...] = dot(owner_pick(asked[...]), start).astype(BF)


def start_rows(seg, state, written, r1, r2, r3, asked):
    whole = pl.BlockSpec(memory_space=pltpu.VMEM)
    return pl.pallas_call(
        start_kernel,
        in_specs=[pl.BlockSpec(memory_space=pltpu.SMEM)] + [whole] * 6,
        out_specs=[whole] * 2,
        out_shape=[
            jax.ShapeDtypeStruct((N, DM), BF),
            jax.ShapeDtypeStruct((SLOTS, DM), BF),
        ],
        compiler_params=pltpu.CompilerParams(vmem_limit_bytes=16 << 20),
        cost_estimate=pl.CostEstimate(
            flops=2 * N * DM * SLOTS, bytes_accessed=2 << 20, transcendentals=0
        ),
        name="start_rows",
    )(seg, state, written, r1, r2, r3, asked)


def attend_kernel(
    core, slots, chosen, chosen_t, tk, tv, tt, d_att, up, wq,
    embedded, d_slots, mine, other,
    skv, qf, src, both, dkv, att, dq, sums,
):
    rows = slots[...]
    pick = (chosen[:, 0:1] == iota((E, SLOTS), 1)).astype(F32).astype(BF)
    src[...] = dot(pick, rows)
    skv[:, :DM] = dot(rows, wq[1]).astype(BF)
    skv[:, DM:] = dot(rows, wq[2]).astype(BF)
    qf[...] = dot(pick, dot(rows, wq[0]).astype(BF))

    lane = iota((STEP, 128), 1)
    first = lane < K
    second = (lane >= K) & (lane < 2 * K)
    scale = 1.0 / math.sqrt(HEAD)

    def per_head(x):
        a = jnp.sum(jnp.where(first, x, 0.0), axis=1, keepdims=True)
        b = jnp.sum(jnp.where(second, x, 0.0), axis=1, keepdims=True)
        return jnp.where(first, a, b)

    def gather(i):
        ids = chosen[i * TILE : (i + 1) * TILE, :]
        slot = iota((TILE, SLOTS), 1)
        pick = jnp.concatenate(
            [(ids[:, 1 + k : 2 + k] == slot).astype(F32) for k in range(K)], axis=0
        ).astype(BF)
        both[i] = dot(pick, skv[...])

    def step(i, j):
        at = slice(i * TILE + j * STEP, i * TILE + (j + 1) * STEP)
        scores = jnp.zeros((STEP, 128), F32)
        d_probs = jnp.zeros((STEP, 128), F32)
        for h in range(HEADS):
            part = slice(h * HEAD, (h + 1) * HEAD)
            part_v = slice(DM + h * HEAD, DM + (h + 1) * HEAD)
            query = qf[at, part]
            d_out = d_att[at, part].astype(F32)
            for k in range(K):
                row = slice(k * TILE + j * STEP, k * TILE + (j + 1) * STEP)
                local = slice(j * STEP, (j + 1) * STEP)
                key = both[i, row, part] + tk[i, k, local, part].astype(F32)
                value = both[i, row, part_v] + tv[i, k, local, part].astype(F32)
                both[i, row, part] = key
                both[i, row, part_v] = value
                here = lane == h * K + k
                scores = jnp.where(here, jnp.sum(query * key, axis=1, keepdims=True), scores)
                d_probs = jnp.where(here, jnp.sum(d_out * value, axis=1, keepdims=True), d_probs)
        powered = jnp.exp(scores * scale)
        probs = powered / per_head(powered)
        d_scores = probs * (d_probs - per_head(probs * d_probs)) * scale
        for h in range(HEADS):
            part = slice(h * HEAD, (h + 1) * HEAD)
            part_v = slice(DM + h * HEAD, DM + (h + 1) * HEAD)
            query = qf[at, part]
            d_out = d_att[at, part].astype(F32)
            attended = jnp.zeros((STEP, HEAD), F32)
            d_query = jnp.zeros((STEP, HEAD), F32)
            for k in range(K):
                row = slice(k * TILE + j * STEP, k * TILE + (j + 1) * STEP)
                c = h * K + k
                p = jnp.broadcast_to(probs[:, c : c + 1], (STEP, HEAD))
                d = jnp.broadcast_to(d_scores[:, c : c + 1], (STEP, HEAD))
                attended += p * both[i, row, part_v]
                d_query += d * both[i, row, part]
                dkv[i, row, part] = (d * query).astype(BF)
                dkv[i, row, part_v] = (p * d_out).astype(BF)
            att[at, part] = attended.astype(BF)
            dq[at, part] = d_query.astype(BF)

    for i in range(TILES):
        gather(i)
    sub = iota((SLOTS, TILE), 0)
    s_kv = g_kv = None
    for i in range(TILES):
        for j in range(TILE // STEP):
            step(i, j)
        spread = jnp.concatenate(
            [
                (sub == chosen_t[1 + k : 2 + k, i * TILE : (i + 1) * TILE]).astype(F32)
                for k in range(K)
            ],
            axis=1,
        ).astype(BF)
        one, two = dot(spread, dkv[i]), dot(tt[i], dkv[i])
        s_kv = one if i == 0 else s_kv + one
        g_kv = two if i == 0 else g_kv + two
    s_kv = s_kv.astype(BF)
    pick_t = (iota((SLOTS, E), 0) == chosen_t[0:1, :]).astype(F32).astype(BF)
    s_q = dot(pick_t, dq[...]).astype(BF)

    def store(i, value):
        sums[i * 4 : (i + 1) * 4] = value.astype(BF).reshape(4, CORES, PIECE, DM)

    store(0, dot_tn(rows, s_q))
    g_kv += dot_tn(rows, s_kv)
    store(1, g_kv[:, :DM])
    store(2, g_kv[:, DM:])
    store(3, dot_tn(att[...], up[...]))
    mine[...] = sums[:, core[0]]
    other[...] = sums[:, 1 - core[0]]
    embedded[...] = (dot(att[...], wq[3]) + src[...]).astype(BF)
    grads = dot(pick_t, up[...]) + dot_nt(s_q, wq[0])
    grads += dot_nt(s_kv[:, :DM], wq[1]) + dot_nt(s_kv[:, DM:], wq[2])
    d_slots[...] = grads.astype(BF)


def attend(core, slots, chosen, chosen_t, time_k, time_v, time_t, d_att, up, weights):
    whole = pl.BlockSpec(memory_space=pltpu.VMEM)
    return pl.pallas_call(
        attend_kernel,
        in_specs=[pl.BlockSpec(memory_space=pltpu.SMEM)] + [whole] * 9,
        out_specs=[whole] * 4,
        out_shape=[
            jax.ShapeDtypeStruct((E, DM), BF),
            jax.ShapeDtypeStruct((SLOTS, DM), BF),
            jax.ShapeDtypeStruct((PLANE, PIECE, DM), BF),
            jax.ShapeDtypeStruct((PLANE, PIECE, DM), BF),
        ],
        scratch_shapes=[
            pltpu.VMEM((SLOTS, 2 * DM), BF),
            pltpu.VMEM((E, DM), F32),
            pltpu.VMEM((E, DM), F32),
            pltpu.VMEM((TILES, ROWS, 2 * DM), F32),
            pltpu.VMEM((TILES, ROWS, 2 * DM), BF),
            pltpu.VMEM((E, DM), BF),
            pltpu.VMEM((E, DM), BF),
            pltpu.VMEM((PLANE, CORES, PIECE, DM), BF),
        ],
        compiler_params=pltpu.CompilerParams(vmem_limit_bytes=40 << 20),
        cost_estimate=pl.CostEstimate(
            flops=6 << 30, bytes_accessed=14 << 20, transcendentals=E * 128
        ),
        name="attend",
    )(core, slots, chosen, chosen_t, time_k, time_v, time_t, d_att, up, weights)


def small(kernel, name, out_shape, in_specs, out_specs, scratch=(), moved=1 << 20):
    return pl.pallas_call(
        kernel,
        in_specs=in_specs,
        out_specs=out_specs,
        out_shape=out_shape,
        scratch_shapes=scratch,
        compiler_params=pltpu.CompilerParams(vmem_limit_bytes=16 << 20),
        cost_estimate=pl.CostEstimate(flops=1 << 19, bytes_accessed=moved, transcendentals=0),
        name=name,
    )


WHOLE = pl.BlockSpec(memory_space=pltpu.VMEM)
SCALAR = pl.BlockSpec(memory_space=pltpu.SMEM)
A_SHAPE = jax.ShapeDtypeStruct((PLANE, HALF, DM), BF)
B_SHAPE = jax.ShapeDtypeStruct((PLANE, HALF, CUT), BF)


def columns_of(seg, back):
    place = lax.rem(seg[0] + back + SEG, SEG)
    return pl.ds(pl.multiple_of(place * CUT, CUT), CUT)


def pair_kernel(seg, mine, partner, a, *bs):
    a[...] = (mine[:, :HALF].astype(F32) + partner[:, :HALF].astype(F32)).astype(BF)
    for ahead, b in enumerate(bs):
        at = columns_of(seg, ahead)
        b[...] = (mine[:, HALF:, at].astype(F32) + partner[:, HALF:, at].astype(F32)).astype(BF)


def pair_sum(seg, mine, partner):
    shapes = [A_SHAPE] + [B_SHAPE] * SEG
    return small(pair_kernel, "pair_sum", shapes, [SCALAR, WHOLE, WHOLE], [WHOLE] * 5)(
        seg, mine, partner
    )


def first_kernel(a, b0, b1, b2, b3, d_slots, part, pack):
    total = a[0].astype(F32)
    for i in range(1, PLANE):
        total += a[i].astype(F32)
    part[...] = total.astype(BF)
    b = (b0[...].astype(F32) + b1[...].astype(F32)) + (b2[...].astype(F32) + b3[...].astype(F32))
    pack[:, :HALF] = b.astype(BF)
    for i in range(SEG):
        at = slice(HALF + i * 2 * CAP, HALF + (i + 1) * 2 * CAP)
        pack[:, at] = d_slots[:, :, i * CUT : (i + 1) * CUT]


def first_sum(a, bs, d_slots):
    shapes = [
        jax.ShapeDtypeStruct((HALF, DM), BF),
        jax.ShapeDtypeStruct((PLANE, HALF + SEG * 2 * CAP, CUT), BF),
    ]
    return small(first_kernel, "first_sum", shapes, [WHOLE] * 6, [WHOLE] * 2)(
        a, *bs, d_slots.reshape(PLANE, 2 * CAP, DM)
    )


def second_kernel(seg, core, pack, own, p1, p2, p3, a, b, keep, give, parts):
    for back, r in enumerate((own, p1, p2, p3)):
        parts[lax.rem(seg[0] + SEG - back, SEG)] = r[...].astype(F32)
    a_total = ((parts[0] + parts[1]) + (parts[2] + parts[3])).astype(BF)
    total = pack[0, :HALF].astype(F32)
    for i in range(1, PLANE):
        total += pack[i, :HALF].astype(F32)
    b_total = total.astype(BF)
    for i in range(PLANE):
        a[i] = a_total
        b[i] = b_total
    first = core[0] == 0
    for i in range(SEG):
        grads = pack[:, HALF + i * 2 * CAP : HALF + (i + 1) * 2 * CAP].astype(F32)
        low = grads[:, :CAP].reshape(SLOTS // 2, CUT)
        high = grads[:, CAP:].reshape(SLOTS // 2, CUT)
        at = slice(i * CUT, (i + 1) * CUT)
        keep[:, at] = jnp.where(first, low, high).astype(BF)
        give[:, at] = jnp.where(first, high, low).astype(BF)


def second_sum(seg, core, pack, own, turned):
    grads = jax.ShapeDtypeStruct((SLOTS // 2, DM), BF)
    shapes = [A_SHAPE, B_SHAPE, grads, grads]
    scratch = [pltpu.VMEM((SEG, HALF, DM), F32)]
    return small(
        second_kernel, "second_sum", shapes, [SCALAR] * 2 + [WHOLE] * 5, [WHOLE] * 4, scratch
    )(seg, core, pack, own, *turned)


def join_kernel(seg, b0, b1, b2, b3, out):
    for back, b in enumerate((b0, b1, b2, b3)):
        out[:, :, columns_of(seg, -back)] = b[...]


def join(seg, bs):
    return small(join_kernel, "join", A_SHAPE, [SCALAR] + [WHOLE] * 4, WHOLE)(seg, *bs)


def whole_kernel(core, a, b, a_far, b_far, out):
    out[:, core[0], :HALF] = a[...].astype(F32)
    out[:, core[0], HALF:] = b[...].astype(F32)
    out[:, 1 - core[0], :HALF] = a_far[...].astype(F32)
    out[:, 1 - core[0], HALF:] = b_far[...].astype(F32)


def whole_grad(core, a, b, a_far, b_far):
    spec = pl.BlockSpec((4, HALF, DM), lambda i: (i, 0, 0))
    return pl.pallas_call(
        whole_kernel,
        grid=(PLANE // 4,),
        in_specs=[SCALAR] + [spec] * 4,
        out_specs=pl.BlockSpec((4, CORES, PIECE, DM), lambda i: (i, 0, 0, 0)),
        out_shape=jax.ShapeDtypeStruct((PLANE, CORES, PIECE, DM), F32),
        compiler_params=pltpu.CompilerParams(vmem_limit_bytes=16 << 20),
        cost_estimate=pl.CostEstimate(flops=1 << 19, bytes_accessed=6 << 20, transcendentals=0),
        name="whole_grad",
    )(core, a, b, a_far, b_far)


def spread_kernel(ids, out):
    out[...] = jnp.broadcast_to(column(ids[...]), (SLOTS, 128)).astype(jnp.int32)


def spread(ids):
    whole = pl.BlockSpec(memory_space=pltpu.VMEM)
    return pl.pallas_call(
        spread_kernel,
        in_specs=[whole],
        out_specs=whole,
        out_shape=jax.ShapeDtypeStruct((SLOTS, 128), jnp.int32),
        compiler_params=pltpu.CompilerParams(vmem_limit_bytes=16 << 20),
        cost_estimate=pl.CostEstimate(flops=1 << 17, bytes_accessed=1 << 17, transcendentals=0),
        name="spread",
    )(ids)


def owner_kernel(core, asked, keep, got, out):
    near = asked[:, core[0]].reshape(SLOTS // 2, 128)
    far = asked[:, 1 - core[0]].reshape(SLOTS // 2, 128)
    out[...] = dot_tn(owner_pick(near), keep[...]) + dot_tn(owner_pick(far), got[...])


def owner_sum(core, asked, keep, got):
    whole = pl.BlockSpec(memory_space=pltpu.VMEM)
    return pl.pallas_call(
        owner_kernel,
        in_specs=[pl.BlockSpec(memory_space=pltpu.SMEM)] + [whole] * 3,
        out_specs=whole,
        out_shape=jax.ShapeDtypeStruct((N, DM), F32),
        compiler_params=pltpu.CompilerParams(vmem_limit_bytes=16 << 20),
        cost_estimate=pl.CostEstimate(
            flops=2 * N * DM * SLOTS, bytes_accessed=1 << 20, transcendentals=0
        ),
        name="owner_sum",
    )(core, asked.reshape(PLANE, CORES, CAP, 128), keep, got)


def exchange(rows, axes, count):
    blocks = rows.reshape(count, -1, rows.shape[-1])
    return lax.all_to_all(blocks, axes, split_axis=0, concat_axis=0, tiled=True).reshape(rows.shape)


def on_device(
    memory_base,
    messages,
    touched,
    gru_input,
    gru_state,
    attn_weights,
    frequency,
    request_rows,
    event_slots,
    delays,
    upstream,
):
    seg = lax.axis_index("y").reshape(1)
    core = lax.axis_index("core").reshape(1)
    asked = exchange(spread(request_rows.reshape(1, SLOTS)), NODE, OWNERS)
    written = gru(touched, memory_base, messages[0], gru_input, gru_state)
    r1 = lax.ppermute(written, "y", [(0, 1), (1, 2), (2, 3)])
    r3 = lax.ppermute(written, "y", [(0, 3)])
    r2 = lax.ppermute(r1, "y", [(1, 2), (2, 3)])
    up = upstream[0]
    written, late, chosen, chosen_t = lax.optimization_barrier(
        (written, delays[0], event_slots[0], event_slots[0].T)
    )
    code, code_t = time_code(late, frequency.reshape(1, DM))
    written, code, code_t = lax.optimization_barrier((written, code, code_t))
    memory, rows = start_rows(seg, memory_base, written, r1, r2, r3, asked)
    rows, code = lax.optimization_barrier((rows, code))
    slots = exchange(rows, NODE, OWNERS)
    time_k, time_v, d_att = project(code, attn_weights, up)
    embedded, d_slots, mine, other = attend(
        core, slots, chosen, chosen_t, time_k, time_v, code_t, d_att, up, attn_weights
    )
    swap = [(0, 1), (1, 0)]

    def turn(x):
        return [
            lax.ppermute(x, "y", [(i, (i + s) % SEG) for i in range(SEG)]) for s in range(1, SEG)
        ]

    def plane(x):
        return lax.all_to_all(x, FLAT, split_axis=0, concat_axis=0, tiled=True)

    a, b0, *bs = pair_sum(seg, mine, lax.ppermute(other, "core", swap))
    bs = [
        lax.ppermute(b, "y", [(i, (i + s) % SEG) for i in range(SEG)])
        for s, b in enumerate(bs, start=1)
    ]
    part, pack = first_sum(plane(a), [b0] + bs, d_slots)
    a, b, keep, give = second_sum(seg, core, plane(pack), part, turn(part))
    b = plane(b)
    a, b = lax.optimization_barrier((a, b))
    turned = turn(b)
    a = plane(a)
    a, b, *turned = lax.optimization_barrier((a, b, *turned))
    a_far = lax.ppermute(a, "core", swap)
    b = join(seg, [b] + turned)
    b_far = lax.ppermute(b, "core", swap)
    memory_grad = owner_sum(core, asked, keep, lax.ppermute(give, "core", swap))
    weight_grad = whole_grad(core, a, b, a_far, b_far)
    return embedded[None], memory[None], memory_grad[None], weight_grad.reshape(4, DM, DM)


def solution(mesh):
    fine = Mesh(mesh.devices.reshape(SEG, X, Z, CORES), ("y", "x", "z", "core"))
    both = P("y", NODE, None)
    in_specs = (P(NODE, None), both, P("y", NODE), P(), P(), P(), P(), both, both, both, both)
    out_specs = (both, both, both, P())
    return jax.shard_map(
        on_device, mesh=fine, in_specs=in_specs, out_specs=out_specs, check_vma=False
    )
```

```python
import functools
import math

import jax
import jax.numpy as jnp
from jax import lax
from jax.experimental import pallas as pl
from jax.experimental.pallas import tpu as pltpu
from jax.sharding import Mesh
from jax.sharding import PartitionSpec as P

SEG, X, Z, CORES = 4, 4, 4, 2
OWNERS = X * Z * CORES
PLANE = X * Z
DM = 512
HEADS = 2
HEAD = DM // HEADS
K = 8
E = 256
N = 256
CAP = 8
SLOTS = 256
PIECE = 64
TILE = 128
TILES = E // TILE
ROWS = K * TILE
STEP = 32
ABSENT = 2.0
NODE = ("x", "z", "core")
FLAT = ("x", "z")
BF = jnp.bfloat16
F32 = jnp.float32

COS = (
    0.9999999698385398,
    -19.739198571306687,
    64.93882672218028,
    -85.44499716023202,
    60.126952745697146,
    -25.820504473745327,
    6.330480832160802,
)


def dot(a, b):
    return jnp.dot(a, b, preferred_element_type=F32)


def dot_tn(a, b):
    return lax.dot_general(a, b, (((0,), (0,)), ((), ())), preferred_element_type=F32)


def dot_nt(a, b):
    return lax.dot_general(a, b, (((1,), (1,)), ((), ())), preferred_element_type=F32)


def iota(shape, axis):
    return lax.broadcasted_iota(jnp.int32, shape, axis)


def column(row):
    n = row.shape[1]
    square = jnp.where(iota((n, n), 0) == iota((n, n), 1), row.astype(F32), 0.0)
    return jnp.sum(square, axis=1, keepdims=True)


def gru_kernel(touched, state, message, w_input, w_state, out, wi, ws, sem):
    copies = [
        pltpu.make_async_copy(w_state, ws, sem.at[0]),
        pltpu.make_async_copy(w_input, wi, sem.at[1]),
    ]
    for copy in copies:
        copy.start()
    keep = column(touched[...]) > 0.5
    m, s = message[...], state[...]
    copies[0].wait()
    from_state = [dot(s, ws[:, i * DM : (i + 1) * DM]) for i in range(3)]
    copies[1].wait()
    update = jax.nn.sigmoid(dot(m, wi[:, :DM]) + from_state[0])
    reset = jax.nn.sigmoid(dot(m, wi[:, DM : 2 * DM]) + from_state[1])
    candidate = jnp.tanh(dot(m, wi[:, 2 * DM :]) + reset * from_state[2])
    fresh = (1.0 - update) * candidate + update * s.astype(F32)
    out[...] = jnp.where(keep, fresh, ABSENT).astype(BF)


def gru(touched, state, message, w_input, w_state):
    whole = pl.BlockSpec(memory_space=pltpu.VMEM)
    far = pl.BlockSpec(memory_space=pl.ANY)
    return pl.pallas_call(
        gru_kernel,
        in_specs=[whole] * 3 + [far] * 2,
        out_specs=whole,
        out_shape=jax.ShapeDtypeStruct((N, DM), BF),
        scratch_shapes=[
            pltpu.VMEM((DM, 3 * DM), BF),
            pltpu.VMEM((DM, 3 * DM), BF),
            pltpu.SemaphoreType.DMA((2,)),
        ],
        compiler_params=pltpu.CompilerParams(vmem_limit_bytes=56 << 20),
        cost_estimate=pl.CostEstimate(
            flops=4 * N * DM * 3 * DM, bytes_accessed=4 << 20, transcendentals=3 * N * DM
        ),
        name="gru",
    )(touched, state, message, w_input, w_state)


def code_kernel(delays, frequency, code, code_t):
    k = pl.program_id(0)
    turns = frequency[...] * (1.0 / (2.0 * math.pi))
    high = jnp.round(turns * 16384.0) * (1.0 / 16384.0)
    low = turns - high
    lane = iota((E, K), 1)
    delay = jnp.sum(jnp.where(lane == k, delays[...].astype(F32), 0.0), axis=1, keepdims=True)
    coarse = delay * high
    part = (coarse - jnp.round(coarse)) + delay * low
    u = part * part
    wave = jnp.full_like(u, COS[-1])
    for c in COS[-2::-1]:
        wave = wave * u + c
    wave_b = wave.astype(BF)
    for i in range(TILES):
        code[i, 0] = wave_b[i * TILE : (i + 1) * TILE]
        code_t[i] = wave[i * TILE : (i + 1) * TILE].T.astype(BF)


def time_code(delays, frequency):
    return pl.pallas_call(
        code_kernel,
        grid=(K,),
        in_specs=[
            pl.BlockSpec((E, K), lambda k: (0, 0)),
            pl.BlockSpec((1, DM), lambda k: (0, 0)),
        ],
        out_specs=[
            pl.BlockSpec((TILES, 1, TILE, DM), lambda k: (0, k, 0, 0)),
            pl.BlockSpec((TILES, DM, TILE), lambda k: (0, 0, k)),
        ],
        out_shape=[
            jax.ShapeDtypeStruct((TILES, K, TILE, DM), BF),
            jax.ShapeDtypeStruct((TILES, DM, ROWS), BF),
        ],
        compiler_params=pltpu.CompilerParams(vmem_limit_bytes=56 << 20),
        cost_estimate=pl.CostEstimate(
            flops=20 * K * E * DM, bytes_accessed=4 << 20, transcendentals=K * E * DM
        ),
        name="time_code",
    )(delays, frequency)


def project_kernel(code, w, time_kv):
    rows = code[0].reshape(K // 2 * TILE, DM)
    for i in range(2):
        part = dot(rows, w[1 + i]).astype(BF).reshape(K // 2, TILE, DM)
        time_kv[0, :, :, i * DM : (i + 1) * DM] = part


def project(code, weights):
    return pl.pallas_call(
        project_kernel,
        grid=(TILES, 2),
        in_specs=[
            pl.BlockSpec((1, K // 2, TILE, DM), lambda i, j: (i, j, 0, 0)),
            pl.BlockSpec((4, DM, DM), lambda i, j: (0, 0, 0)),
        ],
        out_specs=pl.BlockSpec((1, K // 2, TILE, 2 * DM), lambda i, j: (i, j, 0, 0)),
        out_shape=jax.ShapeDtypeStruct((TILES, K, TILE, 2 * DM), BF),
        compiler_params=pltpu.CompilerParams(vmem_limit_bytes=56 << 20),
        cost_estimate=pl.CostEstimate(
            flops=4 * K * E * DM * DM, bytes_accessed=8 << 20, transcendentals=0
        ),
        name="time_projections",
    )(code, weights)


def owner_pick(asked):
    ids = jnp.concatenate([asked] * (N // 128), axis=1)
    return (ids == iota(ids.shape, 1)).astype(F32).astype(BF)


def start_kernel(seg, state, written, r1, r2, r3, asked, memory, rows):
    start = state[...]
    for back, r in ((3, r3), (2, r2), (1, r1)):
        row = r[...]
        start = jnp.where((row.astype(F32) < 1.5) & (seg[0] >= back), row, start)
    own = written[...]
    memory[...] = jnp.where(own.astype(F32) < 1.5, own, start)
    rows[...] = dot(owner_pick(asked[...]), start).astype(BF)


def start_rows(seg, state, written, r1, r2, r3, asked):
    whole = pl.BlockSpec(memory_space=pltpu.VMEM)
    return pl.pallas_call(
        start_kernel,
        in_specs=[pl.BlockSpec(memory_space=pltpu.SMEM)] + [whole] * 6,
        out_specs=[whole] * 2,
        out_shape=[
            jax.ShapeDtypeStruct((N, DM), BF),
            jax.ShapeDtypeStruct((SLOTS, DM), BF),
        ],
        compiler_params=pltpu.CompilerParams(vmem_limit_bytes=16 << 20),
        cost_estimate=pl.CostEstimate(
            flops=2 * N * DM * SLOTS, bytes_accessed=2 << 20, transcendentals=0
        ),
        name="start_rows",
    )(seg, state, written, r1, r2, r3, asked)


def attend_kernel(
    core, slots, chosen, chosen_t, time_kv, time_t, up, w,
    embedded, d_slots, mine, other,
    tkv, tt, wq, sem, skv, d_att, qf, src, both, dkv, att, dq, sums,
):
    moves = ((w, wq), (time_kv, tkv), (time_t, tt))
    copies = [pltpu.make_async_copy(a, b, sem.at[i]) for i, (a, b) in enumerate(moves)]
    for copy in copies:
        copy.start()
    rows = slots[...]
    pick = (chosen[:, 0:1] == iota((E, SLOTS), 1)).astype(F32).astype(BF)
    src[...] = dot(pick, rows)
    copies[0].wait()
    skv[:, :DM] = dot(rows, wq[1]).astype(BF)
    skv[:, DM:] = dot(rows, wq[2]).astype(BF)
    qf[...] = dot(pick, dot(rows, wq[0]).astype(BF))
    d_att[...] = dot_nt(up[...], wq[3])
    copies[1].wait()

    lane = iota((STEP, 128), 1)
    first = lane < K
    second = (lane >= K) & (lane < 2 * K)
    scale = 1.0 / math.sqrt(HEAD)

    def per_head(x):
        a = jnp.sum(jnp.where(first, x, 0.0), axis=1, keepdims=True)
        b = jnp.sum(jnp.where(second, x, 0.0), axis=1, keepdims=True)
        return jnp.where(first, a, b)

    def gather(i):
        ids = chosen[i * TILE : (i + 1) * TILE, :]
        slot = iota((TILE, SLOTS), 1)
        pick = jnp.concatenate(
            [(ids[:, 1 + k : 2 + k] == slot).astype(F32) for k in range(K)], axis=0
        ).astype(BF)
        both[i] = dot(pick, skv[...])

    def step(i, j):
        at = slice(i * TILE + j * STEP, i * TILE + (j + 1) * STEP)
        scores = jnp.zeros((STEP, 128), F32)
        d_probs = jnp.zeros((STEP, 128), F32)
        for h in range(HEADS):
            part = slice(h * HEAD, (h + 1) * HEAD)
            part_v = slice(DM + h * HEAD, DM + (h + 1) * HEAD)
            query = qf[at, part]
            d_out = d_att[at, part]
            for k in range(K):
                row = slice(k * TILE + j * STEP, k * TILE + (j + 1) * STEP)
                local = slice(j * STEP, (j + 1) * STEP)
                key = both[i, row, part] + tkv[i, k, local, part].astype(F32)
                value = both[i, row, part_v] + tkv[i, k, local, part_v].astype(F32)
                both[i, row, part] = key
                both[i, row, part_v] = value
                here = lane == h * K + k
                scores = jnp.where(here, jnp.sum(query * key, axis=1, keepdims=True), scores)
                d_probs = jnp.where(here, jnp.sum(d_out * value, axis=1, keepdims=True), d_probs)
        powered = jnp.exp(scores * scale)
        probs = powered / per_head(powered)
        d_scores = probs * (d_probs - per_head(probs * d_probs)) * scale
        for h in range(HEADS):
            part = slice(h * HEAD, (h + 1) * HEAD)
            part_v = slice(DM + h * HEAD, DM + (h + 1) * HEAD)
            query = qf[at, part]
            d_out = d_att[at, part]
            attended = jnp.zeros((STEP, HEAD), F32)
            d_query = jnp.zeros((STEP, HEAD), F32)
            for k in range(K):
                row = slice(k * TILE + j * STEP, k * TILE + (j + 1) * STEP)
                c = h * K + k
                p = jnp.broadcast_to(probs[:, c : c + 1], (STEP, HEAD))
                d = jnp.broadcast_to(d_scores[:, c : c + 1], (STEP, HEAD))
                attended += p * both[i, row, part_v]
                d_query += d * both[i, row, part]
                dkv[i, row, part] = (d * query).astype(BF)
                dkv[i, row, part_v] = (p * d_out).astype(BF)
            att[at, part] = attended.astype(BF)
            dq[at, part] = d_query.astype(BF)

    for i in range(TILES):
        gather(i)
    sub = iota((SLOTS, TILE), 0)
    s_kv = dot_t = None
    for i in range(TILES):
        for j in range(TILE // STEP):
            step(i, j)
        if i == 0:
            copies[2].wait()
        spread = jnp.concatenate(
            [
                (sub == chosen_t[1 + k : 2 + k, i * TILE : (i + 1) * TILE]).astype(F32)
                for k in range(K)
            ],
            axis=1,
        ).astype(BF)
        one, two = dot(spread, dkv[i]), dot(tt[i], dkv[i])
        s_kv = one if i == 0 else s_kv + one
        dot_t = two if i == 0 else dot_t + two
    s_kv = s_kv.astype(BF)
    pick_t = (iota((SLOTS, E), 0) == chosen_t[0:1, :]).astype(F32).astype(BF)
    s_q = dot(pick_t, dq[...]).astype(BF)

    def store(i, value):
        sums[i * 4 : (i + 1) * 4] = value.astype(BF).reshape(4, CORES, PIECE, DM)

    store(0, dot_tn(rows, s_q))
    g_kv = dot_t + dot_tn(rows, s_kv)
    store(1, g_kv[:, :DM])
    store(2, g_kv[:, DM:])
    store(3, dot_tn(att[...], up[...]))
    mine[...] = sums[:, core[0]]
    other[...] = sums[:, 1 - core[0]]
    embedded[...] = (dot(att[...], wq[3]) + src[...]).astype(BF)
    grads = dot(pick_t, up[...]) + dot_nt(s_q, wq[0])
    grads += dot_nt(s_kv[:, :DM], wq[1]) + dot_nt(s_kv[:, DM:], wq[2])
    d_slots[...] = grads.astype(BF)


def attend(core, slots, chosen, chosen_t, time_kv, time_t, up, weights):
    whole = pl.BlockSpec(memory_space=pltpu.VMEM)
    far = pl.BlockSpec(memory_space=pl.ANY)
    return pl.pallas_call(
        attend_kernel,
        in_specs=[pl.BlockSpec(memory_space=pltpu.SMEM)]
        + [whole] * 3
        + [far] * 2
        + [whole]
        + [far],
        out_specs=[whole] * 4,
        out_shape=[
            jax.ShapeDtypeStruct((E, DM), BF),
            jax.ShapeDtypeStruct((SLOTS, DM), BF),
            jax.ShapeDtypeStruct((PLANE, PIECE, DM), BF),
            jax.ShapeDtypeStruct((PLANE, PIECE, DM), BF),
        ],
        scratch_shapes=[
            pltpu.VMEM((TILES, K, TILE, 2 * DM), BF),
            pltpu.VMEM((TILES, DM, ROWS), BF),
            pltpu.VMEM((4, DM, DM), BF),
            pltpu.SemaphoreType.DMA((3,)),
            pltpu.VMEM((SLOTS, 2 * DM), BF),
            pltpu.VMEM((E, DM), F32),
            pltpu.VMEM((E, DM), F32),
            pltpu.VMEM((E, DM), F32),
            pltpu.VMEM((TILES, ROWS, 2 * DM), F32),
            pltpu.VMEM((TILES, ROWS, 2 * DM), BF),
            pltpu.VMEM((E, DM), BF),
            pltpu.VMEM((E, DM), BF),
            pltpu.VMEM((PLANE, CORES, PIECE, DM), BF),
        ],
        compiler_params=pltpu.CompilerParams(vmem_limit_bytes=50 << 20),
        cost_estimate=pl.CostEstimate(
            flops=6 << 30, bytes_accessed=14 << 20, transcendentals=E * 128
        ),
        name="attend",
    )(core, slots, chosen, chosen_t, time_kv, time_t, up, weights)


def pair_kernel(a, b, d_slots, out):
    out[:, :PIECE] = (a[...].astype(F32) + b[...].astype(F32)).astype(BF)
    out[:, PIECE:] = d_slots[...]


def pair_sum(a, b, d_slots):
    spec = pl.BlockSpec((4, PIECE, DM), lambda i: (i, 0, 0))
    return pl.pallas_call(
        pair_kernel,
        grid=(PLANE // 4,),
        in_specs=[spec, spec, pl.BlockSpec((4, 2 * CAP, DM), lambda i: (i, 0, 0))],
        out_specs=pl.BlockSpec((4, PIECE + 2 * CAP, DM), lambda i: (i, 0, 0)),
        out_shape=jax.ShapeDtypeStruct((PLANE, PIECE + 2 * CAP, DM), BF),
        compiler_params=pltpu.CompilerParams(vmem_limit_bytes=16 << 20),
        cost_estimate=pl.CostEstimate(flops=1 << 19, bytes_accessed=3 << 20, transcendentals=0),
        name="pair_sum",
    )(a, b, d_slots.reshape(PLANE, 2 * CAP, DM))


def plane_kernel(core, a, part, keep, give):
    total = a[0, :PIECE].astype(F32)
    for i in range(1, PLANE):
        total += a[i, :PIECE].astype(F32)
    part[...] = total.astype(BF)
    grads = a[:, PIECE:].astype(F32)
    low, high = grads[:, :CAP].reshape(SLOTS // 2, DM), grads[:, CAP:].reshape(SLOTS // 2, DM)
    first = core[0] == 0
    keep[...] = jnp.where(first, low, high).astype(BF)
    give[...] = jnp.where(first, high, low).astype(BF)


def plane_sum(core, a):
    whole = pl.BlockSpec(memory_space=pltpu.VMEM)
    half = jax.ShapeDtypeStruct((SLOTS // 2, DM), BF)
    return pl.pallas_call(
        plane_kernel,
        in_specs=[pl.BlockSpec(memory_space=pltpu.SMEM), whole],
        out_specs=[whole] * 3,
        out_shape=[jax.ShapeDtypeStruct((PIECE, DM), BF), half, half],
        compiler_params=pltpu.CompilerParams(vmem_limit_bytes=16 << 20),
        cost_estimate=pl.CostEstimate(flops=1 << 19, bytes_accessed=2 << 20, transcendentals=0),
        name="plane_sum",
    )(core, a)


def swap_kernel(a, b, out):
    out[...] = (a[...].astype(F32) + b[...].astype(F32)).astype(BF)


def swap_sum(a, b):
    whole = pl.BlockSpec(memory_space=pltpu.VMEM)
    return pl.pallas_call(
        swap_kernel,
        in_specs=[whole] * 2,
        out_specs=whole,
        out_shape=jax.ShapeDtypeStruct((PIECE, DM), BF),
        compiler_params=pltpu.CompilerParams(vmem_limit_bytes=16 << 20),
        cost_estimate=pl.CostEstimate(flops=1 << 15, bytes_accessed=1 << 17, transcendentals=0),
        name="swap_sum",
    )(a, b)


def seg_kernel(a, b, out):
    total = (a[...].astype(F32) + b[...].astype(F32)).astype(BF)
    for i in range(PLANE):
        out[i] = total


def seg_sum(a, b):
    whole = pl.BlockSpec(memory_space=pltpu.VMEM)
    return pl.pallas_call(
        seg_kernel,
        in_specs=[whole] * 2,
        out_specs=whole,
        out_shape=jax.ShapeDtypeStruct((PLANE, PIECE, DM), BF),
        compiler_params=pltpu.CompilerParams(vmem_limit_bytes=16 << 20),
        cost_estimate=pl.CostEstimate(flops=1 << 15, bytes_accessed=1 << 20, transcendentals=0),
        name="seg_sum",
    )(a, b)


def own_kernel(core, half, out):
    out[:, 0] = half[...].astype(F32)


def far_kernel(core, half, before, out):
    out[:, 0] = half[...].astype(F32)


def whole_grad(core, half, before=None):
    own = before is None

    def place(i, core):
        return (i, core[0] if own else 1 - core[0], 0, 0)

    spec = pl.BlockSpec((4, PIECE, DM), lambda i, core: (i, 0, 0))
    far = pl.BlockSpec(memory_space=pl.ANY)
    return pl.pallas_call(
        own_kernel if own else far_kernel,
        grid_spec=pltpu.PrefetchScalarGridSpec(
            num_scalar_prefetch=1,
            grid=(PLANE // 4,),
            in_specs=[spec] if own else [spec, far],
            out_specs=pl.BlockSpec((4, 1, PIECE, DM), place),
        ),
        out_shape=jax.ShapeDtypeStruct((PLANE, CORES, PIECE, DM), F32),
        input_output_aliases={} if own else {2: 0},
        compiler_params=pltpu.CompilerParams(vmem_limit_bytes=16 << 20),
        cost_estimate=pl.CostEstimate(flops=1 << 18, bytes_accessed=3 << 20, transcendentals=0),
        name="own_half" if own else "far_half",
    )(core, half, *([] if own else [before]))


def spread_kernel(ids, out):
    out[...] = jnp.broadcast_to(column(ids[...]), (SLOTS, 128)).astype(jnp.int32)


def spread(ids):
    whole = pl.BlockSpec(memory_space=pltpu.VMEM)
    return pl.pallas_call(
        spread_kernel,
        in_specs=[whole],
        out_specs=whole,
        out_shape=jax.ShapeDtypeStruct((SLOTS, 128), jnp.int32),
        compiler_params=pltpu.CompilerParams(vmem_limit_bytes=16 << 20),
        cost_estimate=pl.CostEstimate(flops=1 << 17, bytes_accessed=1 << 17, transcendentals=0),
        name="spread",
    )(ids)


def owner_kernel(core, asked, keep, got, out):
    near = asked[:, core[0]].reshape(SLOTS // 2, 128)
    far = asked[:, 1 - core[0]].reshape(SLOTS // 2, 128)
    out[...] = dot_tn(owner_pick(near), keep[...]) + dot_tn(owner_pick(far), got[...])


def owner_sum(core, asked, keep, got):
    whole = pl.BlockSpec(memory_space=pltpu.VMEM)
    return pl.pallas_call(
        owner_kernel,
        in_specs=[pl.BlockSpec(memory_space=pltpu.SMEM)] + [whole] * 3,
        out_specs=whole,
        out_shape=jax.ShapeDtypeStruct((N, DM), F32),
        compiler_params=pltpu.CompilerParams(vmem_limit_bytes=16 << 20),
        cost_estimate=pl.CostEstimate(
            flops=2 * N * DM * SLOTS, bytes_accessed=1 << 20, transcendentals=0
        ),
        name="owner_sum",
    )(core, asked.reshape(PLANE, CORES, CAP, 128), keep, got)


def exchange(rows, axes, count):
    blocks = rows.reshape(count, -1, rows.shape[-1])
    return lax.all_to_all(blocks, axes, split_axis=0, concat_axis=0, tiled=True).reshape(rows.shape)


def plane(x):
    return lax.all_to_all(x, FLAT, split_axis=0, concat_axis=0, tiled=True)


def on_device(
    memory_base,
    messages,
    touched,
    gru_input,
    gru_state,
    attn_weights,
    frequency,
    request_rows,
    event_slots,
    delays,
    upstream,
):
    seg = lax.axis_index("y").reshape(1)
    core = lax.axis_index("core").reshape(1)
    asked = exchange(spread(request_rows.reshape(1, SLOTS)), NODE, OWNERS)
    written = gru(touched, memory_base, messages[0], gru_input, gru_state)
    r1 = lax.ppermute(written, "y", [(0, 1), (1, 2), (2, 3)])
    r2 = lax.ppermute(written, "y", [(0, 2), (1, 3)])
    r3 = lax.ppermute(written, "y", [(0, 3)])
    up = upstream[0]
    written, late, chosen, chosen_t = lax.optimization_barrier(
        (written, delays[0], event_slots[0], event_slots[0].T)
    )
    code, code_t = time_code(late, frequency.reshape(1, DM))
    written, code, code_t = lax.optimization_barrier((written, code, code_t))
    memory, rows = start_rows(seg, memory_base, written, r1, r2, r3, asked)
    rows, code = lax.optimization_barrier((rows, code))
    slots = exchange(rows, NODE, OWNERS)
    time_kv = project(code, attn_weights)
    embedded, d_slots, mine, other = attend(
        core, slots, chosen, chosen_t, time_kv, code_t, up, attn_weights
    )
    swap = [(0, 1), (1, 0)]
    partner = lax.ppermute(other, "core", swap)
    parts = plane(pair_sum(mine, partner, d_slots))
    part, keep, give = plane_sum(core, parts)
    got = lax.ppermute(give, "core", swap)
    part = swap_sum(part, lax.ppermute(part, "y", [(0, 1), (1, 0), (2, 3), (3, 2)]))
    turned = lax.ppermute(part, "y", [(0, 3), (3, 0), (1, 2), (2, 1)])
    memory_grad = owner_sum(core, asked, keep, got)
    part, turned, memory_grad = lax.optimization_barrier((part, turned, memory_grad))
    half = plane(seg_sum(part, turned))
    far = lax.ppermute(half, "core", swap)
    weight_grad = whole_grad(core, far, whole_grad(core, half))
    return embedded[None], memory[None], memory_grad[None], weight_grad.reshape(4, DM, DM)


def solution(mesh):
    fine = Mesh(mesh.devices.reshape(SEG, X, Z, CORES), ("y", "x", "z", "core"))
    both = P("y", NODE, None)
    in_specs = (P(NODE, None), both, P("y", NODE), P(), P(), P(), P(), both, both, both, both)
    out_specs = (both, both, both, P())
    return jax.shard_map(
        on_device, mesh=fine, in_specs=in_specs, out_specs=out_specs, check_vma=False
    )
```

```python
import functools
import math

import jax
import jax.numpy as jnp
from jax import lax
from jax.experimental import pallas as pl
from jax.experimental.pallas import tpu as pltpu
from jax.sharding import Mesh
from jax.sharding import PartitionSpec as P

SEG, X, Z, CORES = 4, 4, 4, 2
OWNERS = X * Z * CORES
PLANE = X * Z
DM = 512
HEADS = 2
HEAD = DM // HEADS
K = 8
E = 256
N = 256
CAP = 8
SLOTS = 256
PIECE = 64
TILE = 128
TILES = E // TILE
ROWS = K * TILE
STEP = 32
ABSENT = 2.0
NODE = ("x", "z", "core")
FLAT = ("x", "z")
BF = jnp.bfloat16
F32 = jnp.float32

COS = (
    0.9999999698385398,
    -19.739198571306687,
    64.93882672218028,
    -85.44499716023202,
    60.126952745697146,
    -25.820504473745327,
    6.330480832160802,
)


def dot(a, b):
    return jnp.dot(a, b, preferred_element_type=F32)


def dot_tn(a, b):
    return lax.dot_general(a, b, (((0,), (0,)), ((), ())), preferred_element_type=F32)


def dot_nt(a, b):
    return lax.dot_general(a, b, (((1,), (1,)), ((), ())), preferred_element_type=F32)


def iota(shape, axis):
    return lax.broadcasted_iota(jnp.int32, shape, axis)


def column(row):
    n = row.shape[1]
    square = jnp.where(iota((n, n), 0) == iota((n, n), 1), row.astype(F32), 0.0)
    return jnp.sum(square, axis=1, keepdims=True)


def gru_kernel(
    touched, ids, state, message, w_input, w_state, out, spread, st, ms, wi, ws, sem
):
    moves = ((state, st), (w_state, ws), (message, ms), (w_input, wi))
    copies = [pltpu.make_async_copy(a, b, sem.at[i]) for i, (a, b) in enumerate(moves)]
    for copy in copies:
        copy.start()
    keep = column(touched[...]) > 0.5
    spread[...] = jnp.broadcast_to(column(ids[...]), (SLOTS, 128)).astype(jnp.int32)
    copies[0].wait()
    copies[1].wait()
    s = st[...]
    from_state = [dot(s, ws[:, i * DM : (i + 1) * DM]) for i in range(3)]
    copies[2].wait()
    copies[3].wait()
    m = ms[...]
    update = jax.nn.sigmoid(dot(m, wi[:, :DM]) + from_state[0])
    reset = jax.nn.sigmoid(dot(m, wi[:, DM : 2 * DM]) + from_state[1])
    candidate = jnp.tanh(dot(m, wi[:, 2 * DM :]) + reset * from_state[2])
    fresh = (1.0 - update) * candidate + update * s.astype(F32)
    out[...] = jnp.where(keep, fresh, ABSENT).astype(BF)


def gru(touched, ids, state, message, w_input, w_state):
    whole = pl.BlockSpec(memory_space=pltpu.VMEM)
    far = pl.BlockSpec(memory_space=pl.ANY)
    return pl.pallas_call(
        gru_kernel,
        in_specs=[whole] * 2 + [far] * 4,
        out_specs=[whole] * 2,
        out_shape=[
            jax.ShapeDtypeStruct((N, DM), BF),
            jax.ShapeDtypeStruct((SLOTS, 128), jnp.int32),
        ],
        scratch_shapes=[
            pltpu.VMEM((N, DM), BF),
            pltpu.VMEM((N, DM), BF),
            pltpu.VMEM((DM, 3 * DM), BF),
            pltpu.VMEM((DM, 3 * DM), BF),
            pltpu.SemaphoreType.DMA((4,)),
        ],
        compiler_params=pltpu.CompilerParams(vmem_limit_bytes=56 << 20),
        cost_estimate=pl.CostEstimate(
            flops=4 * N * DM * 3 * DM, bytes_accessed=4 << 20, transcendentals=3 * N * DM
        ),
        name="gru",
    )(touched, ids, state, message, w_input, w_state)


def time_kernel(tile, delays, frequency, w_key, w_value, code_t, time_kv):
    g = pl.program_id(0)
    turns = frequency[...] * (1.0 / (2.0 * math.pi))
    high = jnp.round(turns * 16384.0) * (1.0 / 16384.0)
    low = turns - high
    waves = []
    for i in range(2):
        block = delays[:, tile * TILE : (tile + 1) * TILE].astype(F32)
        here = iota((K, TILE), 0) == 2 * g + i
        delay = column(jnp.sum(jnp.where(here, block, 0.0), axis=0, keepdims=True))
        coarse = delay * high
        part = (coarse - jnp.round(coarse)) + delay * low
        u = part * part
        wave = jnp.full_like(u, COS[-1])
        for c in COS[-2::-1]:
            wave = wave * u + c
        waves.append(wave)
    wave = jnp.concatenate(waves, axis=0)
    code_t[0] = wave.T.astype(BF)
    wave = wave.astype(BF)
    time_kv[:, :DM] = dot(wave, w_key[0]).astype(BF)
    time_kv[:, DM:] = dot(wave, w_value[0]).astype(BF)


def time_tile(tile, delays, frequency, weights):
    return pl.pallas_call(
        functools.partial(time_kernel, tile),
        grid=(K // 2,),
        in_specs=[
            pl.BlockSpec((K, E), lambda g: (0, 0)),
            pl.BlockSpec((1, DM), lambda g: (0, 0)),
            pl.BlockSpec((1, DM, DM), lambda g: (1, 0, 0)),
            pl.BlockSpec((1, DM, DM), lambda g: (2, 0, 0)),
        ],
        out_specs=[
            pl.BlockSpec((1, DM, 2 * TILE), lambda g: (g, 0, 0)),
            pl.BlockSpec((2 * TILE, 2 * DM), lambda g: (g, 0)),
        ],
        out_shape=[
            jax.ShapeDtypeStruct((K // 2, DM, 2 * TILE), BF),
            jax.ShapeDtypeStruct((ROWS, 2 * DM), BF),
        ],
        compiler_params=pltpu.CompilerParams(vmem_limit_bytes=56 << 20),
        cost_estimate=pl.CostEstimate(
            flops=4 * ROWS * DM * DM, bytes_accessed=5 << 20, transcendentals=ROWS * DM
        ),
        name="time_tile",
    )(delays, frequency, weights, weights)


def owner_pick(asked):
    ids = jnp.concatenate([asked] * (N // 128), axis=1)
    return (ids == iota(ids.shape, 1)).astype(F32).astype(BF)


def start_kernel(seg, state, written, r1, r2, r3, asked, memory, rows):
    start = state[...]
    for back, r in ((3, r3), (2, r2), (1, r1)):
        row = r[...]
        start = jnp.where((row.astype(F32) < 1.5) & (seg[0] >= back), row, start)
    own = written[...]
    memory[...] = jnp.where(own.astype(F32) < 1.5, own, start)
    rows[...] = dot(owner_pick(asked[...]), start).astype(BF)


def start_rows(seg, state, written, r1, r2, r3, asked):
    whole = pl.BlockSpec(memory_space=pltpu.VMEM)
    return pl.pallas_call(
        start_kernel,
        in_specs=[pl.BlockSpec(memory_space=pltpu.SMEM)] + [whole] * 6,
        out_specs=[whole] * 2,
        out_shape=[
            jax.ShapeDtypeStruct((N, DM), BF),
            jax.ShapeDtypeStruct((SLOTS, DM), BF),
        ],
        compiler_params=pltpu.CompilerParams(vmem_limit_bytes=16 << 20),
        cost_estimate=pl.CostEstimate(
            flops=2 * N * DM * SLOTS, bytes_accessed=2 << 20, transcendentals=0
        ),
        name="start_rows",
    )(seg, state, written, r1, r2, r3, asked)


def attend_kernel(
    core, slots, chosen, chosen_t, kv0, t0, kv1, t1, up, w,
    embedded, d_slots, mine, other,
    tkv, tt, wq, sem, skv, d_att, qf, src, both, dkv, att, dq, sums,
):
    moves = (
        (w.at[pl.ds(1, 2)], wq.at[pl.ds(1, 2)]),
        (w.at[0], wq.at[0]),
        (w.at[3], wq.at[3]),
        (kv0, tkv.at[0]),
        (kv1, tkv.at[1]),
        (t0, tt.at[0]),
        (t1, tt.at[1]),
    )
    copies = [pltpu.make_async_copy(a, b, sem.at[i]) for i, (a, b) in enumerate(moves)]
    for copy in copies[:4]:
        copy.start()
    rows = slots[...]
    pick = (chosen[:, 0:1] == iota((E, SLOTS), 1)).astype(F32).astype(BF)
    src[...] = dot(pick, rows)
    copies[0].wait()
    skv[:, :DM] = dot(rows, wq[1]).astype(BF)
    skv[:, DM:] = dot(rows, wq[2]).astype(BF)
    for copy in copies[4:]:
        copy.start()
    copies[1].wait()
    qf[...] = dot(pick, dot(rows, wq[0]).astype(BF))
    copies[2].wait()
    d_att[...] = dot_nt(up[...], wq[3])
    copies[3].wait()

    lane = iota((STEP, 128), 1)
    first = lane < K
    second = (lane >= K) & (lane < 2 * K)
    scale = 1.0 / math.sqrt(HEAD)

    def per_head(x):
        a = jnp.sum(jnp.where(first, x, 0.0), axis=1, keepdims=True)
        b = jnp.sum(jnp.where(second, x, 0.0), axis=1, keepdims=True)
        return jnp.where(first, a, b)

    def gather(i):
        ids = chosen[i * TILE : (i + 1) * TILE, :]
        slot = iota((TILE, SLOTS), 1)
        pick = jnp.concatenate(
            [(ids[:, 1 + k : 2 + k] == slot).astype(F32) for k in range(K)], axis=0
        ).astype(BF)
        both[i] = dot(pick, skv[...])

    def step(i, j):
        at = slice(i * TILE + j * STEP, i * TILE + (j + 1) * STEP)
        scores = jnp.zeros((STEP, 128), F32)
        d_probs = jnp.zeros((STEP, 128), F32)
        for h in range(HEADS):
            part = slice(h * HEAD, (h + 1) * HEAD)
            part_v = slice(DM + h * HEAD, DM + (h + 1) * HEAD)
            query = qf[at, part]
            d_out = d_att[at, part]
            for k in range(K):
                row = slice(k * TILE + j * STEP, k * TILE + (j + 1) * STEP)
                key = both[i, row, part] + tkv[i, row, part].astype(F32)
                value = both[i, row, part_v] + tkv[i, row, part_v].astype(F32)
                both[i, row, part] = key
                both[i, row, part_v] = value
                here = lane == h * K + k
                scores = jnp.where(here, jnp.sum(query * key, axis=1, keepdims=True), scores)
                d_probs = jnp.where(here, jnp.sum(d_out * value, axis=1, keepdims=True), d_probs)
        powered = jnp.exp(scores * scale)
        probs = powered / per_head(powered)
        d_scores = probs * (d_probs - per_head(probs * d_probs)) * scale
        for h in range(HEADS):
            part = slice(h * HEAD, (h + 1) * HEAD)
            part_v = slice(DM + h * HEAD, DM + (h + 1) * HEAD)
            query = qf[at, part]
            d_out = d_att[at, part]
            attended = jnp.zeros((STEP, HEAD), F32)
            d_query = jnp.zeros((STEP, HEAD), F32)
            for k in range(K):
                row = slice(k * TILE + j * STEP, k * TILE + (j + 1) * STEP)
                c = h * K + k
                p = jnp.broadcast_to(probs[:, c : c + 1], (STEP, HEAD))
                d = jnp.broadcast_to(d_scores[:, c : c + 1], (STEP, HEAD))
                attended += p * both[i, row, part_v]
                d_query += d * both[i, row, part]
                dkv[i, row, part] = (d * query).astype(BF)
                dkv[i, row, part_v] = (p * d_out).astype(BF)
            att[at, part] = attended.astype(BF)
            dq[at, part] = d_query.astype(BF)

    for i in range(TILES):
        gather(i)
    sub = iota((SLOTS, TILE), 0)
    s_kv = dot_t = None
    for i in range(TILES):
        if i == 1:
            copies[4].wait()
        for j in range(TILE // STEP):
            step(i, j)
        copies[5 + i].wait()
        code = jnp.concatenate([tt[i, g] for g in range(K // 2)], axis=1)
        spread = jnp.concatenate(
            [
                (sub == chosen_t[1 + k : 2 + k, i * TILE : (i + 1) * TILE]).astype(F32)
                for k in range(K)
            ],
            axis=1,
        ).astype(BF)
        one, two = dot(spread, dkv[i]), dot(code, dkv[i])
        s_kv = one if i == 0 else s_kv + one
        dot_t = two if i == 0 else dot_t + two
    s_kv = s_kv.astype(BF)
    pick_t = (iota((SLOTS, E), 0) == chosen_t[0:1, :]).astype(F32).astype(BF)
    s_q = dot(pick_t, dq[...]).astype(BF)

    def store(i, value):
        sums[i * 4 : (i + 1) * 4] = value.astype(BF).reshape(4, CORES, PIECE, DM)

    store(0, dot_tn(rows, s_q))
    g_kv = dot_t + dot_tn(rows, s_kv)
    store(1, g_kv[:, :DM])
    store(2, g_kv[:, DM:])
    store(3, dot_tn(att[...], up[...]))
    mine[...] = sums[:, core[0]]
    other[...] = sums[:, 1 - core[0]]
    embedded[...] = (dot(att[...], wq[3]) + src[...]).astype(BF)
    grads = dot(pick_t, up[...]) + dot_nt(s_q, wq[0])
    grads += dot_nt(s_kv[:, :DM], wq[1]) + dot_nt(s_kv[:, DM:], wq[2])
    d_slots[...] = grads.astype(BF)


def attend(core, slots, chosen, chosen_t, times, up, weights):
    whole = pl.BlockSpec(memory_space=pltpu.VMEM)
    far = pl.BlockSpec(memory_space=pl.ANY)
    return pl.pallas_call(
        attend_kernel,
        in_specs=[pl.BlockSpec(memory_space=pltpu.SMEM)]
        + [whole] * 3
        + [far] * 4
        + [whole]
        + [far],
        out_specs=[whole] * 4,
        out_shape=[
            jax.ShapeDtypeStruct((E, DM), BF),
            jax.ShapeDtypeStruct((SLOTS, DM), BF),
            jax.ShapeDtypeStruct((PLANE, PIECE, DM), BF),
            jax.ShapeDtypeStruct((PLANE, PIECE, DM), BF),
        ],
        scratch_shapes=[
            pltpu.VMEM((TILES, ROWS, 2 * DM), BF),
            pltpu.VMEM((TILES, K // 2, DM, 2 * TILE), BF),
            pltpu.VMEM((4, DM, DM), BF),
            pltpu.SemaphoreType.DMA((7,)),
            pltpu.VMEM((SLOTS, 2 * DM), BF),
            pltpu.VMEM((E, DM), F32),
            pltpu.VMEM((E, DM), F32),
            pltpu.VMEM((E, DM), F32),
            pltpu.VMEM((TILES, ROWS, 2 * DM), F32),
            pltpu.VMEM((TILES, ROWS, 2 * DM), BF),
            pltpu.VMEM((E, DM), BF),
            pltpu.VMEM((E, DM), BF),
            pltpu.VMEM((PLANE, CORES, PIECE, DM), BF),
        ],
        compiler_params=pltpu.CompilerParams(vmem_limit_bytes=50 << 20),
        cost_estimate=pl.CostEstimate(
            flops=6 << 30, bytes_accessed=14 << 20, transcendentals=E * 128
        ),
        name="attend",
    )(core, slots, chosen, chosen_t, *times, up, weights)


def pair_kernel(a, b, d_slots, out):
    out[:, :PIECE] = (a[...].astype(F32) + b[...].astype(F32)).astype(BF)
    out[:, PIECE:] = d_slots[...]


def pair_sum(a, b, d_slots):
    spec = pl.BlockSpec((4, PIECE, DM), lambda i: (i, 0, 0))
    return pl.pallas_call(
        pair_kernel,
        grid=(PLANE // 4,),
        in_specs=[spec, spec, pl.BlockSpec((4, 2 * CAP, DM), lambda i: (i, 0, 0))],
        out_specs=pl.BlockSpec((4, PIECE + 2 * CAP, DM), lambda i: (i, 0, 0)),
        out_shape=jax.ShapeDtypeStruct((PLANE, PIECE + 2 * CAP, DM), BF),
        compiler_params=pltpu.CompilerParams(vmem_limit_bytes=16 << 20),
        cost_estimate=pl.CostEstimate(flops=1 << 19, bytes_accessed=3 << 20, transcendentals=0),
        name="pair_sum",
    )(a, b, d_slots.reshape(PLANE, 2 * CAP, DM))


def plane_kernel(core, a, part, keep, give):
    total = a[0, :PIECE].astype(F32)
    for i in range(1, PLANE):
        total += a[i, :PIECE].astype(F32)
    total = total.astype(BF)
    for i in range(SEG):
        part[i] = total
    grads = a[:, PIECE:].astype(F32)
    low, high = grads[:, :CAP].reshape(SLOTS // 2, DM), grads[:, CAP:].reshape(SLOTS // 2, DM)
    first = core[0] == 0
    keep[...] = jnp.where(first, low, high).astype(BF)
    give[...] = jnp.where(first, high, low).astype(BF)


def plane_sum(core, a):
    whole = pl.BlockSpec(memory_space=pltpu.VMEM)
    half = jax.ShapeDtypeStruct((SLOTS // 2, DM), BF)
    return pl.pallas_call(
        plane_kernel,
        in_specs=[pl.BlockSpec(memory_space=pltpu.SMEM), whole],
        out_specs=[whole] * 3,
        out_shape=[jax.ShapeDtypeStruct((SEG, PIECE, DM), BF), half, half],
        compiler_params=pltpu.CompilerParams(vmem_limit_bytes=16 << 20),
        cost_estimate=pl.CostEstimate(flops=1 << 19, bytes_accessed=2 << 20, transcendentals=0),
        name="plane_sum",
    )(core, a)


def seg_kernel(parts, out):
    total = (parts[0].astype(F32) + parts[1].astype(F32)) + (
        parts[2].astype(F32) + parts[3].astype(F32)
    )
    total = total.astype(BF)
    for i in range(PLANE):
        out[i] = total


def seg_sum(parts):
    whole = pl.BlockSpec(memory_space=pltpu.VMEM)
    return pl.pallas_call(
        seg_kernel,
        in_specs=[whole],
        out_specs=whole,
        out_shape=jax.ShapeDtypeStruct((PLANE, PIECE, DM), BF),
        compiler_params=pltpu.CompilerParams(vmem_limit_bytes=16 << 20),
        cost_estimate=pl.CostEstimate(flops=1 << 17, bytes_accessed=1 << 20, transcendentals=0),
        name="seg_sum",
    )(parts)


def half_kernel(own, core, half, *rest):
    out, wide, sem = rest[-3:]
    place = core[0] if own else 1 - core[0]
    copies = []
    for i in range(4):
        at = pl.ds(i * PLANE // 4, PLANE // 4)
        wide[at] = half[at].astype(F32)
        copies.append(pltpu.make_async_copy(wide.at[at], out.at[at, place], sem.at[i]))
        copies[-1].start()
    for copy in copies:
        copy.wait()


def whole_grad(core, half, before=None):
    own = before is None
    far = pl.BlockSpec(memory_space=pl.ANY)
    return pl.pallas_call(
        functools.partial(half_kernel, own),
        in_specs=[pl.BlockSpec(memory_space=pltpu.SMEM), pl.BlockSpec(memory_space=pltpu.VMEM)]
        + ([] if own else [far]),
        out_specs=far,
        out_shape=jax.ShapeDtypeStruct((PLANE, CORES, PIECE, DM), F32),
        scratch_shapes=[pltpu.VMEM((PLANE, PIECE, DM), F32), pltpu.SemaphoreType.DMA((4,))],
        input_output_aliases={} if own else {2: 0},
        compiler_params=pltpu.CompilerParams(vmem_limit_bytes=16 << 20),
        cost_estimate=pl.CostEstimate(flops=1 << 18, bytes_accessed=3 << 20, transcendentals=0),
        name="own_half" if own else "far_half",
    )(core, half, *([] if own else [before]))


def owner_kernel(core, asked, keep, got, out):
    near = asked[:, core[0]].reshape(SLOTS // 2, 128)
    far = asked[:, 1 - core[0]].reshape(SLOTS // 2, 128)
    out[...] = dot_tn(owner_pick(near), keep[...]) + dot_tn(owner_pick(far), got[...])


def owner_sum(core, asked, keep, got):
    whole = pl.BlockSpec(memory_space=pltpu.VMEM)
    return pl.pallas_call(
        owner_kernel,
        in_specs=[pl.BlockSpec(memory_space=pltpu.SMEM)] + [whole] * 3,
        out_specs=whole,
        out_shape=jax.ShapeDtypeStruct((N, DM), F32),
        compiler_params=pltpu.CompilerParams(vmem_limit_bytes=16 << 20),
        cost_estimate=pl.CostEstimate(
            flops=2 * N * DM * SLOTS, bytes_accessed=1 << 20, transcendentals=0
        ),
        name="owner_sum",
    )(core, asked.reshape(PLANE, CORES, CAP, 128), keep, got)


def exchange(rows, axes, count):
    blocks = rows.reshape(count, -1, rows.shape[-1])
    return lax.all_to_all(blocks, axes, split_axis=0, concat_axis=0, tiled=True).reshape(rows.shape)


def plane(x):
    return lax.all_to_all(x, FLAT, split_axis=0, concat_axis=0, tiled=True)


def on_device(
    memory_base,
    messages,
    touched,
    gru_input,
    gru_state,
    attn_weights,
    frequency,
    request_rows,
    event_slots,
    delays,
    upstream,
):
    seg = lax.axis_index("y").reshape(1)
    core = lax.axis_index("core").reshape(1)
    written, ids = gru(
        touched, request_rows.reshape(1, SLOTS), memory_base, messages[0], gru_input, gru_state
    )
    r1 = lax.ppermute(written, "y", [(0, 1), (1, 2), (2, 3)])
    r2 = lax.ppermute(written, "y", [(0, 2), (1, 3)])
    r3 = lax.ppermute(written, "y", [(0, 3)])
    asked = exchange(ids, NODE, OWNERS)
    up = upstream[0]
    written, late, chosen, chosen_t = lax.optimization_barrier(
        (written, delays[0].T, event_slots[0], event_slots[0].T)
    )
    waves = frequency.reshape(1, DM)
    t0, kv0 = time_tile(0, late, waves, attn_weights)
    written, late, t0, kv0 = lax.optimization_barrier((written, late, t0, kv0))
    memory, rows = start_rows(seg, memory_base, written, r1, r2, r3, asked)
    rows, late = lax.optimization_barrier((rows, late))
    slots = exchange(rows, NODE, OWNERS)
    t1, kv1 = time_tile(1, late, waves, attn_weights)
    embedded, d_slots, mine, other = attend(
        core, slots, chosen, chosen_t, (kv0, t0, kv1, t1), up, attn_weights
    )
    swap = [(0, 1), (1, 0)]
    partner = lax.ppermute(other, "core", swap)
    parts = plane(pair_sum(mine, partner, d_slots))
    part, keep, give = plane_sum(core, parts)
    got = lax.ppermute(give, "core", swap)
    parts = lax.all_to_all(part, "y", split_axis=0, concat_axis=0, tiled=True)
    parts, got = lax.optimization_barrier((parts, got))
    half = plane(seg_sum(parts))
    memory_grad = owner_sum(core, asked, keep, got)
    far = lax.ppermute(half, "core", swap)
    weight_grad = whole_grad(core, far, whole_grad(core, half))
    return embedded[None], memory[None], memory_grad[None], weight_grad.reshape(4, DM, DM)


def solution(mesh):
    fine = Mesh(mesh.devices.reshape(SEG, X, Z, CORES), ("y", "x", "z", "core"))
    both = P("y", NODE, None)
    in_specs = (P(NODE, None), both, P("y", NODE), P(), P(), P(), P(), both, both, both, both)
    out_specs = (both, both, both, P())
    return jax.shard_map(
        on_device, mesh=fine, in_specs=in_specs, out_specs=out_specs, check_vma=False
    )
```

```python
import functools
import math

import jax
import jax.numpy as jnp
from jax import lax
from jax.experimental import pallas as pl
from jax.experimental.pallas import tpu as pltpu
from jax.sharding import Mesh
from jax.sharding import PartitionSpec as P

SEG, X, Z, CORES = 4, 4, 4, 2
OWNERS = X * Z * CORES
PLANE = X * Z
DM = 512
HEADS = 2
HEAD = DM // HEADS
K = 8
E = 256
N = 256
CAP = 8
SLOTS = 256
PIECE = 64
TILE = 128
TILES = E // TILE
ROWS = K * TILE
STEP = 32
ABSENT = 2.0
NODE = ("x", "z", "core")
FLAT = ("x", "z")
BF = jnp.bfloat16
F32 = jnp.float32

COS = (
    0.9999999698385398,
    -19.739198571306687,
    64.93882672218028,
    -85.44499716023202,
    60.126952745697146,
    -25.820504473745327,
    6.330480832160802,
)


def dot(a, b):
    return jnp.dot(a, b, preferred_element_type=F32)


def dot_tn(a, b):
    return lax.dot_general(a, b, (((0,), (0,)), ((), ())), preferred_element_type=F32)


def dot_nt(a, b):
    return lax.dot_general(a, b, (((1,), (1,)), ((), ())), preferred_element_type=F32)


def iota(shape, axis):
    return lax.broadcasted_iota(jnp.int32, shape, axis)


def column(row):
    n = row.shape[1]
    square = jnp.where(iota((n, n), 0) == iota((n, n), 1), row.astype(F32), 0.0)
    return jnp.sum(square, axis=1, keepdims=True)


def gru_kernel(
    touched, ids, state, message, w_input, w_state, out, spread, st, ms, wi, ws, sem
):
    moves = ((state, st), (w_state, ws), (message, ms), (w_input, wi))
    copies = [pltpu.make_async_copy(a, b, sem.at[i]) for i, (a, b) in enumerate(moves)]
    for copy in copies:
        copy.start()
    keep = column(touched[...]) > 0.5
    spread[...] = jnp.broadcast_to(column(ids[...]), (SLOTS, 128)).astype(jnp.int32)
    copies[0].wait()
    copies[1].wait()
    s = st[...]
    from_state = [dot(s, ws[:, i * DM : (i + 1) * DM]) for i in range(3)]
    copies[2].wait()
    copies[3].wait()
    m = ms[...]
    update = jax.nn.sigmoid(dot(m, wi[:, :DM]) + from_state[0])
    reset = jax.nn.sigmoid(dot(m, wi[:, DM : 2 * DM]) + from_state[1])
    candidate = jnp.tanh(dot(m, wi[:, 2 * DM :]) + reset * from_state[2])
    fresh = (1.0 - update) * candidate + update * s.astype(F32)
    out[...] = jnp.where(keep, fresh, ABSENT).astype(BF)


def gru(touched, ids, state, message, w_input, w_state):
    whole = pl.BlockSpec(memory_space=pltpu.VMEM)
    far = pl.BlockSpec(memory_space=pl.ANY)
    return pl.pallas_call(
        gru_kernel,
        in_specs=[whole] * 2 + [far] * 4,
        out_specs=[whole] * 2,
        out_shape=[
            jax.ShapeDtypeStruct((N, DM), BF),
            jax.ShapeDtypeStruct((SLOTS, 128), jnp.int32),
        ],
        scratch_shapes=[
            pltpu.VMEM((N, DM), BF),
            pltpu.VMEM((N, DM), BF),
            pltpu.VMEM((DM, 3 * DM), BF),
            pltpu.VMEM((DM, 3 * DM), BF),
            pltpu.SemaphoreType.DMA((4,)),
        ],
        compiler_params=pltpu.CompilerParams(vmem_limit_bytes=56 << 20),
        cost_estimate=pl.CostEstimate(
            flops=4 * N * DM * 3 * DM, bytes_accessed=4 << 20, transcendentals=3 * N * DM
        ),
        name="gru",
    )(touched, ids, state, message, w_input, w_state)


def time_kernel(delays, frequency, w, code_t, time_kv):
    turns = frequency[...] * (1.0 / (2.0 * math.pi))
    high = jnp.round(turns * 16384.0) * (1.0 / 16384.0)
    low = turns - high
    for tile in range(TILES):
        for k in range(K):
            delay = column(delays[k : k + 1, tile * TILE : (tile + 1) * TILE])
            coarse = delay * high
            part = (coarse - jnp.round(coarse)) + delay * low
            u = part * part
            wave = jnp.full_like(u, COS[-1])
            for c in COS[-2::-1]:
                wave = wave * u + c
            at = slice(k * TILE, (k + 1) * TILE)
            code_t[tile, :, at] = wave.T.astype(BF)
            wave = wave.astype(BF)
            time_kv[tile, at, :DM] = dot(wave, w[1]).astype(BF)
            time_kv[tile, at, DM:] = dot(wave, w[2]).astype(BF)


def time_parts(delays, frequency, weights):
    whole = pl.BlockSpec(memory_space=pltpu.VMEM)
    return pl.pallas_call(
        time_kernel,
        in_specs=[whole] * 3,
        out_specs=[whole] * 2,
        out_shape=[
            jax.ShapeDtypeStruct((TILES, DM, ROWS), BF),
            jax.ShapeDtypeStruct((TILES, ROWS, 2 * DM), BF),
        ],
        compiler_params=pltpu.CompilerParams(vmem_limit_bytes=24 << 20),
        cost_estimate=pl.CostEstimate(
            flops=4 * K * E * DM * DM, bytes_accessed=8 << 20, transcendentals=K * E * DM
        ),
        name="time_parts",
    )(delays, frequency, weights)


def owner_pick(asked):
    ids = jnp.concatenate([asked] * (N // 128), axis=1)
    return (ids == iota(ids.shape, 1)).astype(F32).astype(BF)


def start_kernel(seg, state, written, r1, r2, r3, asked, memory, rows):
    start = state[...]
    for back, r in ((3, r3), (2, r2), (1, r1)):
        row = r[...]
        start = jnp.where((row.astype(F32) < 1.5) & (seg[0] >= back), row, start)
    own = written[...]
    memory[...] = jnp.where(own.astype(F32) < 1.5, own, start)
    rows[...] = dot(owner_pick(asked[...]), start).astype(BF)


def start_rows(seg, state, written, r1, r2, r3, asked):
    whole = pl.BlockSpec(memory_space=pltpu.VMEM)
    return pl.pallas_call(
        start_kernel,
        in_specs=[pl.BlockSpec(memory_space=pltpu.SMEM)] + [whole] * 6,
        out_specs=[whole] * 2,
        out_shape=[
            jax.ShapeDtypeStruct((N, DM), BF),
            jax.ShapeDtypeStruct((SLOTS, DM), BF),
        ],
        compiler_params=pltpu.CompilerParams(vmem_limit_bytes=16 << 20),
        cost_estimate=pl.CostEstimate(
            flops=2 * N * DM * SLOTS, bytes_accessed=2 << 20, transcendentals=0
        ),
        name="start_rows",
    )(seg, state, written, r1, r2, r3, asked)


def attend_kernel(
    core, slots, chosen, chosen_t, tkv, tt, up, wq,
    embedded, d_slots, mine, other,
    skv, d_att, qf, src, both, dkv, att, dq, sums,
):
    rows = slots[...]
    pick = (chosen[:, 0:1] == iota((E, SLOTS), 1)).astype(F32).astype(BF)
    src[...] = dot(pick, rows)
    skv[:, :DM] = dot(rows, wq[1]).astype(BF)
    skv[:, DM:] = dot(rows, wq[2]).astype(BF)
    qf[...] = dot(pick, dot(rows, wq[0]).astype(BF))
    d_att[...] = dot_nt(up[...], wq[3])

    lane = iota((STEP, 128), 1)
    first = lane < K
    second = (lane >= K) & (lane < 2 * K)
    scale = 1.0 / math.sqrt(HEAD)

    def per_head(x):
        a = jnp.sum(jnp.where(first, x, 0.0), axis=1, keepdims=True)
        b = jnp.sum(jnp.where(second, x, 0.0), axis=1, keepdims=True)
        return jnp.where(first, a, b)

    def gather(i):
        ids = chosen[i * TILE : (i + 1) * TILE, :]
        slot = iota((TILE, SLOTS), 1)
        pick = jnp.concatenate(
            [(ids[:, 1 + k : 2 + k] == slot).astype(F32) for k in range(K)], axis=0
        ).astype(BF)
        both[i] = dot(pick, skv[...])

    def step(i, j):
        at = slice(i * TILE + j * STEP, i * TILE + (j + 1) * STEP)
        scores = jnp.zeros((STEP, 128), F32)
        d_probs = jnp.zeros((STEP, 128), F32)
        for h in range(HEADS):
            part = slice(h * HEAD, (h + 1) * HEAD)
            part_v = slice(DM + h * HEAD, DM + (h + 1) * HEAD)
            query = qf[at, part]
            d_out = d_att[at, part]
            for k in range(K):
                row = slice(k * TILE + j * STEP, k * TILE + (j + 1) * STEP)
                key = both[i, row, part] + tkv[i, row, part].astype(F32)
                value = both[i, row, part_v] + tkv[i, row, part_v].astype(F32)
                both[i, row, part] = key
                both[i, row, part_v] = value
                here = lane == h * K + k
                scores = jnp.where(here, jnp.sum(query * key, axis=1, keepdims=True), scores)
                d_probs = jnp.where(here, jnp.sum(d_out * value, axis=1, keepdims=True), d_probs)
        powered = jnp.exp(scores * scale)
        probs = powered / per_head(powered)
        d_scores = probs * (d_probs - per_head(probs * d_probs)) * scale
        for h in range(HEADS):
            part = slice(h * HEAD, (h + 1) * HEAD)
            part_v = slice(DM + h * HEAD, DM + (h + 1) * HEAD)
            query = qf[at, part]
            d_out = d_att[at, part]
            attended = jnp.zeros((STEP, HEAD), F32)
            d_query = jnp.zeros((STEP, HEAD), F32)
            for k in range(K):
                row = slice(k * TILE + j * STEP, k * TILE + (j + 1) * STEP)
                c = h * K + k
                p = jnp.broadcast_to(probs[:, c : c + 1], (STEP, HEAD))
                d = jnp.broadcast_to(d_scores[:, c : c + 1], (STEP, HEAD))
                attended += p * both[i, row, part_v]
                d_query += d * both[i, row, part]
                dkv[i, row, part] = (d * query).astype(BF)
                dkv[i, row, part_v] = (p * d_out).astype(BF)
            att[at, part] = attended.astype(BF)
            dq[at, part] = d_query.astype(BF)

    for i in range(TILES):
        gather(i)
    sub = iota((SLOTS, TILE), 0)
    s_kv = dot_t = None
    for i in range(TILES):
        for j in range(TILE // STEP):
            step(i, j)
        spread = jnp.concatenate(
            [
                (sub == chosen_t[1 + k : 2 + k, i * TILE : (i + 1) * TILE]).astype(F32)
                for k in range(K)
            ],
            axis=1,
        ).astype(BF)
        one, two = dot(spread, dkv[i]), dot(tt[i], dkv[i])
        s_kv = one if i == 0 else s_kv + one
        dot_t = two if i == 0 else dot_t + two
    s_kv = s_kv.astype(BF)
    pick_t = (iota((SLOTS, E), 0) == chosen_t[0:1, :]).astype(F32).astype(BF)
    s_q = dot(pick_t, dq[...]).astype(BF)

    def store(i, value):
        sums[i * 4 : (i + 1) * 4] = value.astype(BF).reshape(4, CORES, PIECE, DM)

    store(0, dot_tn(rows, s_q))
    g_kv = dot_t + dot_tn(rows, s_kv)
    store(1, g_kv[:, :DM])
    store(2, g_kv[:, DM:])
    store(3, dot_tn(att[...], up[...]))
    mine[...] = sums[:, core[0]]
    other[...] = sums[:, 1 - core[0]]
    embedded[...] = (dot(att[...], wq[3]) + src[...]).astype(BF)
    grads = dot(pick_t, up[...]) + dot_nt(s_q, wq[0])
    grads += dot_nt(s_kv[:, :DM], wq[1]) + dot_nt(s_kv[:, DM:], wq[2])
    d_slots[...] = grads.astype(BF)


def attend(core, slots, chosen, chosen_t, time_kv, code_t, up, weights):
    whole = pl.BlockSpec(memory_space=pltpu.VMEM)
    return pl.pallas_call(
        attend_kernel,
        in_specs=[pl.BlockSpec(memory_space=pltpu.SMEM)] + [whole] * 7,
        out_specs=[whole] * 4,
        out_shape=[
            jax.ShapeDtypeStruct((E, DM), BF),
            jax.ShapeDtypeStruct((SLOTS, DM), BF),
            jax.ShapeDtypeStruct((PLANE, PIECE, DM), BF),
            jax.ShapeDtypeStruct((PLANE, PIECE, DM), BF),
        ],
        scratch_shapes=[
            pltpu.VMEM((SLOTS, 2 * DM), BF),
            pltpu.VMEM((E, DM), F32),
            pltpu.VMEM((E, DM), F32),
            pltpu.VMEM((E, DM), F32),
            pltpu.VMEM((TILES, ROWS, 2 * DM), F32),
            pltpu.VMEM((TILES, ROWS, 2 * DM), BF),
            pltpu.VMEM((E, DM), BF),
            pltpu.VMEM((E, DM), BF),
            pltpu.VMEM((PLANE, CORES, PIECE, DM), BF),
        ],
        compiler_params=pltpu.CompilerParams(vmem_limit_bytes=40 << 20),
        cost_estimate=pl.CostEstimate(
            flops=6 << 30, bytes_accessed=14 << 20, transcendentals=E * 128
        ),
        name="attend",
    )(core, slots, chosen, chosen_t, time_kv, code_t, up, weights)


def pair_kernel(a, b, d_slots, out):
    out[:, :PIECE] = (a[...].astype(F32) + b[...].astype(F32)).astype(BF)
    out[:, PIECE:] = d_slots[...]


def pair_sum(a, b, d_slots):
    spec = pl.BlockSpec((4, PIECE, DM), lambda i: (i, 0, 0))
    return pl.pallas_call(
        pair_kernel,
        grid=(PLANE // 4,),
        in_specs=[spec, spec, pl.BlockSpec((4, 2 * CAP, DM), lambda i: (i, 0, 0))],
        out_specs=pl.BlockSpec((4, PIECE + 2 * CAP, DM), lambda i: (i, 0, 0)),
        out_shape=jax.ShapeDtypeStruct((PLANE, PIECE + 2 * CAP, DM), BF),
        compiler_params=pltpu.CompilerParams(vmem_limit_bytes=16 << 20),
        cost_estimate=pl.CostEstimate(flops=1 << 19, bytes_accessed=3 << 20, transcendentals=0),
        name="pair_sum",
    )(a, b, d_slots.reshape(PLANE, 2 * CAP, DM))


def plane_kernel(core, a, part, keep, give):
    total = a[0, :PIECE].astype(F32)
    for i in range(1, PLANE):
        total += a[i, :PIECE].astype(F32)
    part[...] = total.astype(BF)
    grads = a[:, PIECE:].astype(F32)
    low, high = grads[:, :CAP].reshape(SLOTS // 2, DM), grads[:, CAP:].reshape(SLOTS // 2, DM)
    first = core[0] == 0
    keep[...] = jnp.where(first, low, high).astype(BF)
    give[...] = jnp.where(first, high, low).astype(BF)


def plane_sum(core, a):
    whole = pl.BlockSpec(memory_space=pltpu.VMEM)
    half = jax.ShapeDtypeStruct((SLOTS // 2, DM), BF)
    return pl.pallas_call(
        plane_kernel,
        in_specs=[pl.BlockSpec(memory_space=pltpu.SMEM), whole],
        out_specs=[whole] * 3,
        out_shape=[jax.ShapeDtypeStruct((PIECE, DM), BF), half, half],
        compiler_params=pltpu.CompilerParams(vmem_limit_bytes=16 << 20),
        cost_estimate=pl.CostEstimate(flops=1 << 19, bytes_accessed=2 << 20, transcendentals=0),
        name="plane_sum",
    )(core, a)


def seg_kernel(seg, own, r1, r2, r3, out, parts):
    for back, r in enumerate((own, r1, r2, r3)):
        parts[lax.rem(seg[0] + SEG - back, SEG)] = r[...].astype(F32)
    total = ((parts[0] + parts[1]) + (parts[2] + parts[3])).astype(BF)
    for i in range(PLANE):
        out[i] = total


def seg_sum(seg, own, r1, r2, r3):
    whole = pl.BlockSpec(memory_space=pltpu.VMEM)
    return pl.pallas_call(
        seg_kernel,
        in_specs=[pl.BlockSpec(memory_space=pltpu.SMEM)] + [whole] * 4,
        out_specs=whole,
        out_shape=jax.ShapeDtypeStruct((PLANE, PIECE, DM), BF),
        scratch_shapes=[pltpu.VMEM((SEG, PIECE, DM), F32)],
        compiler_params=pltpu.CompilerParams(vmem_limit_bytes=16 << 20),
        cost_estimate=pl.CostEstimate(flops=1 << 17, bytes_accessed=1 << 20, transcendentals=0),
        name="seg_sum",
    )(seg, own, r1, r2, r3)


def half_kernel(own, core, half, *rest):
    out, wide, sem = rest[-3:]
    place = core[0] if own else 1 - core[0]
    copies = []
    for i in range(4):
        at = pl.ds(i * PLANE // 4, PLANE // 4)
        wide[at] = half[at].astype(F32)
        copies.append(pltpu.make_async_copy(wide.at[at], out.at[at, place], sem.at[i]))
        copies[-1].start()
    for copy in copies:
        copy.wait()


def whole_grad(core, half, before=None):
    own = before is None
    far = pl.BlockSpec(memory_space=pl.ANY)
    return pl.pallas_call(
        functools.partial(half_kernel, own),
        in_specs=[pl.BlockSpec(memory_space=pltpu.SMEM), pl.BlockSpec(memory_space=pltpu.VMEM)]
        + ([] if own else [far]),
        out_specs=far,
        out_shape=jax.ShapeDtypeStruct((PLANE, CORES, PIECE, DM), F32),
        scratch_shapes=[pltpu.VMEM((PLANE, PIECE, DM), F32), pltpu.SemaphoreType.DMA((4,))],
        input_output_aliases={} if own else {2: 0},
        compiler_params=pltpu.CompilerParams(vmem_limit_bytes=16 << 20),
        cost_estimate=pl.CostEstimate(flops=1 << 18, bytes_accessed=3 << 20, transcendentals=0),
        name="own_half" if own else "far_half",
    )(core, half, *([] if own else [before]))


def owner_kernel(core, asked, keep, got, out):
    near = asked[:, core[0]].reshape(SLOTS // 2, 128)
    far = asked[:, 1 - core[0]].reshape(SLOTS // 2, 128)
    out[...] = dot_tn(owner_pick(near), keep[...]) + dot_tn(owner_pick(far), got[...])


def owner_sum(core, asked, keep, got):
    whole = pl.BlockSpec(memory_space=pltpu.VMEM)
    return pl.pallas_call(
        owner_kernel,
        in_specs=[pl.BlockSpec(memory_space=pltpu.SMEM)] + [whole] * 3,
        out_specs=whole,
        out_shape=jax.ShapeDtypeStruct((N, DM), F32),
        compiler_params=pltpu.CompilerParams(vmem_limit_bytes=16 << 20),
        cost_estimate=pl.CostEstimate(
            flops=2 * N * DM * SLOTS, bytes_accessed=1 << 20, transcendentals=0
        ),
        name="owner_sum",
    )(core, asked.reshape(PLANE, CORES, CAP, 128), keep, got)


def exchange(rows, axes, count):
    blocks = rows.reshape(count, -1, rows.shape[-1])
    return lax.all_to_all(blocks, axes, split_axis=0, concat_axis=0, tiled=True).reshape(rows.shape)


def plane(x):
    return lax.all_to_all(x, FLAT, split_axis=0, concat_axis=0, tiled=True)


def on_device(
    memory_base,
    messages,
    touched,
    gru_input,
    gru_state,
    attn_weights,
    frequency,
    request_rows,
    event_slots,
    delays,
    upstream,
):
    seg = lax.axis_index("y").reshape(1)
    core = lax.axis_index("core").reshape(1)
    written, ids = gru(
        touched, request_rows.reshape(1, SLOTS), memory_base, messages[0], gru_input, gru_state
    )
    written, ids, seg, core, late, chosen, chosen_t = lax.optimization_barrier(
        (written, ids, seg, core, delays[0].T, event_slots[0], event_slots[0].T)
    )
    r1 = lax.ppermute(written, "y", [(0, 1), (1, 2), (2, 3)])
    r2 = lax.ppermute(written, "y", [(0, 2), (1, 3)])
    r3 = lax.ppermute(written, "y", [(0, 3)])
    asked = exchange(ids, NODE, OWNERS)
    asked, late = lax.optimization_barrier((asked, late))
    code_t, time_kv = time_parts(late, frequency.reshape(1, DM), attn_weights)
    written, code_t, time_kv = lax.optimization_barrier((written, code_t, time_kv))
    memory, rows = start_rows(seg, memory_base, written, r1, r2, r3, asked)
    slots = exchange(rows, NODE, OWNERS)
    up = upstream[0]
    embedded, d_slots, mine, other = attend(
        core, slots, chosen, chosen_t, time_kv, code_t, up, attn_weights
    )
    swap = [(0, 1), (1, 0)]
    partner = lax.ppermute(other, "core", swap)
    parts = plane(pair_sum(mine, partner, d_slots))
    part, keep, give = plane_sum(core, parts)
    got = lax.ppermute(give, "core", swap)
    r2, r1, r3 = (
        lax.ppermute(part, "y", [(i, (i + s) % SEG) for i in range(SEG)]) for s in (2, 1, 3)
    )
    memory_grad = owner_sum(core, asked, keep, got)
    r2, memory_grad = lax.optimization_barrier((r2, memory_grad))
    half = plane(seg_sum(seg, part, r1, r2, r3))
    far = lax.ppermute(half, "core", swap)
    weight_grad = whole_grad(core, far, whole_grad(core, half))
    return embedded[None], memory[None], memory_grad[None], weight_grad.reshape(4, DM, DM)


def solution(mesh):
    fine = Mesh(mesh.devices.reshape(SEG, X, Z, CORES), ("y", "x", "z", "core"))
    both = P("y", NODE, None)
    in_specs = (P(NODE, None), both, P("y", NODE), P(), P(), P(), P(), both, both, both, both)
    out_specs = (both, both, both, P())
    return jax.shard_map(
        on_device, mesh=fine, in_specs=in_specs, out_specs=out_specs, check_vma=False
    )
```

```python
import functools
import math

import jax
import jax.numpy as jnp
from jax import lax
from jax.experimental import pallas as pl
from jax.experimental.pallas import tpu as pltpu
from jax.sharding import Mesh
from jax.sharding import PartitionSpec as P

SEG, X, Z, CORES = 4, 4, 4, 2
OWNERS = X * Z * CORES
PLANE = X * Z
DM = 512
HEADS = 2
HEAD = DM // HEADS
K = 8
E = 256
N = 256
CAP = 8
SLOTS = 256
PIECE = 64
TILE = 128
TILES = E // TILE
ROWS = K * TILE
STEP = 32
ABSENT = 2.0
NODE = ("x", "z", "core")
FLAT = ("x", "z")
BF = jnp.bfloat16
F32 = jnp.float32

COS = (
    0.9999999698385398,
    -19.739198571306687,
    64.93882672218028,
    -85.44499716023202,
    60.126952745697146,
    -25.820504473745327,
    6.330480832160802,
)


def dot(a, b):
    return jnp.dot(a, b, preferred_element_type=F32)


def dot_tn(a, b):
    return lax.dot_general(a, b, (((0,), (0,)), ((), ())), preferred_element_type=F32)


def dot_nt(a, b):
    return lax.dot_general(a, b, (((1,), (1,)), ((), ())), preferred_element_type=F32)


def iota(shape, axis):
    return lax.broadcasted_iota(jnp.int32, shape, axis)


def column(row):
    n = row.shape[1]
    square = jnp.where(iota((n, n), 0) == iota((n, n), 1), row.astype(F32), 0.0)
    return jnp.sum(square, axis=1, keepdims=True)


def gru_kernel(
    touched, ids, state, message, w_input, w_state, out, spread, st, ms, wi, ws, sem
):
    moves = ((state, st), (w_state, ws), (message, ms), (w_input, wi))
    copies = [pltpu.make_async_copy(a, b, sem.at[i]) for i, (a, b) in enumerate(moves)]
    for copy in copies:
        copy.start()
    keep = column(touched[...]) > 0.5
    spread[...] = jnp.broadcast_to(column(ids[...]), (SLOTS, 128)).astype(jnp.int32)
    copies[0].wait()
    copies[1].wait()
    s = st[...]
    from_state = [dot(s, ws[:, i * DM : (i + 1) * DM]) for i in range(3)]
    copies[2].wait()
    copies[3].wait()
    m = ms[...]
    update = jax.nn.sigmoid(dot(m, wi[:, :DM]) + from_state[0])
    reset = jax.nn.sigmoid(dot(m, wi[:, DM : 2 * DM]) + from_state[1])
    candidate = jnp.tanh(dot(m, wi[:, 2 * DM :]) + reset * from_state[2])
    fresh = (1.0 - update) * candidate + update * s.astype(F32)
    out[...] = jnp.where(keep, fresh, ABSENT).astype(BF)


def gru(touched, ids, state, message, w_input, w_state):
    whole = pl.BlockSpec(memory_space=pltpu.VMEM)
    far = pl.BlockSpec(memory_space=pl.ANY)
    return pl.pallas_call(
        gru_kernel,
        in_specs=[whole] * 2 + [far] * 4,
        out_specs=[whole] * 2,
        out_shape=[
            jax.ShapeDtypeStruct((N, DM), BF),
            jax.ShapeDtypeStruct((SLOTS, 128), jnp.int32),
        ],
        scratch_shapes=[
            pltpu.VMEM((N, DM), BF),
            pltpu.VMEM((N, DM), BF),
            pltpu.VMEM((DM, 3 * DM), BF),
            pltpu.VMEM((DM, 3 * DM), BF),
            pltpu.SemaphoreType.DMA((4,)),
        ],
        compiler_params=pltpu.CompilerParams(vmem_limit_bytes=56 << 20),
        cost_estimate=pl.CostEstimate(
            flops=4 * N * DM * 3 * DM, bytes_accessed=4 << 20, transcendentals=3 * N * DM
        ),
        name="gru",
    )(touched, ids, state, message, w_input, w_state)


def time_kernel(delays, frequency, w, chosen, code_t, time_kv, picked):
    lane = iota((E, 128), 1)
    columns = jnp.zeros((E, 128), F32)
    for j in range(K + 1):
        columns = jnp.where(lane == j, column(chosen[j]), columns)
    picked[...] = columns.astype(jnp.int32)
    turns = frequency[...] * (1.0 / (2.0 * math.pi))
    high = jnp.round(turns * 16384.0) * (1.0 / 16384.0)
    low = turns - high
    for tile in range(TILES):
        for k in range(K):
            delay = column(delays[k : k + 1, tile * TILE : (tile + 1) * TILE])
            coarse = delay * high
            part = (coarse - jnp.round(coarse)) + delay * low
            u = part * part
            wave = jnp.full_like(u, COS[-1])
            for c in COS[-2::-1]:
                wave = wave * u + c
            at = slice(k * TILE, (k + 1) * TILE)
            code_t[tile, :, at] = wave.T.astype(BF)
            wave = wave.astype(BF)
            time_kv[tile, at, :DM] = dot(wave, w[1]).astype(BF)
            time_kv[tile, at, DM:] = dot(wave, w[2]).astype(BF)


def time_parts(delays, frequency, weights, chosen):
    whole = pl.BlockSpec(memory_space=pltpu.VMEM)
    return pl.pallas_call(
        time_kernel,
        in_specs=[whole] * 4,
        out_specs=[whole] * 3,
        out_shape=[
            jax.ShapeDtypeStruct((TILES, DM, ROWS), BF),
            jax.ShapeDtypeStruct((TILES, ROWS, 2 * DM), BF),
            jax.ShapeDtypeStruct((E, 128), jnp.int32),
        ],
        compiler_params=pltpu.CompilerParams(vmem_limit_bytes=24 << 20),
        cost_estimate=pl.CostEstimate(
            flops=4 * K * E * DM * DM, bytes_accessed=8 << 20, transcendentals=K * E * DM
        ),
        name="time_parts",
    )(delays, frequency, weights, chosen)


def owner_pick(asked):
    ids = jnp.concatenate([asked] * (N // 128), axis=1)
    return (ids == iota(ids.shape, 1)).astype(F32).astype(BF)


def start_kernel(seg, state, written, r1, r2, r3, asked, memory, rows):
    start = state[...]
    for back, r in ((3, r3), (2, r2), (1, r1)):
        row = r[...]
        start = jnp.where((row.astype(F32) < 1.5) & (seg[0] >= back), row, start)
    own = written[...]
    memory[...] = jnp.where(own.astype(F32) < 1.5, own, start)
    rows[...] = dot(owner_pick(asked[...]), start).astype(BF)


def start_rows(seg, state, written, r1, r2, r3, asked):
    whole = pl.BlockSpec(memory_space=pltpu.VMEM)
    return pl.pallas_call(
        start_kernel,
        in_specs=[pl.BlockSpec(memory_space=pltpu.SMEM)] + [whole] * 6,
        out_specs=[whole] * 2,
        out_shape=[
            jax.ShapeDtypeStruct((N, DM), BF),
            jax.ShapeDtypeStruct((SLOTS, DM), BF),
        ],
        compiler_params=pltpu.CompilerParams(vmem_limit_bytes=16 << 20),
        cost_estimate=pl.CostEstimate(
            flops=2 * N * DM * SLOTS, bytes_accessed=2 << 20, transcendentals=0
        ),
        name="start_rows",
    )(seg, state, written, r1, r2, r3, asked)


def attend_kernel(
    core, slots, chosen, chosen_t, tkv, tt, up, wq,
    embedded, d_slots, mine, other,
    skv, d_att, qf, src, both, dkv, att, dq, sums,
):
    rows = slots[...]
    pick = (chosen[:, 0:1] == iota((E, SLOTS), 1)).astype(F32).astype(BF)
    src[...] = dot(pick, rows)
    skv[:, :DM] = dot(rows, wq[1]).astype(BF)
    skv[:, DM:] = dot(rows, wq[2]).astype(BF)
    qf[...] = dot(pick, dot(rows, wq[0]).astype(BF))
    d_att[...] = dot_nt(up[...], wq[3])

    lane = iota((STEP, 128), 1)
    first = lane < K
    second = (lane >= K) & (lane < 2 * K)
    scale = 1.0 / math.sqrt(HEAD)

    def per_head(x):
        a = jnp.sum(jnp.where(first, x, 0.0), axis=1, keepdims=True)
        b = jnp.sum(jnp.where(second, x, 0.0), axis=1, keepdims=True)
        return jnp.where(first, a, b)

    def gather(i):
        ids = chosen[i * TILE : (i + 1) * TILE, :]
        slot = iota((TILE, SLOTS), 1)
        pick = jnp.concatenate(
            [(ids[:, 1 + k : 2 + k] == slot).astype(F32) for k in range(K)], axis=0
        ).astype(BF)
        both[i] = dot(pick, skv[...])

    def step(i, j):
        at = slice(i * TILE + j * STEP, i * TILE + (j + 1) * STEP)
        scores = jnp.zeros((STEP, 128), F32)
        d_probs = jnp.zeros((STEP, 128), F32)
        for h in range(HEADS):
            part = slice(h * HEAD, (h + 1) * HEAD)
            part_v = slice(DM + h * HEAD, DM + (h + 1) * HEAD)
            query = qf[at, part]
            d_out = d_att[at, part]
            for k in range(K):
                row = slice(k * TILE + j * STEP, k * TILE + (j + 1) * STEP)
                key = both[i, row, part] + tkv[i, row, part].astype(F32)
                value = both[i, row, part_v] + tkv[i, row, part_v].astype(F32)
                both[i, row, part] = key
                both[i, row, part_v] = value
                here = lane == h * K + k
                scores = jnp.where(here, jnp.sum(query * key, axis=1, keepdims=True), scores)
                d_probs = jnp.where(here, jnp.sum(d_out * value, axis=1, keepdims=True), d_probs)
        powered = jnp.exp(scores * scale)
        probs = powered / per_head(powered)
        d_scores = probs * (d_probs - per_head(probs * d_probs)) * scale
        for h in range(HEADS):
            part = slice(h * HEAD, (h + 1) * HEAD)
            part_v = slice(DM + h * HEAD, DM + (h + 1) * HEAD)
            query = qf[at, part]
            d_out = d_att[at, part]
            attended = jnp.zeros((STEP, HEAD), F32)
            d_query = jnp.zeros((STEP, HEAD), F32)
            for k in range(K):
                row = slice(k * TILE + j * STEP, k * TILE + (j + 1) * STEP)
                c = h * K + k
                p = jnp.broadcast_to(probs[:, c : c + 1], (STEP, HEAD))
                d = jnp.broadcast_to(d_scores[:, c : c + 1], (STEP, HEAD))
                attended += p * both[i, row, part_v]
                d_query += d * both[i, row, part]
                dkv[i, row, part] = (d * query).astype(BF)
                dkv[i, row, part_v] = (p * d_out).astype(BF)
            att[at, part] = attended.astype(BF)
            dq[at, part] = d_query.astype(BF)

    for i in range(TILES):
        gather(i)
    sub = iota((SLOTS, TILE), 0)
    s_kv = dot_t = None
    for i in range(TILES):
        for j in range(TILE // STEP):
            step(i, j)
        spread = jnp.concatenate(
            [
                (sub == chosen_t[1 + k, :, i * TILE : (i + 1) * TILE]).astype(F32)
                for k in range(K)
            ],
            axis=1,
        ).astype(BF)
        one, two = dot(spread, dkv[i]), dot(tt[i], dkv[i])
        s_kv = one if i == 0 else s_kv + one
        dot_t = two if i == 0 else dot_t + two
    s_kv = s_kv.astype(BF)
    pick_t = (iota((SLOTS, E), 0) == chosen_t[0]).astype(F32).astype(BF)
    s_q = dot(pick_t, dq[...]).astype(BF)

    def store(i, value):
        sums[i * 4 : (i + 1) * 4] = value.astype(BF).reshape(4, CORES, PIECE, DM)

    store(0, dot_tn(rows, s_q))
    g_kv = dot_t + dot_tn(rows, s_kv)
    store(1, g_kv[:, :DM])
    store(2, g_kv[:, DM:])
    store(3, dot_tn(att[...], up[...]))
    mine[...] = sums[:, core[0]]
    other[...] = sums[:, 1 - core[0]]
    embedded[...] = (dot(att[...], wq[3]) + src[...]).astype(BF)
    grads = dot(pick_t, up[...]) + dot_nt(s_q, wq[0])
    grads += dot_nt(s_kv[:, :DM], wq[1]) + dot_nt(s_kv[:, DM:], wq[2])
    d_slots[...] = grads.astype(BF)


def attend(core, slots, chosen, chosen_t, time_kv, code_t, up, weights):
    whole = pl.BlockSpec(memory_space=pltpu.VMEM)
    return pl.pallas_call(
        attend_kernel,
        in_specs=[pl.BlockSpec(memory_space=pltpu.SMEM)] + [whole] * 7,
        out_specs=[whole] * 4,
        out_shape=[
            jax.ShapeDtypeStruct((E, DM), BF),
            jax.ShapeDtypeStruct((SLOTS, DM), BF),
            jax.ShapeDtypeStruct((PLANE, PIECE, DM), BF),
            jax.ShapeDtypeStruct((PLANE, PIECE, DM), BF),
        ],
        scratch_shapes=[
            pltpu.VMEM((SLOTS, 2 * DM), BF),
            pltpu.VMEM((E, DM), F32),
            pltpu.VMEM((E, DM), F32),
            pltpu.VMEM((E, DM), F32),
            pltpu.VMEM((TILES, ROWS, 2 * DM), F32),
            pltpu.VMEM((TILES, ROWS, 2 * DM), BF),
            pltpu.VMEM((E, DM), BF),
            pltpu.VMEM((E, DM), BF),
            pltpu.VMEM((PLANE, CORES, PIECE, DM), BF),
        ],
        compiler_params=pltpu.CompilerParams(vmem_limit_bytes=40 << 20),
        cost_estimate=pl.CostEstimate(
            flops=6 << 30, bytes_accessed=14 << 20, transcendentals=E * 128
        ),
        name="attend",
    )(core, slots, chosen, chosen_t, time_kv, code_t, up, weights)


def pair_kernel(a, b, d_slots, out):
    out[:, :PIECE] = (a[...].astype(F32) + b[...].astype(F32)).astype(BF)
    out[:, PIECE:] = d_slots[...]


def pair_sum(a, b, d_slots):
    spec = pl.BlockSpec((4, PIECE, DM), lambda i: (i, 0, 0))
    return pl.pallas_call(
        pair_kernel,
        grid=(PLANE // 4,),
        in_specs=[spec, spec, pl.BlockSpec((4, 2 * CAP, DM), lambda i: (i, 0, 0))],
        out_specs=pl.BlockSpec((4, PIECE + 2 * CAP, DM), lambda i: (i, 0, 0)),
        out_shape=jax.ShapeDtypeStruct((PLANE, PIECE + 2 * CAP, DM), BF),
        compiler_params=pltpu.CompilerParams(vmem_limit_bytes=16 << 20),
        cost_estimate=pl.CostEstimate(flops=1 << 19, bytes_accessed=3 << 20, transcendentals=0),
        name="pair_sum",
    )(a, b, d_slots.reshape(PLANE, 2 * CAP, DM))


def plane_kernel(core, a, part, keep, give):
    total = a[0, :PIECE].astype(F32)
    for i in range(1, PLANE):
        total += a[i, :PIECE].astype(F32)
    part[...] = total.astype(BF)
    grads = a[:, PIECE:].astype(F32)
    low, high = grads[:, :CAP].reshape(SLOTS // 2, DM), grads[:, CAP:].reshape(SLOTS // 2, DM)
    first = core[0] == 0
    keep[...] = jnp.where(first, low, high).astype(BF)
    give[...] = jnp.where(first, high, low).astype(BF)


def plane_sum(core, a):
    whole = pl.BlockSpec(memory_space=pltpu.VMEM)
    half = jax.ShapeDtypeStruct((SLOTS // 2, DM), BF)
    return pl.pallas_call(
        plane_kernel,
        in_specs=[pl.BlockSpec(memory_space=pltpu.SMEM), whole],
        out_specs=[whole] * 3,
        out_shape=[jax.ShapeDtypeStruct((PIECE, DM), BF), half, half],
        compiler_params=pltpu.CompilerParams(vmem_limit_bytes=16 << 20),
        cost_estimate=pl.CostEstimate(flops=1 << 19, bytes_accessed=2 << 20, transcendentals=0),
        name="plane_sum",
    )(core, a)


def seg_kernel(seg, own, r1, r2, r3, out, parts):
    for back, r in enumerate((own, r1, r2, r3)):
        parts[lax.rem(seg[0] + SEG - back, SEG)] = r[...].astype(F32)
    total = ((parts[0] + parts[1]) + (parts[2] + parts[3])).astype(BF)
    for i in range(PLANE):
        out[i] = total


def seg_sum(seg, own, r1, r2, r3):
    whole = pl.BlockSpec(memory_space=pltpu.VMEM)
    return pl.pallas_call(
        seg_kernel,
        in_specs=[pl.BlockSpec(memory_space=pltpu.SMEM)] + [whole] * 4,
        out_specs=whole,
        out_shape=jax.ShapeDtypeStruct((PLANE, PIECE, DM), BF),
        scratch_shapes=[pltpu.VMEM((SEG, PIECE, DM), F32)],
        compiler_params=pltpu.CompilerParams(vmem_limit_bytes=16 << 20),
        cost_estimate=pl.CostEstimate(flops=1 << 17, bytes_accessed=1 << 20, transcendentals=0),
        name="seg_sum",
    )(seg, own, r1, r2, r3)


def half_kernel(own, core, half, *rest):
    out, wide, sem = rest[-3:]
    place = core[0] if own else 1 - core[0]
    copies = []
    for i in range(4):
        at = pl.ds(i * PLANE // 4, PLANE // 4)
        wide[at] = half[at].astype(F32)
        copies.append(pltpu.make_async_copy(wide.at[at], out.at[at, place], sem.at[i]))
        copies[-1].start()
    for copy in copies:
        copy.wait()


def whole_grad(core, half, before=None):
    own = before is None
    far = pl.BlockSpec(memory_space=pl.ANY)
    return pl.pallas_call(
        functools.partial(half_kernel, own),
        in_specs=[pl.BlockSpec(memory_space=pltpu.SMEM), pl.BlockSpec(memory_space=pltpu.VMEM)]
        + ([] if own else [far]),
        out_specs=far,
        out_shape=jax.ShapeDtypeStruct((PLANE, CORES, PIECE, DM), F32),
        scratch_shapes=[pltpu.VMEM((PLANE, PIECE, DM), F32), pltpu.SemaphoreType.DMA((4,))],
        input_output_aliases={} if own else {2: 0},
        compiler_params=pltpu.CompilerParams(vmem_limit_bytes=16 << 20),
        cost_estimate=pl.CostEstimate(flops=1 << 18, bytes_accessed=3 << 20, transcendentals=0),
        name="own_half" if own else "far_half",
    )(core, half, *([] if own else [before]))


def owner_kernel(core, asked, keep, got, out):
    near = asked[:, core[0]].reshape(SLOTS // 2, 128)
    far = asked[:, 1 - core[0]].reshape(SLOTS // 2, 128)
    out[...] = dot_tn(owner_pick(near), keep[...]) + dot_tn(owner_pick(far), got[...])


def owner_sum(core, asked, keep, got):
    whole = pl.BlockSpec(memory_space=pltpu.VMEM)
    return pl.pallas_call(
        owner_kernel,
        in_specs=[pl.BlockSpec(memory_space=pltpu.SMEM)] + [whole] * 3,
        out_specs=whole,
        out_shape=jax.ShapeDtypeStruct((N, DM), F32),
        compiler_params=pltpu.CompilerParams(vmem_limit_bytes=16 << 20),
        cost_estimate=pl.CostEstimate(
            flops=2 * N * DM * SLOTS, bytes_accessed=1 << 20, transcendentals=0
        ),
        name="owner_sum",
    )(core, asked.reshape(PLANE, CORES, CAP, 128), keep, got)


def exchange(rows, axes, count):
    blocks = rows.reshape(count, -1, rows.shape[-1])
    return lax.all_to_all(blocks, axes, split_axis=0, concat_axis=0, tiled=True).reshape(rows.shape)


def plane(x):
    return lax.all_to_all(x, FLAT, split_axis=0, concat_axis=0, tiled=True)


def on_device(
    memory_base,
    messages,
    touched,
    gru_input,
    gru_state,
    attn_weights,
    frequency,
    request_rows,
    event_slots,
    delays,
    upstream,
):
    seg = lax.axis_index("y").reshape(1)
    core = lax.axis_index("core").reshape(1)
    written, ids = gru(
        touched, request_rows.reshape(1, SLOTS), memory_base, messages[0], gru_input, gru_state
    )
    r1 = lax.ppermute(written, "y", [(0, 1), (1, 2), (2, 3)])
    r2 = lax.ppermute(written, "y", [(0, 2), (1, 3)])
    r3 = lax.ppermute(written, "y", [(0, 3)])
    written, late, seg, core = lax.optimization_barrier((written, delays[0].T, seg, core))
    chosen_t = event_slots.transpose(2, 0, 1)
    code_t, time_kv, chosen = time_parts(late, frequency.reshape(1, DM), attn_weights, chosen_t)
    written, ids, code_t, time_kv, chosen = lax.optimization_barrier(
        (written, ids, code_t, time_kv, chosen)
    )
    asked = exchange(ids, NODE, OWNERS)
    memory, rows = start_rows(seg, memory_base, written, r1, r2, r3, asked)
    slots = exchange(rows, NODE, OWNERS)
    up = upstream[0]
    embedded, d_slots, mine, other = attend(
        core, slots, chosen, chosen_t, time_kv, code_t, up, attn_weights
    )
    swap = [(0, 1), (1, 0)]
    partner = lax.ppermute(other, "core", swap)
    parts = plane(pair_sum(mine, partner, d_slots))
    part, keep, give = plane_sum(core, parts)
    got = lax.ppermute(give, "core", swap)
    r2, r1, r3 = (
        lax.ppermute(part, "y", [(i, (i + s) % SEG) for i in range(SEG)]) for s in (2, 1, 3)
    )
    memory_grad = owner_sum(core, asked, keep, got)
    r2, memory_grad = lax.optimization_barrier((r2, memory_grad))
    half = plane(seg_sum(seg, part, r1, r2, r3))
    far = lax.ppermute(half, "core", swap)
    weight_grad = whole_grad(core, far, whole_grad(core, half))
    return embedded[None], memory[None], memory_grad[None], weight_grad.reshape(4, DM, DM)


def solution(mesh):
    fine = Mesh(mesh.devices.reshape(SEG, X, Z, CORES), ("y", "x", "z", "core"))
    both = P("y", NODE, None)
    in_specs = (P(NODE, None), both, P("y", NODE), P(), P(), P(), P(), both, both, both, both)
    out_specs = (both, both, both, P())
    return jax.shard_map(
        on_device, mesh=fine, in_specs=in_specs, out_specs=out_specs, check_vma=False
    )
```

```python
import functools
import math

import jax
import jax.numpy as jnp
from jax import lax
from jax.experimental import pallas as pl
from jax.experimental.pallas import tpu as pltpu
from jax.sharding import Mesh
from jax.sharding import PartitionSpec as P

SEG, X, Z, CORES = 4, 4, 4, 2
OWNERS = X * Z * CORES
PLANE = X * Z
DM = 512
HEADS = 2
HEAD = DM // HEADS
K = 8
E = 256
N = 256
CAP = 8
SLOTS = 256
PIECE = 64
TILE = 128
TILES = E // TILE
ROWS = K * TILE
STEP = 32
ABSENT = 2.0
NODE = ("x", "z", "core")
FLAT = ("x", "z")
BF = jnp.bfloat16
F32 = jnp.float32

COS = (
    0.9999999698385398,
    -19.739198571306687,
    64.93882672218028,
    -85.44499716023202,
    60.126952745697146,
    -25.820504473745327,
    6.330480832160802,
)


def dot(a, b):
    return jnp.dot(a, b, preferred_element_type=F32)


def dot_tn(a, b):
    return lax.dot_general(a, b, (((0,), (0,)), ((), ())), preferred_element_type=F32)


def dot_nt(a, b):
    return lax.dot_general(a, b, (((1,), (1,)), ((), ())), preferred_element_type=F32)


def iota(shape, axis):
    return lax.broadcasted_iota(jnp.int32, shape, axis)


def column(row):
    n = row.shape[1]
    square = jnp.where(iota((n, n), 0) == iota((n, n), 1), row.astype(F32), 0.0)
    return jnp.sum(square, axis=1, keepdims=True)


def gru_kernel(
    touched, ids, state, message, w_input, w_state, out, spread, st, ms, wi, ws, sem
):
    near, rest = pl.ds(0, DM // 2), pl.ds(DM // 2, DM // 2)
    moves = (
        (state, st),
        (w_state.at[near], ws.at[near]),
        (w_state.at[rest], ws.at[rest]),
        (message, ms),
        (w_input.at[near], wi.at[near]),
        (w_input.at[rest], wi.at[rest]),
    )
    copies = [pltpu.make_async_copy(a, b, sem.at[i]) for i, (a, b) in enumerate(moves)]
    for copy in copies:
        copy.start()
    keep = column(touched[...]) > 0.5
    spread[...] = jnp.broadcast_to(column(ids[...]), (SLOTS, 128)).astype(jnp.int32)

    def product(rows, w, waits):
        waits[0].wait()
        waits[1].wait()
        low = [dot(rows[:, : DM // 2], w[: DM // 2, i * DM : (i + 1) * DM]) for i in range(3)]
        waits[2].wait()
        return [
            low[i] + dot(rows[:, DM // 2 :], w[DM // 2 :, i * DM : (i + 1) * DM]) for i in range(3)
        ]

    from_state = product(st, ws, copies[:3])
    from_msg = product(ms, wi, copies[3:])
    s = st[...]
    update = jax.nn.sigmoid(from_msg[0] + from_state[0])
    reset = jax.nn.sigmoid(from_msg[1] + from_state[1])
    candidate = jnp.tanh(from_msg[2] + reset * from_state[2])
    fresh = (1.0 - update) * candidate + update * s.astype(F32)
    out[...] = jnp.where(keep, fresh, ABSENT).astype(BF)


def gru(touched, ids, state, message, w_input, w_state):
    whole = pl.BlockSpec(memory_space=pltpu.VMEM)
    far = pl.BlockSpec(memory_space=pl.ANY)
    return pl.pallas_call(
        gru_kernel,
        in_specs=[whole] * 2 + [far] * 4,
        out_specs=[whole] * 2,
        out_shape=[
            jax.ShapeDtypeStruct((N, DM), BF),
            jax.ShapeDtypeStruct((SLOTS, 128), jnp.int32),
        ],
        scratch_shapes=[
            pltpu.VMEM((N, DM), BF),
            pltpu.VMEM((N, DM), BF),
            pltpu.VMEM((DM, 3 * DM), BF),
            pltpu.VMEM((DM, 3 * DM), BF),
            pltpu.SemaphoreType.DMA((6,)),
        ],
        compiler_params=pltpu.CompilerParams(vmem_limit_bytes=56 << 20),
        cost_estimate=pl.CostEstimate(
            flops=4 * N * DM * 3 * DM, bytes_accessed=4 << 20, transcendentals=3 * N * DM
        ),
        name="gru",
    )(touched, ids, state, message, w_input, w_state)


def time_kernel(delays, frequency, w, chosen, times, picked, held, sem):
    lane = iota((E, 128), 1)
    columns = jnp.zeros((E, 128), F32)
    for j in range(K + 1):
        columns = jnp.where(lane == j, column(chosen[j]), columns)
    picked[...] = columns.astype(jnp.int32)
    turns = frequency[...] * (1.0 / (2.0 * math.pi))
    high = jnp.round(turns * 16384.0) * (1.0 / 16384.0)
    low = turns - high
    copies = []
    for tile in range(TILES):
        for k in range(K):
            delay = column(delays[k : k + 1, tile * TILE : (tile + 1) * TILE])
            coarse = delay * high
            part = (coarse - jnp.round(coarse)) + delay * low
            u = part * part
            wave = jnp.full_like(u, COS[-1])
            for c in COS[-2::-1]:
                wave = wave * u + c
            at = slice(k * TILE, (k + 1) * TILE)
            held[tile, ROWS:, at] = wave.T.astype(BF)
            wave = wave.astype(BF)
            held[tile, at, :DM] = dot(wave, w[1]).astype(BF)
            held[tile, at, DM:] = dot(wave, w[2]).astype(BF)
            moves = []
            if k % 2 == 1:
                moves.append(pl.ds((k - 1) * TILE, 2 * TILE))
            if k == K - 1:
                moves.append(pl.ds(ROWS, DM))
            for rows in moves:
                n = len(copies)
                copy = pltpu.make_async_copy(held.at[tile, rows], times.at[tile, rows], sem.at[n])
                copy.start()
                copies.append(copy)
    for copy in copies:
        copy.wait()


def time_parts(delays, frequency, weights, chosen):
    whole = pl.BlockSpec(memory_space=pltpu.VMEM)
    far = pl.BlockSpec(memory_space=pl.ANY)
    return pl.pallas_call(
        time_kernel,
        in_specs=[whole] * 4,
        out_specs=[far, whole],
        out_shape=[
            jax.ShapeDtypeStruct((TILES, ROWS + DM, ROWS), BF),
            jax.ShapeDtypeStruct((E, 128), jnp.int32),
        ],
        scratch_shapes=[
            pltpu.VMEM((TILES, ROWS + DM, ROWS), BF),
            pltpu.SemaphoreType.DMA((TILES * (K // 2 + 1),)),
        ],
        compiler_params=pltpu.CompilerParams(vmem_limit_bytes=56 << 20),
        cost_estimate=pl.CostEstimate(
            flops=4 * K * E * DM * DM, bytes_accessed=8 << 20, transcendentals=K * E * DM
        ),
        name="time_parts",
    )(delays, frequency, weights, chosen)


def owner_pick(asked):
    ids = jnp.concatenate([asked] * (N // 128), axis=1)
    return (ids == iota(ids.shape, 1)).astype(F32).astype(BF)


def start_kernel(seg, state, written, r1, r2, r3, asked, memory, rows):
    start = state[...]
    for back, r in ((3, r3), (2, r2), (1, r1)):
        row = r[...]
        start = jnp.where((row.astype(F32) < 1.5) & (seg[0] >= back), row, start)
    own = written[...]
    memory[...] = jnp.where(own.astype(F32) < 1.5, own, start)
    rows[...] = dot(owner_pick(asked[...]), start).astype(BF)


def start_rows(seg, state, written, r1, r2, r3, asked):
    whole = pl.BlockSpec(memory_space=pltpu.VMEM)
    return pl.pallas_call(
        start_kernel,
        in_specs=[pl.BlockSpec(memory_space=pltpu.SMEM)] + [whole] * 6,
        out_specs=[whole] * 2,
        out_shape=[
            jax.ShapeDtypeStruct((N, DM), BF),
            jax.ShapeDtypeStruct((SLOTS, DM), BF),
        ],
        compiler_params=pltpu.CompilerParams(vmem_limit_bytes=16 << 20),
        cost_estimate=pl.CostEstimate(
            flops=2 * N * DM * SLOTS, bytes_accessed=2 << 20, transcendentals=0
        ),
        name="start_rows",
    )(seg, state, written, r1, r2, r3, asked)


def attend_kernel(
    core, slots, chosen, chosen_t, times, up, wq,
    embedded, d_slots, mine, other,
    tkv, tt, sem, skv, d_att, qf, src, both, dkv, att, dq, sums,
):
    moves = [(times.at[i, pl.ds(0, ROWS)], tkv.at[i]) for i in range(TILES)]
    moves += [(times.at[i, pl.ds(ROWS, DM)], tt.at[i]) for i in range(TILES)]
    copies = [pltpu.make_async_copy(a, b, sem.at[i]) for i, (a, b) in enumerate(moves)]
    for i in (0, 2, 1, 3):
        copies[i].start()
    rows = slots[...]
    pick = (chosen[:, 0:1] == iota((E, SLOTS), 1)).astype(F32).astype(BF)
    src[...] = dot(pick, rows)
    skv[:, :DM] = dot(rows, wq[1]).astype(BF)
    skv[:, DM:] = dot(rows, wq[2]).astype(BF)
    qf[...] = dot(pick, dot(rows, wq[0]).astype(BF))
    d_att[...] = dot_nt(up[...], wq[3])

    lane = iota((STEP, 128), 1)
    first = lane < K
    second = (lane >= K) & (lane < 2 * K)
    scale = 1.0 / math.sqrt(HEAD)

    def per_head(x):
        a = jnp.sum(jnp.where(first, x, 0.0), axis=1, keepdims=True)
        b = jnp.sum(jnp.where(second, x, 0.0), axis=1, keepdims=True)
        return jnp.where(first, a, b)

    def gather(i):
        ids = chosen[i * TILE : (i + 1) * TILE, :]
        slot = iota((TILE, SLOTS), 1)
        pick = jnp.concatenate(
            [(ids[:, 1 + k : 2 + k] == slot).astype(F32) for k in range(K)], axis=0
        ).astype(BF)
        both[i] = dot(pick, skv[...])

    def step(i, j):
        at = slice(i * TILE + j * STEP, i * TILE + (j + 1) * STEP)
        scores = jnp.zeros((STEP, 128), F32)
        d_probs = jnp.zeros((STEP, 128), F32)
        for h in range(HEADS):
            part = slice(h * HEAD, (h + 1) * HEAD)
            part_v = slice(DM + h * HEAD, DM + (h + 1) * HEAD)
            query = qf[at, part]
            d_out = d_att[at, part]
            for k in range(K):
                row = slice(k * TILE + j * STEP, k * TILE + (j + 1) * STEP)
                key = both[i, row, part] + tkv[i, row, part].astype(F32)
                value = both[i, row, part_v] + tkv[i, row, part_v].astype(F32)
                both[i, row, part] = key
                both[i, row, part_v] = value
                here = lane == h * K + k
                scores = jnp.where(here, jnp.sum(query * key, axis=1, keepdims=True), scores)
                d_probs = jnp.where(here, jnp.sum(d_out * value, axis=1, keepdims=True), d_probs)
        powered = jnp.exp(scores * scale)
        probs = powered / per_head(powered)
        d_scores = probs * (d_probs - per_head(probs * d_probs)) * scale
        for h in range(HEADS):
            part = slice(h * HEAD, (h + 1) * HEAD)
            part_v = slice(DM + h * HEAD, DM + (h + 1) * HEAD)
            query = qf[at, part]
            d_out = d_att[at, part]
            attended = jnp.zeros((STEP, HEAD), F32)
            d_query = jnp.zeros((STEP, HEAD), F32)
            for k in range(K):
                row = slice(k * TILE + j * STEP, k * TILE + (j + 1) * STEP)
                c = h * K + k
                p = jnp.broadcast_to(probs[:, c : c + 1], (STEP, HEAD))
                d = jnp.broadcast_to(d_scores[:, c : c + 1], (STEP, HEAD))
                attended += p * both[i, row, part_v]
                d_query += d * both[i, row, part]
                dkv[i, row, part] = (d * query).astype(BF)
                dkv[i, row, part_v] = (p * d_out).astype(BF)
            att[at, part] = attended.astype(BF)
            dq[at, part] = d_query.astype(BF)

    for i in range(TILES):
        gather(i)
    sub = iota((SLOTS, TILE), 0)
    s_kv = dot_t = None
    for i in range(TILES):
        copies[i].wait()
        for j in range(TILE // STEP):
            step(i, j)
        copies[TILES + i].wait()
        spread = jnp.concatenate(
            [
                (sub == chosen_t[1 + k, :, i * TILE : (i + 1) * TILE]).astype(F32)
                for k in range(K)
            ],
            axis=1,
        ).astype(BF)
        one, two = dot(spread, dkv[i]), dot(tt[i], dkv[i])
        s_kv = one if i == 0 else s_kv + one
        dot_t = two if i == 0 else dot_t + two
    s_kv = s_kv.astype(BF)
    pick_t = (iota((SLOTS, E), 0) == chosen_t[0]).astype(F32).astype(BF)
    s_q = dot(pick_t, dq[...]).astype(BF)

    def store(i, value):
        sums[i * 4 : (i + 1) * 4] = value.astype(BF).reshape(4, CORES, PIECE, DM)

    store(0, dot_tn(rows, s_q))
    g_kv = dot_t + dot_tn(rows, s_kv)
    store(1, g_kv[:, :DM])
    store(2, g_kv[:, DM:])
    store(3, dot_tn(att[...], up[...]))
    mine[...] = sums[:, core[0]]
    other[...] = sums[:, 1 - core[0]]
    embedded[...] = (dot(att[...], wq[3]) + src[...]).astype(BF)
    grads = dot(pick_t, up[...]) + dot_nt(s_q, wq[0])
    grads += dot_nt(s_kv[:, :DM], wq[1]) + dot_nt(s_kv[:, DM:], wq[2])
    d_slots[...] = grads.astype(BF)


def attend(core, slots, chosen, chosen_t, times, up, weights):
    whole = pl.BlockSpec(memory_space=pltpu.VMEM)
    far = pl.BlockSpec(memory_space=pl.ANY)
    return pl.pallas_call(
        attend_kernel,
        in_specs=[pl.BlockSpec(memory_space=pltpu.SMEM)] + [whole] * 3 + [far] + [whole] * 2,
        out_specs=[whole] * 4,
        out_shape=[
            jax.ShapeDtypeStruct((E, DM), BF),
            jax.ShapeDtypeStruct((SLOTS, DM), BF),
            jax.ShapeDtypeStruct((PLANE, PIECE, DM), BF),
            jax.ShapeDtypeStruct((PLANE, PIECE, DM), BF),
        ],
        scratch_shapes=[
            pltpu.VMEM((TILES, ROWS, 2 * DM), BF),
            pltpu.VMEM((TILES, DM, ROWS), BF),
            pltpu.SemaphoreType.DMA((2 * TILES,)),
            pltpu.VMEM((SLOTS, 2 * DM), BF),
            pltpu.VMEM((E, DM), F32),
            pltpu.VMEM((E, DM), F32),
            pltpu.VMEM((E, DM), F32),
            pltpu.VMEM((TILES, ROWS, 2 * DM), F32),
            pltpu.VMEM((TILES, ROWS, 2 * DM), BF),
            pltpu.VMEM((E, DM), BF),
            pltpu.VMEM((E, DM), BF),
            pltpu.VMEM((PLANE, CORES, PIECE, DM), BF),
        ],
        compiler_params=pltpu.CompilerParams(vmem_limit_bytes=49 << 20),
        cost_estimate=pl.CostEstimate(
            flops=6 << 30, bytes_accessed=14 << 20, transcendentals=E * 128
        ),
        name="attend",
    )(core, slots, chosen, chosen_t, times, up, weights)


def pair_kernel(a, b, d_slots, out):
    out[:, :PIECE] = (a[...].astype(F32) + b[...].astype(F32)).astype(BF)
    out[:, PIECE:] = d_slots[...]


def pair_sum(a, b, d_slots):
    spec = pl.BlockSpec((4, PIECE, DM), lambda i: (i, 0, 0))
    return pl.pallas_call(
        pair_kernel,
        grid=(PLANE // 4,),
        in_specs=[spec, spec, pl.BlockSpec((4, 2 * CAP, DM), lambda i: (i, 0, 0))],
        out_specs=pl.BlockSpec((4, PIECE + 2 * CAP, DM), lambda i: (i, 0, 0)),
        out_shape=jax.ShapeDtypeStruct((PLANE, PIECE + 2 * CAP, DM), BF),
        compiler_params=pltpu.CompilerParams(vmem_limit_bytes=16 << 20),
        cost_estimate=pl.CostEstimate(flops=1 << 19, bytes_accessed=3 << 20, transcendentals=0),
        name="pair_sum",
    )(a, b, d_slots.reshape(PLANE, 2 * CAP, DM))


def plane_kernel(core, a, part, keep, give):
    total = a[0, :PIECE].astype(F32)
    for i in range(1, PLANE):
        total += a[i, :PIECE].astype(F32)
    part[...] = total.astype(BF)
    grads = a[:, PIECE:].astype(F32)
    low, high = grads[:, :CAP].reshape(SLOTS // 2, DM), grads[:, CAP:].reshape(SLOTS // 2, DM)
    first = core[0] == 0
    keep[...] = jnp.where(first, low, high).astype(BF)
    give[...] = jnp.where(first, high, low).astype(BF)


def plane_sum(core, a):
    whole = pl.BlockSpec(memory_space=pltpu.VMEM)
    half = jax.ShapeDtypeStruct((SLOTS // 2, DM), BF)
    return pl.pallas_call(
        plane_kernel,
        in_specs=[pl.BlockSpec(memory_space=pltpu.SMEM), whole],
        out_specs=[whole] * 3,
        out_shape=[jax.ShapeDtypeStruct((PIECE, DM), BF), half, half],
        compiler_params=pltpu.CompilerParams(vmem_limit_bytes=16 << 20),
        cost_estimate=pl.CostEstimate(flops=1 << 19, bytes_accessed=2 << 20, transcendentals=0),
        name="plane_sum",
    )(core, a)


def seg_kernel(seg, own, r1, r2, r3, out, parts):
    for back, r in enumerate((own, r1, r2, r3)):
        parts[lax.rem(seg[0] + SEG - back, SEG)] = r[...].astype(F32)
    total = ((parts[0] + parts[1]) + (parts[2] + parts[3])).astype(BF)
    for i in range(PLANE):
        out[i] = total


def seg_sum(seg, own, r1, r2, r3):
    whole = pl.BlockSpec(memory_space=pltpu.VMEM)
    return pl.pallas_call(
        seg_kernel,
        in_specs=[pl.BlockSpec(memory_space=pltpu.SMEM)] + [whole] * 4,
        out_specs=whole,
        out_shape=jax.ShapeDtypeStruct((PLANE, PIECE, DM), BF),
        scratch_shapes=[pltpu.VMEM((SEG, PIECE, DM), F32)],
        compiler_params=pltpu.CompilerParams(vmem_limit_bytes=16 << 20),
        cost_estimate=pl.CostEstimate(flops=1 << 17, bytes_accessed=1 << 20, transcendentals=0),
        name="seg_sum",
    )(seg, own, r1, r2, r3)


def half_kernel(own, core, half, *rest):
    out, wide, sem = rest[-3:]
    place = core[0] if own else 1 - core[0]
    copies = []
    for i in range(4):
        at = pl.ds(i * PLANE // 4, PLANE // 4)
        wide[at] = half[at].astype(F32)
        copies.append(pltpu.make_async_copy(wide.at[at], out.at[at, place], sem.at[i]))
        copies[-1].start()
    for copy in copies:
        copy.wait()


def whole_grad(core, half, before=None):
    own = before is None
    far = pl.BlockSpec(memory_space=pl.ANY)
    return pl.pallas_call(
        functools.partial(half_kernel, own),
        in_specs=[pl.BlockSpec(memory_space=pltpu.SMEM), pl.BlockSpec(memory_space=pltpu.VMEM)]
        + ([] if own else [far]),
        out_specs=far,
        out_shape=jax.ShapeDtypeStruct((PLANE, CORES, PIECE, DM), F32),
        scratch_shapes=[pltpu.VMEM((PLANE, PIECE, DM), F32), pltpu.SemaphoreType.DMA((4,))],
        input_output_aliases={} if own else {2: 0},
        compiler_params=pltpu.CompilerParams(vmem_limit_bytes=16 << 20),
        cost_estimate=pl.CostEstimate(flops=1 << 18, bytes_accessed=3 << 20, transcendentals=0),
        name="own_half" if own else "far_half",
    )(core, half, *([] if own else [before]))


def owner_kernel(core, asked, keep, got, out):
    near = asked[:, core[0]].reshape(SLOTS // 2, 128)
    far = asked[:, 1 - core[0]].reshape(SLOTS // 2, 128)
    out[...] = dot_tn(owner_pick(near), keep[...]) + dot_tn(owner_pick(far), got[...])


def owner_sum(core, asked, keep, got):
    whole = pl.BlockSpec(memory_space=pltpu.VMEM)
    return pl.pallas_call(
        owner_kernel,
        in_specs=[pl.BlockSpec(memory_space=pltpu.SMEM)] + [whole] * 3,
        out_specs=whole,
        out_shape=jax.ShapeDtypeStruct((N, DM), F32),
        compiler_params=pltpu.CompilerParams(vmem_limit_bytes=16 << 20),
        cost_estimate=pl.CostEstimate(
            flops=2 * N * DM * SLOTS, bytes_accessed=1 << 20, transcendentals=0
        ),
        name="owner_sum",
    )(core, asked.reshape(PLANE, CORES, CAP, 128), keep, got)


def exchange(rows, axes, count):
    blocks = rows.reshape(count, -1, rows.shape[-1])
    return lax.all_to_all(blocks, axes, split_axis=0, concat_axis=0, tiled=True).reshape(rows.shape)


def plane(x):
    return lax.all_to_all(x, FLAT, split_axis=0, concat_axis=0, tiled=True)


def on_device(
    memory_base,
    messages,
    touched,
    gru_input,
    gru_state,
    attn_weights,
    frequency,
    request_rows,
    event_slots,
    delays,
    upstream,
):
    seg = lax.axis_index("y").reshape(1)
    core = lax.axis_index("core").reshape(1)
    written, ids = gru(
        touched, request_rows.reshape(1, SLOTS), memory_base, messages[0], gru_input, gru_state
    )
    r1 = lax.ppermute(written, "y", [(0, 1), (1, 2), (2, 3)])
    r2 = lax.ppermute(written, "y", [(0, 2), (1, 3)])
    r3 = lax.ppermute(written, "y", [(0, 3)])
    asked = exchange(ids, NODE, OWNERS)
    written, late, seg, core = lax.optimization_barrier((written, delays[0].T, seg, core))
    chosen_t = event_slots.transpose(2, 0, 1)
    times, chosen = time_parts(late, frequency.reshape(1, DM), attn_weights, chosen_t)
    written, times, chosen = lax.optimization_barrier((written, times, chosen))
    memory, rows = start_rows(seg, memory_base, written, r1, r2, r3, asked)
    slots = exchange(rows, NODE, OWNERS)
    up = upstream[0]
    embedded, d_slots, mine, other = attend(
        core, slots, chosen, chosen_t, times, up, attn_weights
    )
    swap = [(0, 1), (1, 0)]
    partner = lax.ppermute(other, "core", swap)
    parts = plane(pair_sum(mine, partner, d_slots))
    part, keep, give = plane_sum(core, parts)
    got = lax.ppermute(give, "core", swap)
    r2, r1, r3 = (
        lax.ppermute(part, "y", [(i, (i + s) % SEG) for i in range(SEG)]) for s in (2, 1, 3)
    )
    memory_grad = owner_sum(core, asked, keep, got)
    r2, memory_grad = lax.optimization_barrier((r2, memory_grad))
    half = plane(seg_sum(seg, part, r1, r2, r3))
    far = lax.ppermute(half, "core", swap)
    weight_grad = whole_grad(core, far, whole_grad(core, half))
    return embedded[None], memory[None], memory_grad[None], weight_grad.reshape(4, DM, DM)


def solution(mesh):
    fine = Mesh(mesh.devices.reshape(SEG, X, Z, CORES), ("y", "x", "z", "core"))
    both = P("y", NODE, None)
    in_specs = (P(NODE, None), both, P("y", NODE), P(), P(), P(), P(), both, both, both, both)
    out_specs = (both, both, both, P())
    return jax.shard_map(
        on_device, mesh=fine, in_specs=in_specs, out_specs=out_specs, check_vma=False
    )
```

```python
import functools
import math

import jax
import jax.numpy as jnp
from jax import lax
from jax.experimental import pallas as pl
from jax.experimental.pallas import tpu as pltpu
from jax.sharding import Mesh
from jax.sharding import PartitionSpec as P

SEG, X, Z, CORES = 4, 4, 4, 2
OWNERS = X * Z * CORES
PLANE = X * Z
DM = 512
HEADS = 2
HEAD = DM // HEADS
K = 8
E = 256
N = 256
CAP = 8
SLOTS = 256
PIECE = 64
TILE = 128
TILES = E // TILE
ROWS = K * TILE
STEP = 32
ABSENT = 2.0
NODE = ("x", "z", "core")
FLAT = ("x", "z")
BF = jnp.bfloat16
F32 = jnp.float32

COS = (
    0.9999999698385398,
    -19.739198571306687,
    64.93882672218028,
    -85.44499716023202,
    60.126952745697146,
    -25.820504473745327,
    6.330480832160802,
)


def dot(a, b):
    return jnp.dot(a, b, preferred_element_type=F32)


def dot_tn(a, b):
    return lax.dot_general(a, b, (((0,), (0,)), ((), ())), preferred_element_type=F32)


def dot_nt(a, b):
    return lax.dot_general(a, b, (((1,), (1,)), ((), ())), preferred_element_type=F32)


def iota(shape, axis):
    return lax.broadcasted_iota(jnp.int32, shape, axis)


def column(row):
    n = row.shape[1]
    square = jnp.where(iota((n, n), 0) == iota((n, n), 1), row.astype(F32), 0.0)
    return jnp.sum(square, axis=1, keepdims=True)


def gru_kernel(touched, state, message, w_input, w_state, out, st, ms, wi, ws, sem):
    moves = ((state, st), (w_state, ws), (message, ms), (w_input, wi))
    copies = [pltpu.make_async_copy(a, b, sem.at[i]) for i, (a, b) in enumerate(moves)]
    for copy in copies:
        copy.start()
    keep = column(touched[...]) > 0.5
    copies[0].wait()
    copies[1].wait()
    s = st[...]
    from_state = [dot(s, ws[:, i * DM : (i + 1) * DM]) for i in range(3)]
    copies[2].wait()
    copies[3].wait()
    m = ms[...]
    update = jax.nn.sigmoid(dot(m, wi[:, :DM]) + from_state[0])
    reset = jax.nn.sigmoid(dot(m, wi[:, DM : 2 * DM]) + from_state[1])
    candidate = jnp.tanh(dot(m, wi[:, 2 * DM :]) + reset * from_state[2])
    fresh = (1.0 - update) * candidate + update * s.astype(F32)
    out[...] = jnp.where(keep, fresh, ABSENT).astype(BF)


def gru(touched, state, message, w_input, w_state):
    whole = pl.BlockSpec(memory_space=pltpu.VMEM)
    far = pl.BlockSpec(memory_space=pl.ANY)
    return pl.pallas_call(
        gru_kernel,
        in_specs=[whole] + [far] * 4,
        out_specs=whole,
        out_shape=jax.ShapeDtypeStruct((N, DM), BF),
        scratch_shapes=[
            pltpu.VMEM((N, DM), BF),
            pltpu.VMEM((N, DM), BF),
            pltpu.VMEM((DM, 3 * DM), BF),
            pltpu.VMEM((DM, 3 * DM), BF),
            pltpu.SemaphoreType.DMA((4,)),
        ],
        compiler_params=pltpu.CompilerParams(vmem_limit_bytes=56 << 20),
        cost_estimate=pl.CostEstimate(
            flops=4 * N * DM * 3 * DM, bytes_accessed=4 << 20, transcendentals=3 * N * DM
        ),
        name="gru",
    )(touched, state, message, w_input, w_state)


def time_kernel(core, ids, ids_far, delays, frequency, w, chosen, code_t, time_kv, picked, wanted):
    first = core[0] == 0
    for side, row in ((0, ids), (1, ids_far)):
        blocks = jnp.broadcast_to(column(row[...]), (SLOTS, 128)).reshape(PLANE, CORES, CAP, 128)
        mine = jnp.where(first, blocks[:, 0], blocks[:, 1]).astype(jnp.int32)
        wanted[:, core[0] if side == 0 else 1 - core[0]] = mine
    lane = iota((E, 128), 1)
    columns = jnp.zeros((E, 128), F32)
    for j in range(K + 1):
        columns = jnp.where(lane == j, column(chosen[j]), columns)
    picked[...] = columns.astype(jnp.int32)
    turns = frequency[...] * (1.0 / (2.0 * math.pi))
    high = jnp.round(turns * 16384.0) * (1.0 / 16384.0)
    low = turns - high
    for tile in range(TILES):
        for k in range(K):
            delay = column(delays[k : k + 1, tile * TILE : (tile + 1) * TILE])
            coarse = delay * high
            part = (coarse - jnp.round(coarse)) + delay * low
            u = part * part
            wave = jnp.full_like(u, COS[-1])
            for c in COS[-2::-1]:
                wave = wave * u + c
            at = slice(k * TILE, (k + 1) * TILE)
            code_t[tile, :, at] = wave.T.astype(BF)
            wave = wave.astype(BF)
            time_kv[tile, at, :DM] = dot(wave, w[1]).astype(BF)
            time_kv[tile, at, DM:] = dot(wave, w[2]).astype(BF)


def time_parts(core, ids, ids_far, delays, frequency, weights, chosen):
    whole = pl.BlockSpec(memory_space=pltpu.VMEM)
    return pl.pallas_call(
        time_kernel,
        in_specs=[pl.BlockSpec(memory_space=pltpu.SMEM)] + [whole] * 6,
        out_specs=[whole] * 4,
        out_shape=[
            jax.ShapeDtypeStruct((TILES, DM, ROWS), BF),
            jax.ShapeDtypeStruct((TILES, ROWS, 2 * DM), BF),
            jax.ShapeDtypeStruct((E, 128), jnp.int32),
            jax.ShapeDtypeStruct((PLANE, CORES, CAP, 128), jnp.int32),
        ],
        compiler_params=pltpu.CompilerParams(vmem_limit_bytes=24 << 20),
        cost_estimate=pl.CostEstimate(
            flops=4 * K * E * DM * DM, bytes_accessed=8 << 20, transcendentals=K * E * DM
        ),
        name="time_parts",
    )(core, ids, ids_far, delays, frequency, weights, chosen)


def owner_pick(asked):
    ids = jnp.concatenate([asked] * (N // 128), axis=1)
    return (ids == iota(ids.shape, 1)).astype(F32).astype(BF)


def start_kernel(seg, state, written, r1, r2, r3, asked, memory, rows):
    start = state[...]
    for back, r in ((3, r3), (2, r2), (1, r1)):
        row = r[...]
        start = jnp.where((row.astype(F32) < 1.5) & (seg[0] >= back), row, start)
    own = written[...]
    memory[...] = jnp.where(own.astype(F32) < 1.5, own, start)
    rows[...] = dot(owner_pick(asked[...]), start).astype(BF)


def start_rows(seg, state, written, r1, r2, r3, asked):
    whole = pl.BlockSpec(memory_space=pltpu.VMEM)
    return pl.pallas_call(
        start_kernel,
        in_specs=[pl.BlockSpec(memory_space=pltpu.SMEM)] + [whole] * 6,
        out_specs=[whole] * 2,
        out_shape=[
            jax.ShapeDtypeStruct((N, DM), BF),
            jax.ShapeDtypeStruct((SLOTS, DM), BF),
        ],
        compiler_params=pltpu.CompilerParams(vmem_limit_bytes=16 << 20),
        cost_estimate=pl.CostEstimate(
            flops=2 * N * DM * SLOTS, bytes_accessed=2 << 20, transcendentals=0
        ),
        name="start_rows",
    )(seg, state, written, r1, r2, r3, asked)


def attend_kernel(
    core, slots, chosen, chosen_t, tkv, tt, up, wq,
    mine, other, att, src, pick_t, s_qkv,
    skv, d_att, qf, both, dkv, dq,
):
    rows = slots[...]
    pick = (chosen[:, 0:1] == iota((E, SLOTS), 1)).astype(F32).astype(BF)
    src[...] = dot(pick, rows).astype(BF)
    skv[:, :DM] = dot(rows, wq[1]).astype(BF)
    skv[:, DM:] = dot(rows, wq[2]).astype(BF)
    qf[...] = dot(pick, dot(rows, wq[0]).astype(BF))
    d_att[...] = dot_nt(up[...], wq[3])

    lane = iota((STEP, 128), 1)
    lane_a = lane < K
    lane_b = (lane >= K) & (lane < 2 * K)
    scale = 1.0 / math.sqrt(HEAD)

    def per_head(x):
        a = jnp.sum(jnp.where(lane_a, x, 0.0), axis=1, keepdims=True)
        b = jnp.sum(jnp.where(lane_b, x, 0.0), axis=1, keepdims=True)
        return jnp.where(lane_a, a, b)

    def gather(i):
        ids = chosen[i * TILE : (i + 1) * TILE, :]
        slot = iota((TILE, SLOTS), 1)
        pick = jnp.concatenate(
            [(ids[:, 1 + k : 2 + k] == slot).astype(F32) for k in range(K)], axis=0
        ).astype(BF)
        both[i] = dot(pick, skv[...])

    def step(i, j):
        at = slice(i * TILE + j * STEP, i * TILE + (j + 1) * STEP)
        scores = jnp.zeros((STEP, 128), F32)
        d_probs = jnp.zeros((STEP, 128), F32)
        for h in range(HEADS):
            part = slice(h * HEAD, (h + 1) * HEAD)
            part_v = slice(DM + h * HEAD, DM + (h + 1) * HEAD)
            query = qf[at, part]
            d_out = d_att[at, part]
            for k in range(K):
                row = slice(k * TILE + j * STEP, k * TILE + (j + 1) * STEP)
                key = both[i, row, part] + tkv[i, row, part].astype(F32)
                value = both[i, row, part_v] + tkv[i, row, part_v].astype(F32)
                both[i, row, part] = key
                both[i, row, part_v] = value
                here = lane == h * K + k
                scores = jnp.where(here, jnp.sum(query * key, axis=1, keepdims=True), scores)
                d_probs = jnp.where(here, jnp.sum(d_out * value, axis=1, keepdims=True), d_probs)
        powered = jnp.exp(scores * scale)
        probs = powered / per_head(powered)
        d_scores = probs * (d_probs - per_head(probs * d_probs)) * scale
        for h in range(HEADS):
            part = slice(h * HEAD, (h + 1) * HEAD)
            part_v = slice(DM + h * HEAD, DM + (h + 1) * HEAD)
            query = qf[at, part]
            d_out = d_att[at, part]
            attended = jnp.zeros((STEP, HEAD), F32)
            d_query = jnp.zeros((STEP, HEAD), F32)
            for k in range(K):
                row = slice(k * TILE + j * STEP, k * TILE + (j + 1) * STEP)
                c = h * K + k
                p = jnp.broadcast_to(probs[:, c : c + 1], (STEP, HEAD))
                d = jnp.broadcast_to(d_scores[:, c : c + 1], (STEP, HEAD))
                attended += p * both[i, row, part_v]
                d_query += d * both[i, row, part]
                dkv[i, row, part] = (d * query).astype(BF)
                dkv[i, row, part_v] = (p * d_out).astype(BF)
            att[at, part] = attended.astype(BF)
            dq[at, part] = d_query.astype(BF)

    for i in range(TILES):
        gather(i)
    sub = iota((SLOTS, TILE), 0)
    s_kv = dot_t = None
    for i in range(TILES):
        for j in range(TILE // STEP):
            step(i, j)
        spread = jnp.concatenate(
            [
                (sub == chosen_t[1 + k, :, i * TILE : (i + 1) * TILE]).astype(F32)
                for k in range(K)
            ],
            axis=1,
        ).astype(BF)
        one, two = dot(spread, dkv[i]), dot(tt[i], dkv[i])
        s_kv = one if i == 0 else s_kv + one
        dot_t = two if i == 0 else dot_t + two
    s_kv = s_kv.astype(BF)
    pick_t[...] = (iota((SLOTS, E), 0) == chosen_t[0]).astype(F32).astype(BF)
    s_q = dot(pick_t[...], dq[...]).astype(BF)
    s_qkv[:, :DM] = s_q
    s_qkv[:, DM:] = s_kv
    first = core[0] == 0

    def store(i, value):
        blocks = value.reshape(4, CORES, PIECE, DM)
        at = slice(i * 4, (i + 1) * 4)
        mine[at] = jnp.where(first, blocks[:, 0], blocks[:, 1]).astype(BF)
        other[at] = jnp.where(first, blocks[:, 1], blocks[:, 0]).astype(BF)

    store(0, dot_tn(rows, s_q))
    g_kv = dot_t + dot_tn(rows, s_kv)
    store(1, g_kv[:, :DM])
    store(2, g_kv[:, DM:])
    store(3, dot_tn(att[...], up[...]))


def events_kernel(att, src, pick_t, s_qkv, up, w, embedded, d_slots):
    embedded[...] = (dot(att[...], w[3]) + src[...].astype(F32)).astype(BF)
    grads = dot(pick_t[...], up[...])
    for i in range(3):
        grads += dot_nt(s_qkv[:, i * DM : (i + 1) * DM], w[i])
    d_slots[...] = grads.astype(BF)


def events(att, src, pick_t, s_qkv, up, weights):
    whole = pl.BlockSpec(memory_space=pltpu.VMEM)
    return pl.pallas_call(
        events_kernel,
        in_specs=[whole] * 6,
        out_specs=[whole] * 2,
        out_shape=[jax.ShapeDtypeStruct((E, DM), BF), jax.ShapeDtypeStruct((SLOTS, DM), BF)],
        compiler_params=pltpu.CompilerParams(vmem_limit_bytes=16 << 20),
        cost_estimate=pl.CostEstimate(flops=1 << 29, bytes_accessed=4 << 20, transcendentals=0),
        name="events",
    )(att, src, pick_t, s_qkv, up, weights)


def attend(core, slots, chosen, chosen_t, time_kv, code_t, up, weights):
    whole = pl.BlockSpec(memory_space=pltpu.VMEM)
    return pl.pallas_call(
        attend_kernel,
        in_specs=[pl.BlockSpec(memory_space=pltpu.SMEM)] + [whole] * 7,
        out_specs=[whole] * 6,
        out_shape=[
            jax.ShapeDtypeStruct((PLANE, PIECE, DM), BF),
            jax.ShapeDtypeStruct((PLANE, PIECE, DM), BF),
            jax.ShapeDtypeStruct((E, DM), BF),
            jax.ShapeDtypeStruct((E, DM), BF),
            jax.ShapeDtypeStruct((SLOTS, E), BF),
            jax.ShapeDtypeStruct((SLOTS, 3 * DM), BF),
        ],
        scratch_shapes=[
            pltpu.VMEM((SLOTS, 2 * DM), BF),
            pltpu.VMEM((E, DM), F32),
            pltpu.VMEM((E, DM), F32),
            pltpu.VMEM((TILES, ROWS, 2 * DM), F32),
            pltpu.VMEM((TILES, ROWS, 2 * DM), BF),
            pltpu.VMEM((E, DM), BF),
        ],
        compiler_params=pltpu.CompilerParams(vmem_limit_bytes=40 << 20),
        cost_estimate=pl.CostEstimate(
            flops=6 << 30, bytes_accessed=14 << 20, transcendentals=E * 128
        ),
        name="attend",
    )(core, slots, chosen, chosen_t, time_kv, code_t, up, weights)


def pair_kernel(a, b, d_slots, out):
    out[:, :PIECE] = (a[...].astype(F32) + b[...].astype(F32)).astype(BF)
    out[:, PIECE:] = d_slots[...]


def pair_sum(a, b, d_slots):
    spec = pl.BlockSpec((4, PIECE, DM), lambda i: (i, 0, 0))
    return pl.pallas_call(
        pair_kernel,
        grid=(PLANE // 4,),
        in_specs=[spec, spec, pl.BlockSpec((4, 2 * CAP, DM), lambda i: (i, 0, 0))],
        out_specs=pl.BlockSpec((4, PIECE + 2 * CAP, DM), lambda i: (i, 0, 0)),
        out_shape=jax.ShapeDtypeStruct((PLANE, PIECE + 2 * CAP, DM), BF),
        compiler_params=pltpu.CompilerParams(vmem_limit_bytes=16 << 20),
        cost_estimate=pl.CostEstimate(flops=1 << 19, bytes_accessed=3 << 20, transcendentals=0),
        name="pair_sum",
    )(a, b, d_slots.reshape(PLANE, 2 * CAP, DM))


def plane_kernel(core, a, part, keep, give):
    total = a[0, :PIECE].astype(F32)
    for i in range(1, PLANE):
        total += a[i, :PIECE].astype(F32)
    part[...] = total.astype(BF)
    grads = a[:, PIECE:].astype(F32)
    low, high = grads[:, :CAP].reshape(SLOTS // 2, DM), grads[:, CAP:].reshape(SLOTS // 2, DM)
    first = core[0] == 0
    keep[...] = jnp.where(first, low, high).astype(BF)
    give[...] = jnp.where(first, high, low).astype(BF)


def plane_sum(core, a):
    whole = pl.BlockSpec(memory_space=pltpu.VMEM)
    half = jax.ShapeDtypeStruct((SLOTS // 2, DM), BF)
    return pl.pallas_call(
        plane_kernel,
        in_specs=[pl.BlockSpec(memory_space=pltpu.SMEM), whole],
        out_specs=[whole] * 3,
        out_shape=[jax.ShapeDtypeStruct((PIECE, DM), BF), half, half],
        compiler_params=pltpu.CompilerParams(vmem_limit_bytes=16 << 20),
        cost_estimate=pl.CostEstimate(flops=1 << 19, bytes_accessed=2 << 20, transcendentals=0),
        name="plane_sum",
    )(core, a)


def seg_kernel(seg, own, r1, r2, r3, out, parts):
    for back, r in enumerate((own, r1, r2, r3)):
        parts[lax.rem(seg[0] + SEG - back, SEG)] = r[...].astype(F32)
    total = ((parts[0] + parts[1]) + (parts[2] + parts[3])).astype(BF)
    for i in range(PLANE):
        out[i] = total


def seg_sum(seg, own, r1, r2, r3):
    whole = pl.BlockSpec(memory_space=pltpu.VMEM)
    return pl.pallas_call(
        seg_kernel,
        in_specs=[pl.BlockSpec(memory_space=pltpu.SMEM)] + [whole] * 4,
        out_specs=whole,
        out_shape=jax.ShapeDtypeStruct((PLANE, PIECE, DM), BF),
        scratch_shapes=[pltpu.VMEM((SEG, PIECE, DM), F32)],
        compiler_params=pltpu.CompilerParams(vmem_limit_bytes=16 << 20),
        cost_estimate=pl.CostEstimate(flops=1 << 17, bytes_accessed=1 << 20, transcendentals=0),
        name="seg_sum",
    )(seg, own, r1, r2, r3)


def half_kernel(own, core, half, *rest):
    out, wide, sem = rest[-3:]
    place = core[0] if own else 1 - core[0]
    copies = []
    for i in range(4):
        at = pl.ds(i * PLANE // 4, PLANE // 4)
        wide[at] = half[at].astype(F32)
        copies.append(pltpu.make_async_copy(wide.at[at], out.at[at, place], sem.at[i]))
        copies[-1].start()
    for copy in copies:
        copy.wait()


def whole_grad(core, half, before=None):
    own = before is None
    far = pl.BlockSpec(memory_space=pl.ANY)
    return pl.pallas_call(
        functools.partial(half_kernel, own),
        in_specs=[pl.BlockSpec(memory_space=pltpu.SMEM), pl.BlockSpec(memory_space=pltpu.VMEM)]
        + ([] if own else [far]),
        out_specs=far,
        out_shape=jax.ShapeDtypeStruct((PLANE, CORES, PIECE, DM), F32),
        scratch_shapes=[pltpu.VMEM((PLANE, PIECE, DM), F32), pltpu.SemaphoreType.DMA((4,))],
        input_output_aliases={} if own else {2: 0},
        compiler_params=pltpu.CompilerParams(vmem_limit_bytes=16 << 20),
        cost_estimate=pl.CostEstimate(flops=1 << 18, bytes_accessed=3 << 20, transcendentals=0),
        name="own_half" if own else "far_half",
    )(core, half, *([] if own else [before]))


def owner_kernel(core, asked, keep, got, out):
    near = asked[:, core[0]].reshape(SLOTS // 2, 128)
    far = asked[:, 1 - core[0]].reshape(SLOTS // 2, 128)
    out[...] = dot_tn(owner_pick(near), keep[...]) + dot_tn(owner_pick(far), got[...])


def owner_sum(core, asked, keep, got):
    whole = pl.BlockSpec(memory_space=pltpu.VMEM)
    return pl.pallas_call(
        owner_kernel,
        in_specs=[pl.BlockSpec(memory_space=pltpu.SMEM)] + [whole] * 3,
        out_specs=whole,
        out_shape=jax.ShapeDtypeStruct((N, DM), F32),
        compiler_params=pltpu.CompilerParams(vmem_limit_bytes=16 << 20),
        cost_estimate=pl.CostEstimate(
            flops=2 * N * DM * SLOTS, bytes_accessed=1 << 20, transcendentals=0
        ),
        name="owner_sum",
    )(core, asked.reshape(PLANE, CORES, CAP, 128), keep, got)


def exchange(rows, axes, count):
    blocks = rows.reshape(count, -1, rows.shape[-1])
    return lax.all_to_all(blocks, axes, split_axis=0, concat_axis=0, tiled=True).reshape(rows.shape)


def plane(x):
    return lax.all_to_all(x, FLAT, split_axis=0, concat_axis=0, tiled=True)


def on_device(
    memory_base,
    messages,
    touched,
    gru_input,
    gru_state,
    attn_weights,
    frequency,
    request_rows,
    event_slots,
    delays,
    upstream,
):
    seg = lax.axis_index("y").reshape(1)
    core = lax.axis_index("core").reshape(1)
    swap = [(0, 1), (1, 0)]
    ids = request_rows.reshape(1, SLOTS)
    ids_far = lax.ppermute(ids, "core", swap)
    written = gru(touched, memory_base, messages[0], gru_input, gru_state)
    r1 = lax.ppermute(written, "y", [(0, 1), (1, 2), (2, 3)])
    r2 = lax.ppermute(written, "y", [(0, 2), (1, 3)])
    r3 = lax.ppermute(written, "y", [(0, 3)])
    written, late, seg, core = lax.optimization_barrier((written, delays[0].T, seg, core))
    chosen_t = event_slots.transpose(2, 0, 1)
    code_t, time_kv, chosen, wanted = time_parts(
        core, ids, ids_far, late, frequency.reshape(1, DM), attn_weights, chosen_t
    )
    written, wanted, code_t, time_kv, chosen = lax.optimization_barrier(
        (written, wanted, code_t, time_kv, chosen)
    )
    asked = plane(wanted).reshape(SLOTS, 128)
    memory, rows = start_rows(seg, memory_base, written, r1, r2, r3, asked)
    slots = exchange(rows, NODE, OWNERS)
    up = upstream[0]
    mine, other, *kept = attend(
        core, slots, chosen, chosen_t, time_kv, code_t, up, attn_weights
    )
    partner = lax.ppermute(other, "core", swap)
    embedded, d_slots = events(*kept, up, attn_weights)
    parts = plane(pair_sum(mine, partner, d_slots))
    part, keep, give = plane_sum(core, parts)
    got = lax.ppermute(give, "core", swap)
    turns = {s: [(i, (i + s) % SEG) for i in range(SEG)] for s in (1, 2, 3)}
    r2 = lax.ppermute(part, "y", turns[2])
    memory_grad = owner_sum(core, asked, keep, got)
    late, memory_grad = lax.optimization_barrier((part, memory_grad))
    r1, r3 = (lax.ppermute(late, "y", turns[s]) for s in (1, 3))
    half = plane(seg_sum(seg, part, r1, r2, r3))
    far = lax.ppermute(half, "core", swap)
    weight_grad = whole_grad(core, far, whole_grad(core, half))
    return embedded[None], memory[None], memory_grad[None], weight_grad.reshape(4, DM, DM)


def solution(mesh):
    fine = Mesh(mesh.devices.reshape(SEG, X, Z, CORES), ("y", "x", "z", "core"))
    both = P("y", NODE, None)
    in_specs = (P(NODE, None), both, P("y", NODE), P(), P(), P(), P(), both, both, both, both)
    out_specs = (both, both, both, P())
    return jax.shard_map(
        on_device, mesh=fine, in_specs=in_specs, out_specs=out_specs, check_vma=False
    )
```

```python
import functools
import math

import jax
import jax.numpy as jnp
from jax import lax
from jax.experimental import pallas as pl
from jax.experimental.pallas import tpu as pltpu
from jax.sharding import Mesh
from jax.sharding import PartitionSpec as P

SEG, X, Z, CORES = 4, 4, 4, 2
OWNERS = X * Z * CORES
PLANE = X * Z
DM = 512
HEADS = 2
HEAD = DM // HEADS
K = 8
E = 256
N = 256
CAP = 8
SLOTS = 256
PIECE = 64
TILE = 128
TILES = E // TILE
ROWS = K * TILE
STEP = 32
ABSENT = 2.0
NODE = ("x", "z", "core")
FLAT = ("x", "z")
BF = jnp.bfloat16
F32 = jnp.float32

COS = (
    0.9999992107823232,
    -19.738980355764145,
    64.92865742103731,
    -85.27162153434116,
    58.79049212030933,
    -21.07110562791079,
)


def dot(a, b):
    return jnp.dot(a, b, preferred_element_type=F32)


def dot_tn(a, b):
    return lax.dot_general(a, b, (((0,), (0,)), ((), ())), preferred_element_type=F32)


def dot_nt(a, b):
    return lax.dot_general(a, b, (((1,), (1,)), ((), ())), preferred_element_type=F32)


def iota(shape, axis):
    return lax.broadcasted_iota(jnp.int32, shape, axis)


def column(row):
    n = row.shape[1]
    square = jnp.where(iota((n, n), 0) == iota((n, n), 1), row.astype(F32), 0.0)
    return jnp.sum(square, axis=1, keepdims=True)


def gru_kernel(touched, state, message, w_input, w_state, out, st, ms, wi, ws, sem):
    moves = ((state, st), (w_state, ws), (message, ms), (w_input, wi))
    copies = [pltpu.make_async_copy(a, b, sem.at[i]) for i, (a, b) in enumerate(moves)]
    for i, copy in enumerate(copies):
        copy.start(priority=i % 2)
    keep = column(touched[...]) > 0.5
    copies[0].wait()
    copies[1].wait()
    s = st[...]
    from_state = [dot(s, ws[:, i * DM : (i + 1) * DM]) for i in range(3)]
    copies[2].wait()
    copies[3].wait()
    m = ms[...]
    update = jax.nn.sigmoid(dot(m, wi[:, :DM]) + from_state[0])
    reset = jax.nn.sigmoid(dot(m, wi[:, DM : 2 * DM]) + from_state[1])
    candidate = jnp.tanh(dot(m, wi[:, 2 * DM :]) + reset * from_state[2])
    fresh = (1.0 - update) * candidate + update * s.astype(F32)
    out[...] = jnp.where(keep, fresh, ABSENT).astype(BF)


def gru(touched, state, message, w_input, w_state):
    whole = pl.BlockSpec(memory_space=pltpu.VMEM)
    far = pl.BlockSpec(memory_space=pl.ANY)
    return pl.pallas_call(
        gru_kernel,
        in_specs=[whole] + [far] * 4,
        out_specs=whole,
        out_shape=jax.ShapeDtypeStruct((N, DM), BF),
        scratch_shapes=[
            pltpu.VMEM((N, DM), BF),
            pltpu.VMEM((N, DM), BF),
            pltpu.VMEM((DM, 3 * DM), BF),
            pltpu.VMEM((DM, 3 * DM), BF),
            pltpu.SemaphoreType.DMA((4,)),
        ],
        compiler_params=pltpu.CompilerParams(vmem_limit_bytes=56 << 20),
        cost_estimate=pl.CostEstimate(
            flops=4 * N * DM * 3 * DM, bytes_accessed=4 << 20, transcendentals=3 * N * DM
        ),
        name="gru",
    )(touched, state, message, w_input, w_state)


def time_kernel(core, ids, ids_far, delays, frequency, w, chosen, code_t, time_kv, picked, wanted):
    first = core[0] == 0
    for side, row in ((0, ids), (1, ids_far)):
        blocks = jnp.broadcast_to(column(row[...]), (SLOTS, 128)).reshape(PLANE, CORES, CAP, 128)
        mine = jnp.where(first, blocks[:, 0], blocks[:, 1]).astype(jnp.int32)
        wanted[:, core[0] if side == 0 else 1 - core[0]] = mine
    lane = iota((E, 128), 1)
    columns = jnp.zeros((E, 128), F32)
    for j in range(K + 1):
        columns = jnp.where(lane == j, column(chosen[j]), columns)
    picked[...] = columns.astype(jnp.int32)
    turns = frequency[...] * (1.0 / (2.0 * math.pi))
    for tile in range(TILES):
        for k in range(K):
            delay = column(delays[k : k + 1, tile * TILE : (tile + 1) * TILE])
            angle = delay * turns
            part = angle - jnp.round(angle)
            u = part * part
            wave = jnp.full_like(u, COS[-1])
            for c in COS[-2::-1]:
                wave = wave * u + c
            at = slice(k * TILE, (k + 1) * TILE)
            code_t[tile, :, at] = wave.T.astype(BF)
            wave = wave.astype(BF)
            time_kv[tile, at, :DM] = dot(wave, w[1]).astype(BF)
            time_kv[tile, at, DM:] = dot(wave, w[2]).astype(BF)


def time_parts(core, ids, ids_far, delays, frequency, weights, chosen):
    whole = pl.BlockSpec(memory_space=pltpu.VMEM)
    return pl.pallas_call(
        time_kernel,
        in_specs=[pl.BlockSpec(memory_space=pltpu.SMEM)] + [whole] * 6,
        out_specs=[whole] * 4,
        out_shape=[
            jax.ShapeDtypeStruct((TILES, DM, ROWS), BF),
            jax.ShapeDtypeStruct((TILES, ROWS, 2 * DM), BF),
            jax.ShapeDtypeStruct((E, 128), jnp.int32),
            jax.ShapeDtypeStruct((PLANE, CORES, CAP, 128), jnp.int32),
        ],
        compiler_params=pltpu.CompilerParams(vmem_limit_bytes=24 << 20),
        cost_estimate=pl.CostEstimate(
            flops=4 * K * E * DM * DM, bytes_accessed=8 << 20, transcendentals=K * E * DM
        ),
        name="time_parts",
    )(core, ids, ids_far, delays, frequency, weights, chosen)


def owner_pick(asked):
    ids = jnp.concatenate([asked] * (N // 128), axis=1)
    return (ids == iota(ids.shape, 1)).astype(F32).astype(BF)


def start_kernel(seg, state, written, r1, r2, r3, asked, memory, rows):
    start = state[...]
    for back, r in ((3, r3), (2, r2), (1, r1)):
        row = r[...]
        start = jnp.where((row.astype(F32) < 1.5) & (seg[0] >= back), row, start)
    own = written[...]
    memory[...] = jnp.where(own.astype(F32) < 1.5, own, start)
    rows[...] = dot(owner_pick(asked[...]), start).astype(BF)


def start_rows(seg, state, written, r1, r2, r3, asked):
    whole = pl.BlockSpec(memory_space=pltpu.VMEM)
    return pl.pallas_call(
        start_kernel,
        in_specs=[pl.BlockSpec(memory_space=pltpu.SMEM)] + [whole] * 6,
        out_specs=[whole] * 2,
        out_shape=[
            jax.ShapeDtypeStruct((N, DM), BF),
            jax.ShapeDtypeStruct((SLOTS, DM), BF),
        ],
        compiler_params=pltpu.CompilerParams(vmem_limit_bytes=16 << 20),
        cost_estimate=pl.CostEstimate(
            flops=2 * N * DM * SLOTS, bytes_accessed=2 << 20, transcendentals=0
        ),
        name="start_rows",
    )(seg, state, written, r1, r2, r3, asked)


def attend_kernel(
    core, slots, chosen, chosen_t, tkv, tt, up, wq,
    mine, other, att, src, pick_t, s_qkv,
    skv, d_att, qf, both, dkv, dq,
):
    rows = slots[...]
    pick = (chosen[:, 0:1] == iota((E, SLOTS), 1)).astype(F32).astype(BF)
    src[...] = dot(pick, rows).astype(BF)
    skv[:, :DM] = dot(rows, wq[1]).astype(BF)
    skv[:, DM:] = dot(rows, wq[2]).astype(BF)
    qf[...] = dot(pick, dot(rows, wq[0]).astype(BF))
    d_att[...] = dot_nt(up[...], wq[3])

    lane = iota((STEP, 128), 1)
    lane_a = lane < K
    lane_b = (lane >= K) & (lane < 2 * K)
    scale = 1.0 / math.sqrt(HEAD)

    def per_head(x):
        a = jnp.sum(jnp.where(lane_a, x, 0.0), axis=1, keepdims=True)
        b = jnp.sum(jnp.where(lane_b, x, 0.0), axis=1, keepdims=True)
        return jnp.where(lane_a, a, b)

    def gather(i):
        ids = chosen[i * TILE : (i + 1) * TILE, :]
        slot = iota((TILE, SLOTS), 1)
        pick = jnp.concatenate(
            [(ids[:, 1 + k : 2 + k] == slot).astype(F32) for k in range(K)], axis=0
        ).astype(BF)
        both[i] = dot(pick, skv[...])

    def step(i, j):
        at = slice(i * TILE + j * STEP, i * TILE + (j + 1) * STEP)
        scores = jnp.zeros((STEP, 128), F32)
        d_probs = jnp.zeros((STEP, 128), F32)
        for h in range(HEADS):
            part = slice(h * HEAD, (h + 1) * HEAD)
            part_v = slice(DM + h * HEAD, DM + (h + 1) * HEAD)
            query = qf[at, part]
            d_out = d_att[at, part]
            for k in range(K):
                row = slice(k * TILE + j * STEP, k * TILE + (j + 1) * STEP)
                key = both[i, row, part] + tkv[i, row, part].astype(F32)
                value = both[i, row, part_v] + tkv[i, row, part_v].astype(F32)
                both[i, row, part] = key
                both[i, row, part_v] = value
                here = lane == h * K + k
                scores = jnp.where(here, jnp.sum(query * key, axis=1, keepdims=True), scores)
                d_probs = jnp.where(here, jnp.sum(d_out * value, axis=1, keepdims=True), d_probs)
        powered = jnp.exp(scores * scale)
        probs = powered / per_head(powered)
        d_scores = probs * (d_probs - per_head(probs * d_probs)) * scale
        for h in range(HEADS):
            part = slice(h * HEAD, (h + 1) * HEAD)
            part_v = slice(DM + h * HEAD, DM + (h + 1) * HEAD)
            query = qf[at, part]
            d_out = d_att[at, part]
            attended = jnp.zeros((STEP, HEAD), F32)
            d_query = jnp.zeros((STEP, HEAD), F32)
            for k in range(K):
                row = slice(k * TILE + j * STEP, k * TILE + (j + 1) * STEP)
                c = h * K + k
                p = jnp.broadcast_to(probs[:, c : c + 1], (STEP, HEAD))
                d = jnp.broadcast_to(d_scores[:, c : c + 1], (STEP, HEAD))
                attended += p * both[i, row, part_v]
                d_query += d * both[i, row, part]
                dkv[i, row, part] = (d * query).astype(BF)
                dkv[i, row, part_v] = (p * d_out).astype(BF)
            att[at, part] = attended.astype(BF)
            dq[at, part] = d_query.astype(BF)

    for i in range(TILES):
        gather(i)
    sub = iota((SLOTS, TILE), 0)
    s_kv = dot_t = None
    for i in range(TILES):
        for j in range(TILE // STEP):
            step(i, j)
        spread = jnp.concatenate(
            [
                (sub == chosen_t[1 + k, :, i * TILE : (i + 1) * TILE]).astype(F32)
                for k in range(K)
            ],
            axis=1,
        ).astype(BF)
        one, two = dot(spread, dkv[i]), dot(tt[i], dkv[i])
        s_kv = one if i == 0 else s_kv + one
        dot_t = two if i == 0 else dot_t + two
    s_kv = s_kv.astype(BF)
    pick_t[...] = (iota((SLOTS, E), 0) == chosen_t[0]).astype(F32).astype(BF)
    s_q = dot(pick_t[...], dq[...]).astype(BF)
    s_qkv[:, :DM] = s_q
    s_qkv[:, DM:] = s_kv
    first = core[0] == 0

    def store(i, value):
        blocks = value.reshape(4, CORES, PIECE, DM)
        at = slice(i * 4, (i + 1) * 4)
        mine[at] = jnp.where(first, blocks[:, 0], blocks[:, 1]).astype(BF)
        other[at] = jnp.where(first, blocks[:, 1], blocks[:, 0]).astype(BF)

    store(0, dot_tn(rows, s_q))
    g_kv = dot_t + dot_tn(rows, s_kv)
    store(1, g_kv[:, :DM])
    store(2, g_kv[:, DM:])
    store(3, dot_tn(att[...], up[...]))


def events_kernel(core, att, src, pick_t, s_qkv, up, w, embedded, keep, give):
    embedded[...] = (dot(att[...], w[3]) + src[...].astype(F32)).astype(BF)
    grads = dot(pick_t[...], up[...])
    for i in range(3):
        grads += dot_nt(s_qkv[:, i * DM : (i + 1) * DM], w[i])
    blocks = grads.reshape(PLANE, CORES, CAP, DM)
    first = core[0] == 0
    low, high = (blocks[:, i].reshape(SLOTS // 2, DM) for i in range(2))
    keep[...] = jnp.where(first, low, high).astype(BF)
    give[...] = jnp.where(first, high, low).astype(BF)


def events(core, att, src, pick_t, s_qkv, up, weights):
    whole = pl.BlockSpec(memory_space=pltpu.VMEM)
    return pl.pallas_call(
        events_kernel,
        in_specs=[pl.BlockSpec(memory_space=pltpu.SMEM)] + [whole] * 6,
        out_specs=[whole] * 3,
        out_shape=[jax.ShapeDtypeStruct((E, DM), BF)]
        + [jax.ShapeDtypeStruct((SLOTS // 2, DM), BF)] * 2,
        compiler_params=pltpu.CompilerParams(vmem_limit_bytes=16 << 20),
        cost_estimate=pl.CostEstimate(flops=1 << 29, bytes_accessed=4 << 20, transcendentals=0),
        name="events",
    )(core, att, src, pick_t, s_qkv, up, weights)


def attend(core, slots, chosen, chosen_t, time_kv, code_t, up, weights):
    whole = pl.BlockSpec(memory_space=pltpu.VMEM)
    return pl.pallas_call(
        attend_kernel,
        in_specs=[pl.BlockSpec(memory_space=pltpu.SMEM)] + [whole] * 7,
        out_specs=[whole] * 6,
        out_shape=[
            jax.ShapeDtypeStruct((PLANE, PIECE, DM), BF),
            jax.ShapeDtypeStruct((PLANE, PIECE, DM), BF),
            jax.ShapeDtypeStruct((E, DM), BF),
            jax.ShapeDtypeStruct((E, DM), BF),
            jax.ShapeDtypeStruct((SLOTS, E), BF),
            jax.ShapeDtypeStruct((SLOTS, 3 * DM), BF),
        ],
        scratch_shapes=[
            pltpu.VMEM((SLOTS, 2 * DM), BF),
            pltpu.VMEM((E, DM), F32),
            pltpu.VMEM((E, DM), F32),
            pltpu.VMEM((TILES, ROWS, 2 * DM), F32),
            pltpu.VMEM((TILES, ROWS, 2 * DM), BF),
            pltpu.VMEM((E, DM), BF),
        ],
        compiler_params=pltpu.CompilerParams(vmem_limit_bytes=40 << 20),
        cost_estimate=pl.CostEstimate(
            flops=6 << 30, bytes_accessed=14 << 20, transcendentals=E * 128
        ),
        name="attend",
    )(core, slots, chosen, chosen_t, time_kv, code_t, up, weights)


def pair_kernel(a, b, keep, got, out):
    out[:, :PIECE] = (a[...].astype(F32) + b[...].astype(F32)).astype(BF)
    near, far = (x[...].astype(F32).reshape(4, CAP, DM) for x in (keep, got))
    out[:, PIECE:] = jnp.concatenate([near, far], axis=1).astype(BF)


def pair_sum(a, b, keep, got):
    spec = pl.BlockSpec((4, PIECE, DM), lambda i: (i, 0, 0))
    rows = pl.BlockSpec((4 * CAP, DM), lambda i: (i, 0))
    return pl.pallas_call(
        pair_kernel,
        grid=(PLANE // 4,),
        in_specs=[spec, spec, rows, rows],
        out_specs=pl.BlockSpec((4, PIECE + 2 * CAP, DM), lambda i: (i, 0, 0)),
        out_shape=jax.ShapeDtypeStruct((PLANE, PIECE + 2 * CAP, DM), BF),
        compiler_params=pltpu.CompilerParams(vmem_limit_bytes=16 << 20),
        cost_estimate=pl.CostEstimate(flops=1 << 19, bytes_accessed=3 << 20, transcendentals=0),
        name="pair_sum",
    )(a, b, keep, got)


def plane_kernel(a, part, near, far):
    total = a[0, :PIECE].astype(F32)
    for i in range(1, PLANE):
        total += a[i, :PIECE].astype(F32)
    part[...] = total.astype(BF)
    grads = a[:, PIECE:].astype(F32)
    near[...] = grads[:, :CAP].reshape(SLOTS // 2, DM).astype(BF)
    far[...] = grads[:, CAP:].reshape(SLOTS // 2, DM).astype(BF)


def plane_sum(a):
    whole = pl.BlockSpec(memory_space=pltpu.VMEM)
    half = jax.ShapeDtypeStruct((SLOTS // 2, DM), BF)
    return pl.pallas_call(
        plane_kernel,
        in_specs=[whole],
        out_specs=[whole] * 3,
        out_shape=[jax.ShapeDtypeStruct((PIECE, DM), BF), half, half],
        compiler_params=pltpu.CompilerParams(vmem_limit_bytes=16 << 20),
        cost_estimate=pl.CostEstimate(flops=1 << 19, bytes_accessed=2 << 20, transcendentals=0),
        name="plane_sum",
    )(a)


def seg_kernel(seg, own, r1, r2, r3, out, parts):
    for back, r in enumerate((own, r1, r2, r3)):
        parts[lax.rem(seg[0] + SEG - back, SEG)] = r[...].astype(F32)
    total = ((parts[0] + parts[1]) + (parts[2] + parts[3])).astype(BF)
    for i in range(PLANE):
        out[i] = total


def seg_sum(seg, own, r1, r2, r3):
    whole = pl.BlockSpec(memory_space=pltpu.VMEM)
    return pl.pallas_call(
        seg_kernel,
        in_specs=[pl.BlockSpec(memory_space=pltpu.SMEM)] + [whole] * 4,
        out_specs=whole,
        out_shape=jax.ShapeDtypeStruct((PLANE, PIECE, DM), BF),
        scratch_shapes=[pltpu.VMEM((SEG, PIECE, DM), F32)],
        compiler_params=pltpu.CompilerParams(vmem_limit_bytes=16 << 20),
        cost_estimate=pl.CostEstimate(flops=1 << 17, bytes_accessed=1 << 20, transcendentals=0),
        name="seg_sum",
    )(seg, own, r1, r2, r3)


def half_kernel(own, core, half, *rest):
    out, wide, sem = rest[-3:]
    place = core[0] if own else 1 - core[0]
    copies = []
    for i in range(4):
        at = pl.ds(i * PLANE // 4, PLANE // 4)
        wide[at] = half[at].astype(F32)
        copies.append(pltpu.make_async_copy(wide.at[at], out.at[at, place], sem.at[i]))
        copies[-1].start(priority=i % 2)
    for copy in copies:
        copy.wait()


def whole_grad(core, half, before=None):
    own = before is None
    far = pl.BlockSpec(memory_space=pl.ANY)
    return pl.pallas_call(
        functools.partial(half_kernel, own),
        in_specs=[pl.BlockSpec(memory_space=pltpu.SMEM), pl.BlockSpec(memory_space=pltpu.VMEM)]
        + ([] if own else [far]),
        out_specs=far,
        out_shape=jax.ShapeDtypeStruct((PLANE, CORES, PIECE, DM), F32),
        scratch_shapes=[pltpu.VMEM((PLANE, PIECE, DM), F32), pltpu.SemaphoreType.DMA((4,))],
        input_output_aliases={} if own else {2: 0},
        compiler_params=pltpu.CompilerParams(vmem_limit_bytes=16 << 20),
        cost_estimate=pl.CostEstimate(flops=1 << 18, bytes_accessed=3 << 20, transcendentals=0),
        name="own_half" if own else "far_half",
    )(core, half, *([] if own else [before]))


def owner_kernel(core, asked, keep, got, out):
    near = asked[:, core[0]].reshape(SLOTS // 2, 128)
    far = asked[:, 1 - core[0]].reshape(SLOTS // 2, 128)
    out[...] = dot_tn(owner_pick(near), keep[...]) + dot_tn(owner_pick(far), got[...])


def owner_sum(core, asked, keep, got):
    whole = pl.BlockSpec(memory_space=pltpu.VMEM)
    return pl.pallas_call(
        owner_kernel,
        in_specs=[pl.BlockSpec(memory_space=pltpu.SMEM)] + [whole] * 3,
        out_specs=whole,
        out_shape=jax.ShapeDtypeStruct((N, DM), F32),
        compiler_params=pltpu.CompilerParams(vmem_limit_bytes=16 << 20),
        cost_estimate=pl.CostEstimate(
            flops=2 * N * DM * SLOTS, bytes_accessed=1 << 20, transcendentals=0
        ),
        name="owner_sum",
    )(core, asked.reshape(PLANE, CORES, CAP, 128), keep, got)


def exchange(rows, axes, count):
    blocks = rows.reshape(count, -1, rows.shape[-1])
    return lax.all_to_all(blocks, axes, split_axis=0, concat_axis=0, tiled=True).reshape(rows.shape)


def plane(x):
    return lax.all_to_all(x, FLAT, split_axis=0, concat_axis=0, tiled=True)


def on_device(
    memory_base,
    messages,
    touched,
    gru_input,
    gru_state,
    attn_weights,
    frequency,
    request_rows,
    event_slots,
    delays,
    upstream,
):
    seg = lax.axis_index("y").reshape(1)
    core = lax.axis_index("core").reshape(1)
    swap = [(0, 1), (1, 0)]
    ids = request_rows.reshape(1, SLOTS)
    ids_far = lax.ppermute(ids, "core", swap)
    written = gru(touched, memory_base, messages[0], gru_input, gru_state)
    r1 = lax.ppermute(written, "y", [(0, 1), (1, 2), (2, 3)])
    r2 = lax.ppermute(written, "y", [(0, 2), (1, 3)])
    r3 = lax.ppermute(written, "y", [(0, 3)])
    written, late, seg, core = lax.optimization_barrier((written, delays[0].T, seg, core))
    chosen_t = event_slots.transpose(2, 0, 1)
    code_t, time_kv, chosen, wanted = time_parts(
        core, ids, ids_far, late, frequency.reshape(1, DM), attn_weights, chosen_t
    )
    written, wanted, code_t, time_kv, chosen = lax.optimization_barrier(
        (written, wanted, code_t, time_kv, chosen)
    )
    asked = plane(wanted).reshape(SLOTS, 128)
    memory, rows = start_rows(seg, memory_base, written, r1, r2, r3, asked)
    slots = exchange(rows, NODE, OWNERS)
    up = upstream[0]
    mine, other, *kept = attend(
        core, slots, chosen, chosen_t, time_kv, code_t, up, attn_weights
    )
    partner = lax.ppermute(other, "core", swap)
    embedded, keep, give = events(core, *kept, up, attn_weights)
    got = lax.ppermute(give, "core", swap)
    part, near, far = plane_sum(plane(pair_sum(mine, partner, keep, got)))
    r2, r3, r1 = (
        lax.ppermute(part, "y", [(i, (i + s) % SEG) for i in range(SEG)]) for s in (2, 3, 1)
    )
    half = plane(seg_sum(seg, part, r1, r2, r3))
    memory_grad = owner_sum(core, asked, near, far)
    far = lax.ppermute(half, "core", swap)
    weight_grad = whole_grad(core, far, whole_grad(core, half))
    return embedded[None], memory[None], memory_grad[None], weight_grad.reshape(4, DM, DM)


def solution(mesh):
    fine = Mesh(mesh.devices.reshape(SEG, X, Z, CORES), ("y", "x", "z", "core"))
    both = P("y", NODE, None)
    in_specs = (P(NODE, None), both, P("y", NODE), P(), P(), P(), P(), both, both, both, both)
    out_specs = (both, both, both, P())
    return jax.shard_map(
        on_device, mesh=fine, in_specs=in_specs, out_specs=out_specs, check_vma=False
    )
```

```python
import functools
import math

import jax
import jax.numpy as jnp
from jax import lax
from jax.experimental import pallas as pl
from jax.experimental.pallas import tpu as pltpu
from jax.sharding import Mesh
from jax.sharding import PartitionSpec as P

SEG, X, Z, CORES = 4, 4, 4, 2
OWNERS = X * Z * CORES
PLANE = X * Z
DM = 512
HEADS = 2
HEAD = DM // HEADS
K = 8
E = 256
N = 256
CAP = 8
SLOTS = 256
PIECE = 64
TILE = 128
TILES = E // TILE
ROWS = K * TILE
STEP = 32
ABSENT = 2.0
NODE = ("x", "z", "core")
FLAT = ("x", "z")
BF = jnp.bfloat16
F32 = jnp.float32

COS = (
    0.9999992107823232,
    -19.738980355764145,
    64.92865742103731,
    -85.27162153434116,
    58.79049212030933,
    -21.07110562791079,
)


def dot(a, b):
    return jnp.dot(a, b, preferred_element_type=F32)


def dot_tn(a, b):
    return lax.dot_general(a, b, (((0,), (0,)), ((), ())), preferred_element_type=F32)


def dot_nt(a, b):
    return lax.dot_general(a, b, (((1,), (1,)), ((), ())), preferred_element_type=F32)


def iota(shape, axis):
    return lax.broadcasted_iota(jnp.int32, shape, axis)


def column(row):
    n = row.shape[1]
    square = jnp.where(iota((n, n), 0) == iota((n, n), 1), row.astype(F32), 0.0)
    return jnp.sum(square, axis=1, keepdims=True)


def gru_kernel(touched, state, message, w_input, w_state, out, st, ms, wi, ws, sem):
    moves = ((state, st), (w_state, ws), (message, ms), (w_input, wi))
    copies = [pltpu.make_async_copy(a, b, sem.at[i]) for i, (a, b) in enumerate(moves)]
    for i, copy in enumerate(copies):
        copy.start(priority=i % 2)
    keep = column(touched[...]) > 0.5
    copies[0].wait()
    copies[1].wait()
    s = st[...]
    from_state = [dot(s, ws[:, i * DM : (i + 1) * DM]) for i in range(3)]
    copies[2].wait()
    copies[3].wait()
    m = ms[...]
    update = jax.nn.sigmoid(dot(m, wi[:, :DM]) + from_state[0])
    reset = jax.nn.sigmoid(dot(m, wi[:, DM : 2 * DM]) + from_state[1])
    candidate = jnp.tanh(dot(m, wi[:, 2 * DM :]) + reset * from_state[2])
    fresh = (1.0 - update) * candidate + update * s.astype(F32)
    out[...] = jnp.where(keep, fresh, ABSENT).astype(BF)


def gru(touched, state, message, w_input, w_state):
    whole = pl.BlockSpec(memory_space=pltpu.VMEM)
    far = pl.BlockSpec(memory_space=pl.ANY)
    return pl.pallas_call(
        gru_kernel,
        in_specs=[whole] + [far] * 4,
        out_specs=whole,
        out_shape=jax.ShapeDtypeStruct((N, DM), BF),
        scratch_shapes=[
            pltpu.VMEM((N, DM), BF),
            pltpu.VMEM((N, DM), BF),
            pltpu.VMEM((DM, 3 * DM), BF),
            pltpu.VMEM((DM, 3 * DM), BF),
            pltpu.SemaphoreType.DMA((4,)),
        ],
        compiler_params=pltpu.CompilerParams(vmem_limit_bytes=56 << 20),
        cost_estimate=pl.CostEstimate(
            flops=4 * N * DM * 3 * DM, bytes_accessed=4 << 20, transcendentals=3 * N * DM
        ),
        name="gru",
    )(touched, state, message, w_input, w_state)


def time_kernel(ids, delays, frequency, w, chosen, code_t, time_kv, picked, wanted):
    wanted[...] = jnp.broadcast_to(column(ids[...]), (SLOTS, 128)).astype(jnp.int32)
    lane = iota((E, 128), 1)
    columns = jnp.zeros((E, 128), F32)
    for j in range(K + 1):
        columns = jnp.where(lane == j, column(chosen[j]), columns)
    picked[...] = columns.astype(jnp.int32)
    turns = frequency[...] * (1.0 / (2.0 * math.pi))
    for tile in range(TILES):
        for k in range(K):
            delay = column(delays[k : k + 1, tile * TILE : (tile + 1) * TILE])
            angle = delay * turns
            part = angle - jnp.round(angle)
            u = part * part
            wave = jnp.full_like(u, COS[-1])
            for c in COS[-2::-1]:
                wave = wave * u + c
            at = slice(k * TILE, (k + 1) * TILE)
            code_t[tile, :, at] = wave.T.astype(BF)
            wave = wave.astype(BF)
            time_kv[tile, at, :DM] = dot(wave, w[1]).astype(BF)
            time_kv[tile, at, DM:] = dot(wave, w[2]).astype(BF)


def time_parts(ids, delays, frequency, weights, chosen):
    whole = pl.BlockSpec(memory_space=pltpu.VMEM)
    return pl.pallas_call(
        time_kernel,
        in_specs=[whole] * 5,
        out_specs=[whole] * 4,
        out_shape=[
            jax.ShapeDtypeStruct((TILES, DM, ROWS), BF),
            jax.ShapeDtypeStruct((TILES, ROWS, 2 * DM), BF),
            jax.ShapeDtypeStruct((E, 128), jnp.int32),
            jax.ShapeDtypeStruct((SLOTS, 128), jnp.int32),
        ],
        compiler_params=pltpu.CompilerParams(vmem_limit_bytes=24 << 20),
        cost_estimate=pl.CostEstimate(
            flops=4 * K * E * DM * DM, bytes_accessed=8 << 20, transcendentals=K * E * DM
        ),
        name="time_parts",
    )(ids, delays, frequency, weights, chosen)


def owner_pick(asked):
    ids = jnp.concatenate([asked] * (N // 128), axis=1)
    return (ids == iota(ids.shape, 1)).astype(F32).astype(BF)


def start_kernel(seg, state, written, r1, r2, r3, asked, memory, rows):
    start = state[...]
    for back, r in ((3, r3), (2, r2), (1, r1)):
        row = r[...]
        start = jnp.where((row.astype(F32) < 1.5) & (seg[0] >= back), row, start)
    own = written[...]
    memory[...] = jnp.where(own.astype(F32) < 1.5, own, start)
    rows[...] = dot(owner_pick(asked[...]), start).astype(BF)


def start_rows(seg, state, written, r1, r2, r3, asked):
    whole = pl.BlockSpec(memory_space=pltpu.VMEM)
    return pl.pallas_call(
        start_kernel,
        in_specs=[pl.BlockSpec(memory_space=pltpu.SMEM)] + [whole] * 6,
        out_specs=[whole] * 2,
        out_shape=[
            jax.ShapeDtypeStruct((N, DM), BF),
            jax.ShapeDtypeStruct((SLOTS, DM), BF),
        ],
        compiler_params=pltpu.CompilerParams(vmem_limit_bytes=16 << 20),
        cost_estimate=pl.CostEstimate(
            flops=2 * N * DM * SLOTS, bytes_accessed=2 << 20, transcendentals=0
        ),
        name="start_rows",
    )(seg, state, written, r1, r2, r3, asked)


def attend_kernel(
    core, slots, chosen, chosen_t, tkv, tt, up, wq,
    mine, other, att, src, pick_t, s_qkv,
    skv, d_att, qf, both, dkv, dq,
):
    rows = slots[...]
    pick = (chosen[:, 0:1] == iota((E, SLOTS), 1)).astype(F32).astype(BF)
    src[...] = dot(pick, rows).astype(BF)
    skv[:, :DM] = dot(rows, wq[1]).astype(BF)
    skv[:, DM:] = dot(rows, wq[2]).astype(BF)
    qf[...] = dot(pick, dot(rows, wq[0]).astype(BF))
    d_att[...] = dot_nt(up[...], wq[3])

    lane = iota((STEP, 128), 1)
    lane_a = lane < K
    lane_b = (lane >= K) & (lane < 2 * K)
    scale = 1.0 / math.sqrt(HEAD)

    def per_head(x):
        a = jnp.sum(jnp.where(lane_a, x, 0.0), axis=1, keepdims=True)
        b = jnp.sum(jnp.where(lane_b, x, 0.0), axis=1, keepdims=True)
        return jnp.where(lane_a, a, b)

    def gather(i):
        ids = chosen[i * TILE : (i + 1) * TILE, :]
        slot = iota((TILE, SLOTS), 1)
        pick = jnp.concatenate(
            [(ids[:, 1 + k : 2 + k] == slot).astype(F32) for k in range(K)], axis=0
        ).astype(BF)
        both[i] = dot(pick, skv[...])

    def step(i, j):
        at = slice(i * TILE + j * STEP, i * TILE + (j + 1) * STEP)
        scores = jnp.zeros((STEP, 128), F32)
        d_probs = jnp.zeros((STEP, 128), F32)
        for h in range(HEADS):
            part = slice(h * HEAD, (h + 1) * HEAD)
            part_v = slice(DM + h * HEAD, DM + (h + 1) * HEAD)
            query = qf[at, part]
            d_out = d_att[at, part]
            for k in range(K):
                row = slice(k * TILE + j * STEP, k * TILE + (j + 1) * STEP)
                key = both[i, row, part] + tkv[i, row, part].astype(F32)
                value = both[i, row, part_v] + tkv[i, row, part_v].astype(F32)
                both[i, row, part] = key
                both[i, row, part_v] = value
                here = lane == h * K + k
                scores = jnp.where(here, jnp.sum(query * key, axis=1, keepdims=True), scores)
                d_probs = jnp.where(here, jnp.sum(d_out * value, axis=1, keepdims=True), d_probs)
        powered = jnp.exp(scores * scale)
        probs = powered / per_head(powered)
        d_scores = probs * (d_probs - per_head(probs * d_probs)) * scale
        for h in range(HEADS):
            part = slice(h * HEAD, (h + 1) * HEAD)
            part_v = slice(DM + h * HEAD, DM + (h + 1) * HEAD)
            query = qf[at, part]
            d_out = d_att[at, part]
            attended = jnp.zeros((STEP, HEAD), F32)
            d_query = jnp.zeros((STEP, HEAD), F32)
            for k in range(K):
                row = slice(k * TILE + j * STEP, k * TILE + (j + 1) * STEP)
                c = h * K + k
                p = jnp.broadcast_to(probs[:, c : c + 1], (STEP, HEAD))
                d = jnp.broadcast_to(d_scores[:, c : c + 1], (STEP, HEAD))
                attended += p * both[i, row, part_v]
                d_query += d * both[i, row, part]
                dkv[i, row, part] = (d * query).astype(BF)
                dkv[i, row, part_v] = (p * d_out).astype(BF)
            att[at, part] = attended.astype(BF)
            dq[at, part] = d_query.astype(BF)

    for i in range(TILES):
        gather(i)
    sub = iota((SLOTS, TILE), 0)
    s_kv = dot_t = None
    for i in range(TILES):
        for j in range(TILE // STEP):
            step(i, j)
        spread = jnp.concatenate(
            [
                (sub == chosen_t[1 + k, :, i * TILE : (i + 1) * TILE]).astype(F32)
                for k in range(K)
            ],
            axis=1,
        ).astype(BF)
        one, two = dot(spread, dkv[i]), dot(tt[i], dkv[i])
        s_kv = one if i == 0 else s_kv + one
        dot_t = two if i == 0 else dot_t + two
    s_kv = s_kv.astype(BF)
    pick_t[...] = (iota((SLOTS, E), 0) == chosen_t[0]).astype(F32).astype(BF)
    s_q = dot(pick_t[...], dq[...]).astype(BF)
    s_qkv[:, :DM] = s_q
    s_qkv[:, DM:] = s_kv
    first = core[0] == 0

    def store(i, value):
        blocks = value.reshape(4, CORES, PIECE, DM)
        at = slice(i * 4, (i + 1) * 4)
        mine[at] = jnp.where(first, blocks[:, 0], blocks[:, 1]).astype(BF)
        other[at] = jnp.where(first, blocks[:, 1], blocks[:, 0]).astype(BF)

    store(0, dot_tn(rows, s_q))
    g_kv = dot_t + dot_tn(rows, s_kv)
    store(1, g_kv[:, :DM])
    store(2, g_kv[:, DM:])
    store(3, dot_tn(att[...], up[...]))


def events_kernel(att, src, pick_t, s_qkv, up, w, embedded, d_slots):
    embedded[...] = (dot(att[...], w[3]) + src[...].astype(F32)).astype(BF)
    grads = dot(pick_t[...], up[...])
    for i in range(3):
        grads += dot_nt(s_qkv[:, i * DM : (i + 1) * DM], w[i])
    d_slots[...] = grads.astype(BF)


def events(att, src, pick_t, s_qkv, up, weights):
    whole = pl.BlockSpec(memory_space=pltpu.VMEM)
    return pl.pallas_call(
        events_kernel,
        in_specs=[whole] * 6,
        out_specs=[whole] * 2,
        out_shape=[jax.ShapeDtypeStruct((E, DM), BF), jax.ShapeDtypeStruct((SLOTS, DM), BF)],
        compiler_params=pltpu.CompilerParams(vmem_limit_bytes=16 << 20),
        cost_estimate=pl.CostEstimate(flops=1 << 29, bytes_accessed=4 << 20, transcendentals=0),
        name="events",
    )(att, src, pick_t, s_qkv, up, weights)


def attend(core, slots, chosen, chosen_t, time_kv, code_t, up, weights):
    whole = pl.BlockSpec(memory_space=pltpu.VMEM)
    return pl.pallas_call(
        attend_kernel,
        in_specs=[pl.BlockSpec(memory_space=pltpu.SMEM)] + [whole] * 7,
        out_specs=[whole] * 6,
        out_shape=[
            jax.ShapeDtypeStruct((PLANE, PIECE, DM), BF),
            jax.ShapeDtypeStruct((PLANE, PIECE, DM), BF),
            jax.ShapeDtypeStruct((E, DM), BF),
            jax.ShapeDtypeStruct((E, DM), BF),
            jax.ShapeDtypeStruct((SLOTS, E), BF),
            jax.ShapeDtypeStruct((SLOTS, 3 * DM), BF),
        ],
        scratch_shapes=[
            pltpu.VMEM((SLOTS, 2 * DM), BF),
            pltpu.VMEM((E, DM), F32),
            pltpu.VMEM((E, DM), F32),
            pltpu.VMEM((TILES, ROWS, 2 * DM), F32),
            pltpu.VMEM((TILES, ROWS, 2 * DM), BF),
            pltpu.VMEM((E, DM), BF),
        ],
        compiler_params=pltpu.CompilerParams(vmem_limit_bytes=40 << 20),
        cost_estimate=pl.CostEstimate(
            flops=6 << 30, bytes_accessed=14 << 20, transcendentals=E * 128
        ),
        name="attend",
    )(core, slots, chosen, chosen_t, time_kv, code_t, up, weights)


def pair_kernel(a, b, out):
    out[...] = (a[...].astype(F32) + b[...].astype(F32)).astype(BF)


def pair_sum(a, b):
    whole = pl.BlockSpec(memory_space=pltpu.VMEM)
    return pl.pallas_call(
        pair_kernel,
        in_specs=[whole] * 2,
        out_specs=whole,
        out_shape=jax.ShapeDtypeStruct((PLANE, PIECE, DM), BF),
        compiler_params=pltpu.CompilerParams(vmem_limit_bytes=16 << 20),
        cost_estimate=pl.CostEstimate(flops=1 << 19, bytes_accessed=3 << 20, transcendentals=0),
        name="pair_sum",
    )(a, b)


def plane_kernel(a, part):
    total = a[0].astype(F32)
    for i in range(1, PLANE):
        total += a[i].astype(F32)
    part[...] = total.astype(BF)


def plane_sum(a):
    whole = pl.BlockSpec(memory_space=pltpu.VMEM)
    return pl.pallas_call(
        plane_kernel,
        in_specs=[whole],
        out_specs=whole,
        out_shape=jax.ShapeDtypeStruct((PIECE, DM), BF),
        compiler_params=pltpu.CompilerParams(vmem_limit_bytes=16 << 20),
        cost_estimate=pl.CostEstimate(flops=1 << 19, bytes_accessed=2 << 20, transcendentals=0),
        name="plane_sum",
    )(a)


def seg_kernel(seg, own, r1, r2, r3, out, parts):
    for back, r in enumerate((own, r1, r2, r3)):
        parts[lax.rem(seg[0] + SEG - back, SEG)] = r[...].astype(F32)
    total = ((parts[0] + parts[1]) + (parts[2] + parts[3])).astype(BF)
    for i in range(PLANE):
        out[i] = total


def seg_sum(seg, own, r1, r2, r3):
    whole = pl.BlockSpec(memory_space=pltpu.VMEM)
    return pl.pallas_call(
        seg_kernel,
        in_specs=[pl.BlockSpec(memory_space=pltpu.SMEM)] + [whole] * 4,
        out_specs=whole,
        out_shape=jax.ShapeDtypeStruct((PLANE, PIECE, DM), BF),
        scratch_shapes=[pltpu.VMEM((SEG, PIECE, DM), F32)],
        compiler_params=pltpu.CompilerParams(vmem_limit_bytes=16 << 20),
        cost_estimate=pl.CostEstimate(flops=1 << 17, bytes_accessed=1 << 20, transcendentals=0),
        name="seg_sum",
    )(seg, own, r1, r2, r3)


def half_kernel(own, core, half, *rest):
    out, wide, sem = rest[-3:]
    place = core[0] if own else 1 - core[0]
    copies = []
    for i in range(4):
        at = pl.ds(i * PLANE // 4, PLANE // 4)
        wide[at] = half[at].astype(F32)
        copies.append(pltpu.make_async_copy(wide.at[at], out.at[at, place], sem.at[i]))
        copies[-1].start(priority=i % 2)
    for copy in copies:
        copy.wait()


def whole_grad(core, half, before=None):
    own = before is None
    far = pl.BlockSpec(memory_space=pl.ANY)
    return pl.pallas_call(
        functools.partial(half_kernel, own),
        in_specs=[pl.BlockSpec(memory_space=pltpu.SMEM), pl.BlockSpec(memory_space=pltpu.VMEM)]
        + ([] if own else [far]),
        out_specs=far,
        out_shape=jax.ShapeDtypeStruct((PLANE, CORES, PIECE, DM), F32),
        scratch_shapes=[pltpu.VMEM((PLANE, PIECE, DM), F32), pltpu.SemaphoreType.DMA((4,))],
        input_output_aliases={} if own else {2: 0},
        compiler_params=pltpu.CompilerParams(vmem_limit_bytes=16 << 20),
        cost_estimate=pl.CostEstimate(flops=1 << 18, bytes_accessed=3 << 20, transcendentals=0),
        name="own_half" if own else "far_half",
    )(core, half, *([] if own else [before]))


def owner_kernel(asked, grads, out):
    out[...] = dot_tn(owner_pick(asked[...]), grads[...])


def owner_sum(asked, grads):
    whole = pl.BlockSpec(memory_space=pltpu.VMEM)
    return pl.pallas_call(
        owner_kernel,
        in_specs=[whole] * 2,
        out_specs=whole,
        out_shape=jax.ShapeDtypeStruct((N, DM), F32),
        compiler_params=pltpu.CompilerParams(vmem_limit_bytes=16 << 20),
        cost_estimate=pl.CostEstimate(
            flops=2 * N * DM * SLOTS, bytes_accessed=1 << 20, transcendentals=0
        ),
        name="owner_sum",
    )(asked, grads)


def exchange(rows, axes, count):
    blocks = rows.reshape(count, -1, rows.shape[-1])
    return lax.all_to_all(blocks, axes, split_axis=0, concat_axis=0, tiled=True).reshape(rows.shape)


def plane(x):
    return lax.all_to_all(x, FLAT, split_axis=0, concat_axis=0, tiled=True)


def on_device(
    memory_base,
    messages,
    touched,
    gru_input,
    gru_state,
    attn_weights,
    frequency,
    request_rows,
    event_slots,
    delays,
    upstream,
):
    seg = lax.axis_index("y").reshape(1)
    core = lax.axis_index("core").reshape(1)
    swap = [(0, 1), (1, 0)]
    ids = request_rows.reshape(1, SLOTS)
    written = gru(touched, memory_base, messages[0], gru_input, gru_state)
    r1 = lax.ppermute(written, "y", [(0, 1), (1, 2), (2, 3)])
    r2 = lax.ppermute(written, "y", [(0, 2), (1, 3)])
    r3 = lax.ppermute(written, "y", [(0, 3)])
    written, late, seg, core = lax.optimization_barrier((written, delays[0].T, seg, core))
    chosen_t = event_slots.transpose(2, 0, 1)
    code_t, time_kv, chosen, wanted = time_parts(
        ids, late, frequency.reshape(1, DM), attn_weights, chosen_t
    )
    written, wanted, code_t, time_kv, chosen = lax.optimization_barrier(
        (written, wanted, code_t, time_kv, chosen)
    )
    asked = exchange(wanted, NODE, OWNERS)
    memory, rows = start_rows(seg, memory_base, written, r1, r2, r3, asked)
    slots = exchange(rows, NODE, OWNERS)
    up = upstream[0]
    mine, other, *kept = attend(
        core, slots, chosen, chosen_t, time_kv, code_t, up, attn_weights
    )
    partner = lax.ppermute(other, "core", swap)
    embedded, d_slots = events(*kept, up, attn_weights)
    pairs, d_slots = lax.optimization_barrier((pair_sum(mine, partner), d_slots))
    parts, back = lax.optimization_barrier((plane(pairs), exchange(d_slots, NODE, OWNERS)))
    part = plane_sum(parts)
    r2, r3, r1 = (
        lax.ppermute(part, "y", [(i, (i + s) % SEG) for i in range(SEG)]) for s in (2, 3, 1)
    )
    half = plane(seg_sum(seg, part, r1, r2, r3))
    memory_grad = owner_sum(asked, back)
    far = lax.ppermute(half, "core", swap)
    weight_grad = whole_grad(core, far, whole_grad(core, half))
    return embedded[None], memory[None], memory_grad[None], weight_grad.reshape(4, DM, DM)


def solution(mesh):
    fine = Mesh(mesh.devices.reshape(SEG, X, Z, CORES), ("y", "x", "z", "core"))
    both = P("y", NODE, None)
    in_specs = (P(NODE, None), both, P("y", NODE), P(), P(), P(), P(), both, both, both, both)
    out_specs = (both, both, both, P())
    return jax.shard_map(
        on_device, mesh=fine, in_specs=in_specs, out_specs=out_specs, check_vma=False
    )
```

```python
import functools
import math

import jax
import jax.numpy as jnp
from jax import lax
from jax.experimental import pallas as pl
from jax.experimental.pallas import tpu as pltpu
from jax.sharding import Mesh
from jax.sharding import PartitionSpec as P

SEG, X, Z, CORES = 4, 4, 4, 2
OWNERS = X * Z * CORES
PLANE = X * Z
DM = 512
HEADS = 2
HEAD = DM // HEADS
K = 8
E = 256
N = 256
CAP = 8
SLOTS = 256
PIECE = 64
TILE = 128
TILES = E // TILE
ROWS = K * TILE
STEP = 32
ABSENT = 2.0
NODE = ("x", "z", "core")
FLAT = ("x", "z")
BF = jnp.bfloat16
F32 = jnp.float32

COS = (
    0.9999992107823232,
    -19.738980355764145,
    64.92865742103731,
    -85.27162153434116,
    58.79049212030933,
    -21.07110562791079,
)


def dot(a, b):
    return jnp.dot(a, b, preferred_element_type=F32)


def dot_tn(a, b):
    return lax.dot_general(a, b, (((0,), (0,)), ((), ())), preferred_element_type=F32)


def dot_nt(a, b):
    return lax.dot_general(a, b, (((1,), (1,)), ((), ())), preferred_element_type=F32)


def iota(shape, axis):
    return lax.broadcasted_iota(jnp.int32, shape, axis)


def column(row):
    n = row.shape[1]
    square = jnp.where(iota((n, n), 0) == iota((n, n), 1), row.astype(F32), 0.0)
    return jnp.sum(square, axis=1, keepdims=True)


def gru_kernel(touched, state, message, w_input, w_state, out, st, ms, wi, ws, sem):
    moves = ((state, st), (w_state, ws), (message, ms), (w_input, wi))
    copies = [pltpu.make_async_copy(a, b, sem.at[i]) for i, (a, b) in enumerate(moves)]
    for i, copy in enumerate(copies):
        copy.start(priority=i % 2)
    keep = column(touched[...]) > 0.5
    copies[0].wait()
    copies[1].wait()
    s = st[...]
    from_state = [dot(s, ws[:, i * DM : (i + 1) * DM]) for i in range(3)]
    copies[2].wait()
    copies[3].wait()
    m = ms[...]
    update = jax.nn.sigmoid(dot(m, wi[:, :DM]) + from_state[0])
    reset = jax.nn.sigmoid(dot(m, wi[:, DM : 2 * DM]) + from_state[1])
    candidate = jnp.tanh(dot(m, wi[:, 2 * DM :]) + reset * from_state[2])
    fresh = (1.0 - update) * candidate + update * s.astype(F32)
    out[...] = jnp.where(keep, fresh, ABSENT).astype(BF)


def gru(touched, state, message, w_input, w_state):
    whole = pl.BlockSpec(memory_space=pltpu.VMEM)
    far = pl.BlockSpec(memory_space=pl.ANY)
    return pl.pallas_call(
        gru_kernel,
        in_specs=[whole] + [far] * 4,
        out_specs=whole,
        out_shape=jax.ShapeDtypeStruct((N, DM), BF),
        scratch_shapes=[
            pltpu.VMEM((N, DM), BF),
            pltpu.VMEM((N, DM), BF),
            pltpu.VMEM((DM, 3 * DM), BF),
            pltpu.VMEM((DM, 3 * DM), BF),
            pltpu.SemaphoreType.DMA((4,)),
        ],
        compiler_params=pltpu.CompilerParams(vmem_limit_bytes=56 << 20),
        cost_estimate=pl.CostEstimate(
            flops=4 * N * DM * 3 * DM, bytes_accessed=4 << 20, transcendentals=3 * N * DM
        ),
        name="gru",
    )(touched, state, message, w_input, w_state)


def time_kernel(ids, delays, frequency, w, chosen, code_t, time_kv, picked, wanted, code):
    wanted[...] = jnp.broadcast_to(column(ids[...]), (SLOTS, 128)).astype(jnp.int32)
    lane = iota((E, 128), 1)
    columns = jnp.zeros((E, 128), F32)
    for j in range(K + 1):
        columns = jnp.where(lane == j, column(chosen[j]), columns)
    picked[...] = columns.astype(jnp.int32)
    turns = frequency[...] * (1.0 / (2.0 * math.pi))
    for tile in range(TILES):
        for k in range(K):
            delay = column(delays[k : k + 1, tile * TILE : (tile + 1) * TILE])
            angle = delay * turns
            part = angle - jnp.round(angle)
            u = part * part
            wave = jnp.full_like(u, COS[-1])
            for c in COS[-2::-1]:
                wave = wave * u + c
            at = slice(k * TILE, (k + 1) * TILE)
            code_t[tile, :, at] = wave.T.astype(BF)
            code[tile, at] = wave.astype(BF)
        for i in range(2):
            time_kv[tile, :, i * DM : (i + 1) * DM] = dot(code[tile], w[1 + i]).astype(BF)


def time_parts(ids, delays, frequency, weights, chosen):
    whole = pl.BlockSpec(memory_space=pltpu.VMEM)
    return pl.pallas_call(
        time_kernel,
        in_specs=[whole] * 5,
        out_specs=[whole] * 4,
        out_shape=[
            jax.ShapeDtypeStruct((TILES, DM, ROWS), BF),
            jax.ShapeDtypeStruct((TILES, ROWS, 2 * DM), BF),
            jax.ShapeDtypeStruct((E, 128), jnp.int32),
            jax.ShapeDtypeStruct((SLOTS, 128), jnp.int32),
        ],
        scratch_shapes=[pltpu.VMEM((TILES, ROWS, DM), BF)],
        compiler_params=pltpu.CompilerParams(vmem_limit_bytes=24 << 20),
        cost_estimate=pl.CostEstimate(
            flops=4 * K * E * DM * DM, bytes_accessed=8 << 20, transcendentals=K * E * DM
        ),
        name="time_parts",
    )(ids, delays, frequency, weights, chosen)


def owner_pick(asked):
    ids = jnp.concatenate([asked] * (N // 128), axis=1)
    return (ids == iota(ids.shape, 1)).astype(F32).astype(BF)


def start_kernel(seg, state, written, r1, r2, r3, asked, memory, rows):
    start = state[...]
    for back, r in ((3, r3), (2, r2), (1, r1)):
        row = r[...]
        start = jnp.where((row.astype(F32) < 1.5) & (seg[0] >= back), row, start)
    own = written[...]
    memory[...] = jnp.where(own.astype(F32) < 1.5, own, start)
    rows[...] = dot(owner_pick(asked[...]), start).astype(BF)


def start_rows(seg, state, written, r1, r2, r3, asked):
    whole = pl.BlockSpec(memory_space=pltpu.VMEM)
    return pl.pallas_call(
        start_kernel,
        in_specs=[pl.BlockSpec(memory_space=pltpu.SMEM)] + [whole] * 6,
        out_specs=[whole] * 2,
        out_shape=[
            jax.ShapeDtypeStruct((N, DM), BF),
            jax.ShapeDtypeStruct((SLOTS, DM), BF),
        ],
        compiler_params=pltpu.CompilerParams(vmem_limit_bytes=16 << 20),
        cost_estimate=pl.CostEstimate(
            flops=2 * N * DM * SLOTS, bytes_accessed=2 << 20, transcendentals=0
        ),
        name="start_rows",
    )(seg, state, written, r1, r2, r3, asked)


def attend_kernel(
    core, slots, chosen, chosen_t, tkv, tt, up, wq,
    mine, other, att, src, pick_t, s_qkv,
    skv, d_att, qf, both, dkv, dq,
):
    rows = slots[...]
    pick = (chosen[:, 0:1] == iota((E, SLOTS), 1)).astype(F32).astype(BF)
    src[...] = dot(pick, rows).astype(BF)
    skv[:, :DM] = dot(rows, wq[1]).astype(BF)
    skv[:, DM:] = dot(rows, wq[2]).astype(BF)
    qf[...] = dot(pick, dot(rows, wq[0]).astype(BF))
    d_att[...] = dot_nt(up[...], wq[3])

    lane = iota((STEP, 128), 1)
    lane_a = lane < K
    lane_b = (lane >= K) & (lane < 2 * K)
    scale = 1.0 / math.sqrt(HEAD)

    def per_head(x):
        a = jnp.sum(jnp.where(lane_a, x, 0.0), axis=1, keepdims=True)
        b = jnp.sum(jnp.where(lane_b, x, 0.0), axis=1, keepdims=True)
        return jnp.where(lane_a, a, b)

    def gather(i):
        ids = chosen[i * TILE : (i + 1) * TILE, :]
        slot = iota((TILE, SLOTS), 1)
        pick = jnp.concatenate(
            [(ids[:, 1 + k : 2 + k] == slot).astype(F32) for k in range(K)], axis=0
        ).astype(BF)
        both[i] = dot(pick, skv[...])

    def step(i, j):
        at = slice(i * TILE + j * STEP, i * TILE + (j + 1) * STEP)
        scores = jnp.zeros((STEP, 128), F32)
        d_probs = jnp.zeros((STEP, 128), F32)
        for h in range(HEADS):
            part = slice(h * HEAD, (h + 1) * HEAD)
            part_v = slice(DM + h * HEAD, DM + (h + 1) * HEAD)
            query = qf[at, part]
            d_out = d_att[at, part]
            for k in range(K):
                row = slice(k * TILE + j * STEP, k * TILE + (j + 1) * STEP)
                key = both[i, row, part] + tkv[i, row, part].astype(F32)
                value = both[i, row, part_v] + tkv[i, row, part_v].astype(F32)
                both[i, row, part] = key
                both[i, row, part_v] = value
                here = lane == h * K + k
                scores = jnp.where(here, jnp.sum(query * key, axis=1, keepdims=True), scores)
                d_probs = jnp.where(here, jnp.sum(d_out * value, axis=1, keepdims=True), d_probs)
        powered = jnp.exp(scores * scale)
        probs = powered / per_head(powered)
        d_scores = probs * (d_probs - per_head(probs * d_probs)) * scale
        for h in range(HEADS):
            part = slice(h * HEAD, (h + 1) * HEAD)
            part_v = slice(DM + h * HEAD, DM + (h + 1) * HEAD)
            query = qf[at, part]
            d_out = d_att[at, part]
            attended = jnp.zeros((STEP, HEAD), F32)
            d_query = jnp.zeros((STEP, HEAD), F32)
            for k in range(K):
                row = slice(k * TILE + j * STEP, k * TILE + (j + 1) * STEP)
                c = h * K + k
                p = jnp.broadcast_to(probs[:, c : c + 1], (STEP, HEAD))
                d = jnp.broadcast_to(d_scores[:, c : c + 1], (STEP, HEAD))
                attended += p * both[i, row, part_v]
                d_query += d * both[i, row, part]
                dkv[i, row, part] = (d * query).astype(BF)
                dkv[i, row, part_v] = (p * d_out).astype(BF)
            att[at, part] = attended.astype(BF)
            dq[at, part] = d_query.astype(BF)

    for i in range(TILES):
        gather(i)
    sub = iota((SLOTS, TILE), 0)
    s_kv = dot_t = None
    for i in range(TILES):
        for j in range(TILE // STEP):
            step(i, j)
        spread = jnp.concatenate(
            [
                (sub == chosen_t[1 + k, :, i * TILE : (i + 1) * TILE]).astype(F32)
                for k in range(K)
            ],
            axis=1,
        ).astype(BF)
        one, two = dot(spread, dkv[i]), dot(tt[i], dkv[i])
        s_kv = one if i == 0 else s_kv + one
        dot_t = two if i == 0 else dot_t + two
    s_kv = s_kv.astype(BF)
    pick_t[...] = (iota((SLOTS, E), 0) == chosen_t[0]).astype(F32).astype(BF)
    s_q = dot(pick_t[...], dq[...]).astype(BF)
    s_qkv[:, :DM] = s_q
    s_qkv[:, DM:] = s_kv
    first = core[0] == 0

    def store(i, value):
        blocks = value.reshape(4, CORES, PIECE, DM)
        at = slice(i * 4, (i + 1) * 4)
        mine[at] = jnp.where(first, blocks[:, 0], blocks[:, 1]).astype(BF)
        other[at] = jnp.where(first, blocks[:, 1], blocks[:, 0]).astype(BF)

    store(0, dot_tn(rows, s_q))
    g_kv = dot_t + dot_tn(rows, s_kv)
    store(1, g_kv[:, :DM])
    store(2, g_kv[:, DM:])
    store(3, dot_tn(att[...], up[...]))


def events_kernel(core, att, src, pick_t, s_qkv, up, w, embedded, keep, give):
    embedded[...] = (dot(att[...], w[3]) + src[...].astype(F32)).astype(BF)
    grads = dot(pick_t[...], up[...])
    for i in range(3):
        grads += dot_nt(s_qkv[:, i * DM : (i + 1) * DM], w[i])
    blocks = grads.reshape(PLANE, CORES, CAP, DM)
    first = core[0] == 0
    low, high = (blocks[:, i].reshape(SLOTS // 2, DM) for i in range(2))
    keep[...] = jnp.where(first, low, high).astype(BF)
    give[...] = jnp.where(first, high, low).astype(BF)


def events(core, att, src, pick_t, s_qkv, up, weights):
    whole = pl.BlockSpec(memory_space=pltpu.VMEM)
    return pl.pallas_call(
        events_kernel,
        in_specs=[pl.BlockSpec(memory_space=pltpu.SMEM)] + [whole] * 6,
        out_specs=[whole] * 3,
        out_shape=[jax.ShapeDtypeStruct((E, DM), BF)]
        + [jax.ShapeDtypeStruct((SLOTS // 2, DM), BF)] * 2,
        compiler_params=pltpu.CompilerParams(vmem_limit_bytes=16 << 20),
        cost_estimate=pl.CostEstimate(flops=1 << 29, bytes_accessed=4 << 20, transcendentals=0),
        name="events",
    )(core, att, src, pick_t, s_qkv, up, weights)


def attend(core, slots, chosen, chosen_t, time_kv, code_t, up, weights):
    whole = pl.BlockSpec(memory_space=pltpu.VMEM)
    return pl.pallas_call(
        attend_kernel,
        in_specs=[pl.BlockSpec(memory_space=pltpu.SMEM)] + [whole] * 7,
        out_specs=[whole] * 6,
        out_shape=[
            jax.ShapeDtypeStruct((PLANE, PIECE, DM), BF),
            jax.ShapeDtypeStruct((PLANE, PIECE, DM), BF),
            jax.ShapeDtypeStruct((E, DM), BF),
            jax.ShapeDtypeStruct((E, DM), BF),
            jax.ShapeDtypeStruct((SLOTS, E), BF),
            jax.ShapeDtypeStruct((SLOTS, 3 * DM), BF),
        ],
        scratch_shapes=[
            pltpu.VMEM((SLOTS, 2 * DM), BF),
            pltpu.VMEM((E, DM), F32),
            pltpu.VMEM((E, DM), F32),
            pltpu.VMEM((TILES, ROWS, 2 * DM), F32),
            pltpu.VMEM((TILES, ROWS, 2 * DM), BF),
            pltpu.VMEM((E, DM), BF),
        ],
        compiler_params=pltpu.CompilerParams(vmem_limit_bytes=40 << 20),
        cost_estimate=pl.CostEstimate(
            flops=6 << 30, bytes_accessed=14 << 20, transcendentals=E * 128
        ),
        name="attend",
    )(core, slots, chosen, chosen_t, time_kv, code_t, up, weights)


def pair_kernel(a, b, keep, got, out):
    out[:, :PIECE] = (a[...].astype(F32) + b[...].astype(F32)).astype(BF)
    near, far = (x[...].astype(F32).reshape(4, CAP, DM) for x in (keep, got))
    out[:, PIECE:] = jnp.concatenate([near, far], axis=1).astype(BF)


def pair_sum(a, b, keep, got):
    spec = pl.BlockSpec((4, PIECE, DM), lambda i: (i, 0, 0))
    rows = pl.BlockSpec((4 * CAP, DM), lambda i: (i, 0))
    return pl.pallas_call(
        pair_kernel,
        grid=(PLANE // 4,),
        in_specs=[spec, spec, rows, rows],
        out_specs=pl.BlockSpec((4, PIECE + 2 * CAP, DM), lambda i: (i, 0, 0)),
        out_shape=jax.ShapeDtypeStruct((PLANE, PIECE + 2 * CAP, DM), BF),
        compiler_params=pltpu.CompilerParams(vmem_limit_bytes=16 << 20),
        cost_estimate=pl.CostEstimate(flops=1 << 19, bytes_accessed=3 << 20, transcendentals=0),
        name="pair_sum",
    )(a, b, keep, got)


def plane_kernel(a, part, near, far):
    total = a[0, :PIECE].astype(F32)
    for i in range(1, PLANE):
        total += a[i, :PIECE].astype(F32)
    part[...] = total.astype(BF)
    grads = a[:, PIECE:].astype(F32)
    near[...] = grads[:, :CAP].reshape(SLOTS // 2, DM).astype(BF)
    far[...] = grads[:, CAP:].reshape(SLOTS // 2, DM).astype(BF)


def plane_sum(a):
    whole = pl.BlockSpec(memory_space=pltpu.VMEM)
    half = jax.ShapeDtypeStruct((SLOTS // 2, DM), BF)
    return pl.pallas_call(
        plane_kernel,
        in_specs=[whole],
        out_specs=[whole] * 3,
        out_shape=[jax.ShapeDtypeStruct((PIECE, DM), BF), half, half],
        compiler_params=pltpu.CompilerParams(vmem_limit_bytes=16 << 20),
        cost_estimate=pl.CostEstimate(flops=1 << 19, bytes_accessed=2 << 20, transcendentals=0),
        name="plane_sum",
    )(a)


def seg_kernel(seg, own, r1, r2, r3, out, parts):
    for back, r in enumerate((own, r1, r2, r3)):
        parts[lax.rem(seg[0] + SEG - back, SEG)] = r[...].astype(F32)
    total = ((parts[0] + parts[1]) + (parts[2] + parts[3])).astype(BF)
    for i in range(PLANE):
        out[i] = total


def seg_sum(seg, own, r1, r2, r3):
    whole = pl.BlockSpec(memory_space=pltpu.VMEM)
    return pl.pallas_call(
        seg_kernel,
        in_specs=[pl.BlockSpec(memory_space=pltpu.SMEM)] + [whole] * 4,
        out_specs=whole,
        out_shape=jax.ShapeDtypeStruct((PLANE, PIECE, DM), BF),
        scratch_shapes=[pltpu.VMEM((SEG, PIECE, DM), F32)],
        compiler_params=pltpu.CompilerParams(vmem_limit_bytes=16 << 20),
        cost_estimate=pl.CostEstimate(flops=1 << 17, bytes_accessed=1 << 20, transcendentals=0),
        name="seg_sum",
    )(seg, own, r1, r2, r3)


def half_kernel(own, core, half, *rest):
    out, wide, sem = rest[-3:]
    place = core[0] if own else 1 - core[0]
    copies = []
    for i in range(4):
        at = pl.ds(i * PLANE // 4, PLANE // 4)
        wide[at] = half[at].astype(F32)
        copies.append(pltpu.make_async_copy(wide.at[at], out.at[at, place], sem.at[i]))
        copies[-1].start(priority=i % 2)
    for copy in copies:
        copy.wait()


def whole_grad(core, half, before=None):
    own = before is None
    far = pl.BlockSpec(memory_space=pl.ANY)
    return pl.pallas_call(
        functools.partial(half_kernel, own),
        in_specs=[pl.BlockSpec(memory_space=pltpu.SMEM), pl.BlockSpec(memory_space=pltpu.VMEM)]
        + ([] if own else [far]),
        out_specs=far,
        out_shape=jax.ShapeDtypeStruct((PLANE, CORES, PIECE, DM), F32),
        scratch_shapes=[pltpu.VMEM((PLANE, PIECE, DM), F32), pltpu.SemaphoreType.DMA((4,))],
        input_output_aliases={} if own else {2: 0},
        compiler_params=pltpu.CompilerParams(vmem_limit_bytes=16 << 20),
        cost_estimate=pl.CostEstimate(flops=1 << 18, bytes_accessed=3 << 20, transcendentals=0),
        name="own_half" if own else "far_half",
    )(core, half, *([] if own else [before]))


def owner_kernel(core, asked, keep, got, out):
    near = asked[:, core[0]].reshape(SLOTS // 2, 128)
    far = asked[:, 1 - core[0]].reshape(SLOTS // 2, 128)
    out[...] = dot_tn(owner_pick(near), keep[...]) + dot_tn(owner_pick(far), got[...])


def owner_sum(core, asked, keep, got):
    whole = pl.BlockSpec(memory_space=pltpu.VMEM)
    return pl.pallas_call(
        owner_kernel,
        in_specs=[pl.BlockSpec(memory_space=pltpu.SMEM)] + [whole] * 3,
        out_specs=whole,
        out_shape=jax.ShapeDtypeStruct((N, DM), F32),
        compiler_params=pltpu.CompilerParams(vmem_limit_bytes=16 << 20),
        cost_estimate=pl.CostEstimate(
            flops=2 * N * DM * SLOTS, bytes_accessed=1 << 20, transcendentals=0
        ),
        name="owner_sum",
    )(core, asked.reshape(PLANE, CORES, CAP, 128), keep, got)


def exchange(rows, axes, count):
    blocks = rows.reshape(count, -1, rows.shape[-1])
    return lax.all_to_all(blocks, axes, split_axis=0, concat_axis=0, tiled=True).reshape(rows.shape)


def plane(x):
    return lax.all_to_all(x, FLAT, split_axis=0, concat_axis=0, tiled=True)


def on_device(
    memory_base,
    messages,
    touched,
    gru_input,
    gru_state,
    attn_weights,
    frequency,
    request_rows,
    event_slots,
    delays,
    upstream,
):
    seg = lax.axis_index("y").reshape(1)
    core = lax.axis_index("core").reshape(1)
    swap = [(0, 1), (1, 0)]
    ids = request_rows.reshape(1, SLOTS)
    written = gru(touched, memory_base, messages[0], gru_input, gru_state)
    r1 = lax.ppermute(written, "y", [(0, 1), (1, 2), (2, 3)])
    r2 = lax.ppermute(written, "y", [(0, 2), (1, 3)])
    r3 = lax.ppermute(written, "y", [(0, 3)])
    written, late, seg, core = lax.optimization_barrier((written, delays[0].T, seg, core))
    chosen_t = event_slots.transpose(2, 0, 1)
    code_t, time_kv, chosen, wanted = time_parts(
        ids, late, frequency.reshape(1, DM), attn_weights, chosen_t
    )
    written, wanted, code_t, time_kv, chosen = lax.optimization_barrier(
        (written, wanted, code_t, time_kv, chosen)
    )
    asked = exchange(wanted, NODE, OWNERS)
    memory, rows = start_rows(seg, memory_base, written, r1, r2, r3, asked)
    slots = exchange(rows, NODE, OWNERS)
    up = upstream[0]
    mine, other, *kept = attend(
        core, slots, chosen, chosen_t, time_kv, code_t, up, attn_weights
    )
    partner = lax.ppermute(other, "core", swap)
    embedded, keep, give = events(core, *kept, up, attn_weights)
    got = lax.ppermute(give, "core", swap)
    part, near, far = plane_sum(plane(pair_sum(mine, partner, keep, got)))
    r2, r3, r1 = (
        lax.ppermute(part, "y", [(i, (i + s) % SEG) for i in range(SEG)]) for s in (2, 3, 1)
    )
    half = plane(seg_sum(seg, part, r1, r2, r3))
    memory_grad = owner_sum(core, asked, near, far)
    far = lax.ppermute(half, "core", swap)
    weight_grad = whole_grad(core, far, whole_grad(core, half))
    return embedded[None], memory[None], memory_grad[None], weight_grad.reshape(4, DM, DM)


def solution(mesh):
    fine = Mesh(mesh.devices.reshape(SEG, X, Z, CORES), ("y", "x", "z", "core"))
    both = P("y", NODE, None)
    in_specs = (P(NODE, None), both, P("y", NODE), P(), P(), P(), P(), both, both, both, both)
    out_specs = (both, both, both, P())
    return jax.shard_map(
        on_device, mesh=fine, in_specs=in_specs, out_specs=out_specs, check_vma=False
    )
```

```python
import functools
import math

import jax
import jax.numpy as jnp
from jax import lax
from jax.experimental import pallas as pl
from jax.experimental.pallas import tpu as pltpu
from jax.sharding import Mesh
from jax.sharding import PartitionSpec as P

SEG, X, Z, CORES = 4, 4, 4, 2
OWNERS = X * Z * CORES
PLANE = X * Z
DM = 512
HEADS = 2
HEAD = DM // HEADS
K = 8
E = 256
N = 256
CAP = 8
SLOTS = 256
PIECE = 64
TILE = 128
TILES = E // TILE
ROWS = K * TILE
STEP = 32
ABSENT = 2.0
NODE = ("x", "z", "core")
FLAT = ("x", "z")
BF = jnp.bfloat16
F32 = jnp.float32

COS = (
    0.9999992107823232,
    -19.738980355764145,
    64.92865742103731,
    -85.27162153434116,
    58.79049212030933,
    -21.07110562791079,
)


def dot(a, b):
    return jnp.dot(a, b, preferred_element_type=F32)


def dot_tn(a, b):
    return lax.dot_general(a, b, (((0,), (0,)), ((), ())), preferred_element_type=F32)


def dot_nt(a, b):
    return lax.dot_general(a, b, (((1,), (1,)), ((), ())), preferred_element_type=F32)


def iota(shape, axis):
    return lax.broadcasted_iota(jnp.int32, shape, axis)


def column(row):
    n = row.shape[1]
    square = jnp.where(iota((n, n), 0) == iota((n, n), 1), row.astype(F32), 0.0)
    return jnp.sum(square, axis=1, keepdims=True)


def gru_kernel(touched, state, message, w_input, w_state, out, st, ms, wi, ws, sem):
    moves = ((state, st), (w_state, ws), (message, ms), (w_input, wi))
    copies = [pltpu.make_async_copy(a, b, sem.at[i]) for i, (a, b) in enumerate(moves)]
    for i, copy in enumerate(copies):
        copy.start(priority=i % 2)
    keep = column(touched[...]) > 0.5
    copies[0].wait()
    copies[1].wait()
    s = st[...]
    from_state = [dot(s, ws[:, i * DM : (i + 1) * DM]) for i in range(3)]
    copies[2].wait()
    copies[3].wait()
    m = ms[...]
    update = jax.nn.sigmoid(dot(m, wi[:, :DM]) + from_state[0])
    reset = jax.nn.sigmoid(dot(m, wi[:, DM : 2 * DM]) + from_state[1])
    candidate = jnp.tanh(dot(m, wi[:, 2 * DM :]) + reset * from_state[2])
    fresh = (1.0 - update) * candidate + update * s.astype(F32)
    out[...] = jnp.where(keep, fresh, ABSENT).astype(BF)


def gru(touched, state, message, w_input, w_state):
    whole = pl.BlockSpec(memory_space=pltpu.VMEM)
    far = pl.BlockSpec(memory_space=pl.ANY)
    return pl.pallas_call(
        gru_kernel,
        in_specs=[whole] + [far] * 4,
        out_specs=whole,
        out_shape=jax.ShapeDtypeStruct((N, DM), BF),
        scratch_shapes=[
            pltpu.VMEM((N, DM), BF),
            pltpu.VMEM((N, DM), BF),
            pltpu.VMEM((DM, 3 * DM), BF),
            pltpu.VMEM((DM, 3 * DM), BF),
            pltpu.SemaphoreType.DMA((4,)),
        ],
        compiler_params=pltpu.CompilerParams(vmem_limit_bytes=56 << 20),
        cost_estimate=pl.CostEstimate(
            flops=4 * N * DM * 3 * DM, bytes_accessed=4 << 20, transcendentals=3 * N * DM
        ),
        name="gru",
    )(touched, state, message, w_input, w_state)


def time_kernel(ids, delays, frequency, w, chosen, code_t, time_kv, picked, wanted, code):
    wanted[...] = jnp.broadcast_to(column(ids[...]), (SLOTS, 128)).astype(jnp.int32)
    lane = iota((E, 128), 1)
    columns = jnp.zeros((E, 128), F32)
    for j in range(K + 1):
        columns = jnp.where(lane == j, column(chosen[j]), columns)
    picked[...] = columns.astype(jnp.int32)
    turns = frequency[...] * (1.0 / (2.0 * math.pi))
    for tile in range(TILES):
        for k in range(K):
            delay = column(delays[k : k + 1, tile * TILE : (tile + 1) * TILE])
            angle = delay * turns
            part = angle - jnp.round(angle)
            u = part * part
            wave = jnp.full_like(u, COS[-1])
            for c in COS[-2::-1]:
                wave = wave * u + c
            at = slice(k * TILE, (k + 1) * TILE)
            wave = wave.astype(BF)
            code_t[tile, :, at] = wave.T
            code[tile, at] = wave
        for i in range(2):
            time_kv[tile, :, i * DM : (i + 1) * DM] = dot(code[tile], w[1 + i]).astype(BF)


def time_parts(ids, delays, frequency, weights, chosen):
    whole = pl.BlockSpec(memory_space=pltpu.VMEM)
    return pl.pallas_call(
        time_kernel,
        in_specs=[whole] * 5,
        out_specs=[whole] * 4,
        out_shape=[
            jax.ShapeDtypeStruct((TILES, DM, ROWS), BF),
            jax.ShapeDtypeStruct((TILES, ROWS, 2 * DM), BF),
            jax.ShapeDtypeStruct((E, 128), jnp.int32),
            jax.ShapeDtypeStruct((SLOTS, 128), jnp.int32),
        ],
        scratch_shapes=[pltpu.VMEM((TILES, ROWS, DM), BF)],
        compiler_params=pltpu.CompilerParams(vmem_limit_bytes=24 << 20),
        cost_estimate=pl.CostEstimate(
            flops=4 * K * E * DM * DM, bytes_accessed=8 << 20, transcendentals=K * E * DM
        ),
        name="time_parts",
    )(ids, delays, frequency, weights, chosen)


def owner_pick(asked):
    ids = jnp.concatenate([asked] * (N // 128), axis=1)
    return (ids == iota(ids.shape, 1)).astype(F32).astype(BF)


def start_kernel(seg, state, written, r1, r2, r3, asked, memory, rows):
    start = state[...]
    for back, r in ((3, r3), (2, r2), (1, r1)):
        row = r[...]
        start = jnp.where((row.astype(F32) < 1.5) & (seg[0] >= back), row, start)
    own = written[...]
    memory[...] = jnp.where(own.astype(F32) < 1.5, own, start)
    rows[...] = dot(owner_pick(asked[...]), start).astype(BF)


def start_rows(seg, state, written, r1, r2, r3, asked):
    whole = pl.BlockSpec(memory_space=pltpu.VMEM)
    return pl.pallas_call(
        start_kernel,
        in_specs=[pl.BlockSpec(memory_space=pltpu.SMEM)] + [whole] * 6,
        out_specs=[whole] * 2,
        out_shape=[
            jax.ShapeDtypeStruct((N, DM), BF),
            jax.ShapeDtypeStruct((SLOTS, DM), BF),
        ],
        compiler_params=pltpu.CompilerParams(vmem_limit_bytes=16 << 20),
        cost_estimate=pl.CostEstimate(
            flops=2 * N * DM * SLOTS, bytes_accessed=2 << 20, transcendentals=0
        ),
        name="start_rows",
    )(seg, state, written, r1, r2, r3, asked)


def attend_kernel(
    core, slots, chosen, chosen_t, tkv, tt, up, wq,
    mine, other, att, src, pick_t, s_qkv,
    skv, d_att, qf, both, dkv, dq,
):
    rows = slots[...]
    pick = (chosen[:, 0:1] == iota((E, SLOTS), 1)).astype(F32).astype(BF)
    src[...] = dot(pick, rows).astype(BF)
    skv[:, :DM] = dot(rows, wq[1]).astype(BF)
    skv[:, DM:] = dot(rows, wq[2]).astype(BF)
    qf[...] = dot(pick, dot(rows, wq[0]).astype(BF))
    d_att[...] = dot_nt(up[...], wq[3])

    lane = iota((STEP, 128), 1)
    lane_a = lane < K
    lane_b = (lane >= K) & (lane < 2 * K)
    scale = 1.0 / math.sqrt(HEAD)

    def per_head(x):
        a = jnp.sum(jnp.where(lane_a, x, 0.0), axis=1, keepdims=True)
        b = jnp.sum(jnp.where(lane_b, x, 0.0), axis=1, keepdims=True)
        return jnp.where(lane_a, a, b)

    def gather(i):
        ids = chosen[i * TILE : (i + 1) * TILE, :]
        slot = iota((TILE, SLOTS), 1)
        pick = jnp.concatenate(
            [(ids[:, 1 + k : 2 + k] == slot).astype(F32) for k in range(K)], axis=0
        ).astype(BF)
        both[i] = dot(pick, skv[...])

    def step(i, j):
        at = slice(i * TILE + j * STEP, i * TILE + (j + 1) * STEP)
        scores = jnp.zeros((STEP, 128), F32)
        d_probs = jnp.zeros((STEP, 128), F32)
        for h in range(HEADS):
            part = slice(h * HEAD, (h + 1) * HEAD)
            part_v = slice(DM + h * HEAD, DM + (h + 1) * HEAD)
            query = qf[at, part]
            d_out = d_att[at, part]
            for k in range(K):
                row = slice(k * TILE + j * STEP, k * TILE + (j + 1) * STEP)
                key = both[i, row, part] + tkv[i, row, part].astype(F32)
                value = both[i, row, part_v] + tkv[i, row, part_v].astype(F32)
                both[i, row, part] = key
                both[i, row, part_v] = value
                here = lane == h * K + k
                scores = jnp.where(here, jnp.sum(query * key, axis=1, keepdims=True), scores)
                d_probs = jnp.where(here, jnp.sum(d_out * value, axis=1, keepdims=True), d_probs)
        powered = jnp.exp(scores * scale)
        probs = powered / per_head(powered)
        d_scores = probs * (d_probs - per_head(probs * d_probs)) * scale
        for h in range(HEADS):
            part = slice(h * HEAD, (h + 1) * HEAD)
            part_v = slice(DM + h * HEAD, DM + (h + 1) * HEAD)
            query = qf[at, part]
            d_out = d_att[at, part]
            attended = jnp.zeros((STEP, HEAD), F32)
            d_query = jnp.zeros((STEP, HEAD), F32)
            for k in range(K):
                row = slice(k * TILE + j * STEP, k * TILE + (j + 1) * STEP)
                c = h * K + k
                p = jnp.broadcast_to(probs[:, c : c + 1], (STEP, HEAD))
                d = jnp.broadcast_to(d_scores[:, c : c + 1], (STEP, HEAD))
                attended += p * both[i, row, part_v]
                d_query += d * both[i, row, part]
                dkv[i, row, part] = (d * query).astype(BF)
                dkv[i, row, part_v] = (p * d_out).astype(BF)
            att[at, part] = attended.astype(BF)
            dq[at, part] = d_query.astype(BF)

    for i in range(TILES):
        gather(i)
    sub = iota((SLOTS, TILE), 0)
    s_kv = dot_t = None
    for i in range(TILES):
        for j in range(TILE // STEP):
            step(i, j)
        spread = jnp.concatenate(
            [
                (sub == chosen_t[1 + k, :, i * TILE : (i + 1) * TILE]).astype(F32)
                for k in range(K)
            ],
            axis=1,
        ).astype(BF)
        one, two = dot(spread, dkv[i]), dot(tt[i], dkv[i])
        s_kv = one if i == 0 else s_kv + one
        dot_t = two if i == 0 else dot_t + two
    s_kv = s_kv.astype(BF)
    pick_t[...] = (iota((SLOTS, E), 0) == chosen_t[0]).astype(F32).astype(BF)
    s_q = dot(pick_t[...], dq[...]).astype(BF)
    s_qkv[:, :DM] = s_q
    s_qkv[:, DM:] = s_kv
    first = core[0] == 0

    def store(i, value):
        blocks = value.reshape(4, CORES, PIECE, DM)
        at = slice(i * 4, (i + 1) * 4)
        mine[at] = jnp.where(first, blocks[:, 0], blocks[:, 1]).astype(BF)
        other[at] = jnp.where(first, blocks[:, 1], blocks[:, 0]).astype(BF)

    store(0, dot_tn(rows, s_q))
    g_kv = dot_t + dot_tn(rows, s_kv)
    store(1, g_kv[:, :DM])
    store(2, g_kv[:, DM:])
    store(3, dot_tn(att[...], up[...]))


def events_kernel(core, att, src, pick_t, s_qkv, up, w, embedded, keep, give):
    embedded[...] = (dot(att[...], w[3]) + src[...].astype(F32)).astype(BF)
    grads = dot(pick_t[...], up[...])
    for i in range(3):
        grads += dot_nt(s_qkv[:, i * DM : (i + 1) * DM], w[i])
    blocks = grads.reshape(PLANE, CORES, CAP, DM)
    first = core[0] == 0
    low, high = (blocks[:, i].reshape(SLOTS // 2, DM) for i in range(2))
    keep[...] = jnp.where(first, low, high).astype(BF)
    give[...] = jnp.where(first, high, low).astype(BF)


def events(core, att, src, pick_t, s_qkv, up, weights):
    whole = pl.BlockSpec(memory_space=pltpu.VMEM)
    return pl.pallas_call(
        events_kernel,
        in_specs=[pl.BlockSpec(memory_space=pltpu.SMEM)] + [whole] * 6,
        out_specs=[whole] * 3,
        out_shape=[jax.ShapeDtypeStruct((E, DM), BF)]
        + [jax.ShapeDtypeStruct((SLOTS // 2, DM), BF)] * 2,
        compiler_params=pltpu.CompilerParams(vmem_limit_bytes=16 << 20),
        cost_estimate=pl.CostEstimate(flops=1 << 29, bytes_accessed=4 << 20, transcendentals=0),
        name="events",
    )(core, att, src, pick_t, s_qkv, up, weights)


def attend(core, slots, chosen, chosen_t, time_kv, code_t, up, weights):
    whole = pl.BlockSpec(memory_space=pltpu.VMEM)
    return pl.pallas_call(
        attend_kernel,
        in_specs=[pl.BlockSpec(memory_space=pltpu.SMEM)] + [whole] * 7,
        out_specs=[whole] * 6,
        out_shape=[
            jax.ShapeDtypeStruct((PLANE, PIECE, DM), BF),
            jax.ShapeDtypeStruct((PLANE, PIECE, DM), BF),
            jax.ShapeDtypeStruct((E, DM), BF),
            jax.ShapeDtypeStruct((E, DM), BF),
            jax.ShapeDtypeStruct((SLOTS, E), BF),
            jax.ShapeDtypeStruct((SLOTS, 3 * DM), BF),
        ],
        scratch_shapes=[
            pltpu.VMEM((SLOTS, 2 * DM), BF),
            pltpu.VMEM((E, DM), F32),
            pltpu.VMEM((E, DM), F32),
            pltpu.VMEM((TILES, ROWS, 2 * DM), F32),
            pltpu.VMEM((TILES, ROWS, 2 * DM), BF),
            pltpu.VMEM((E, DM), BF),
        ],
        compiler_params=pltpu.CompilerParams(vmem_limit_bytes=40 << 20),
        cost_estimate=pl.CostEstimate(
            flops=6 << 30, bytes_accessed=14 << 20, transcendentals=E * 128
        ),
        name="attend",
    )(core, slots, chosen, chosen_t, time_kv, code_t, up, weights)


def pair_kernel(a, b, keep, got, out):
    out[:, :PIECE] = (a[...].astype(F32) + b[...].astype(F32)).astype(BF)
    near, far = (x[...].astype(F32).reshape(4, CAP, DM) for x in (keep, got))
    out[:, PIECE:] = jnp.concatenate([near, far], axis=1).astype(BF)


def pair_sum(a, b, keep, got):
    spec = pl.BlockSpec((4, PIECE, DM), lambda i: (i, 0, 0))
    rows = pl.BlockSpec((4 * CAP, DM), lambda i: (i, 0))
    return pl.pallas_call(
        pair_kernel,
        grid=(PLANE // 4,),
        in_specs=[spec, spec, rows, rows],
        out_specs=pl.BlockSpec((4, PIECE + 2 * CAP, DM), lambda i: (i, 0, 0)),
        out_shape=jax.ShapeDtypeStruct((PLANE, PIECE + 2 * CAP, DM), BF),
        compiler_params=pltpu.CompilerParams(vmem_limit_bytes=16 << 20),
        cost_estimate=pl.CostEstimate(flops=1 << 19, bytes_accessed=3 << 20, transcendentals=0),
        name="pair_sum",
    )(a, b, keep, got)


def plane_kernel(a, part, near, far):
    total = a[0, :PIECE].astype(F32)
    for i in range(1, PLANE):
        total += a[i, :PIECE].astype(F32)
    part[...] = total.astype(BF)
    grads = a[:, PIECE:].astype(F32)
    near[...] = grads[:, :CAP].reshape(SLOTS // 2, DM).astype(BF)
    far[...] = grads[:, CAP:].reshape(SLOTS // 2, DM).astype(BF)


def plane_sum(a):
    whole = pl.BlockSpec(memory_space=pltpu.VMEM)
    half = jax.ShapeDtypeStruct((SLOTS // 2, DM), BF)
    return pl.pallas_call(
        plane_kernel,
        in_specs=[whole],
        out_specs=[whole] * 3,
        out_shape=[jax.ShapeDtypeStruct((PIECE, DM), BF), half, half],
        compiler_params=pltpu.CompilerParams(vmem_limit_bytes=16 << 20),
        cost_estimate=pl.CostEstimate(flops=1 << 19, bytes_accessed=2 << 20, transcendentals=0),
        name="plane_sum",
    )(a)


def seg_kernel(seg, own, r1, r2, r3, out, parts):
    for back, r in enumerate((own, r1, r2, r3)):
        parts[lax.rem(seg[0] + SEG - back, SEG)] = r[...].astype(F32)
    total = ((parts[0] + parts[1]) + (parts[2] + parts[3])).astype(BF)
    for i in range(PLANE):
        out[i] = total


def seg_sum(seg, own, r1, r2, r3):
    whole = pl.BlockSpec(memory_space=pltpu.VMEM)
    return pl.pallas_call(
        seg_kernel,
        in_specs=[pl.BlockSpec(memory_space=pltpu.SMEM)] + [whole] * 4,
        out_specs=whole,
        out_shape=jax.ShapeDtypeStruct((PLANE, PIECE, DM), BF),
        scratch_shapes=[pltpu.VMEM((SEG, PIECE, DM), F32)],
        compiler_params=pltpu.CompilerParams(vmem_limit_bytes=16 << 20),
        cost_estimate=pl.CostEstimate(flops=1 << 17, bytes_accessed=1 << 20, transcendentals=0),
        name="seg_sum",
    )(seg, own, r1, r2, r3)


def half_kernel(own, core, half, *rest):
    out, wide, sem = rest[-3:]
    place = core[0] if own else 1 - core[0]
    copies = []
    for i in range(4):
        at = pl.ds(i * PLANE // 4, PLANE // 4)
        wide[at] = half[at].astype(F32)
        copies.append(pltpu.make_async_copy(wide.at[at], out.at[at, place], sem.at[i]))
        copies[-1].start(priority=i % 2)
    for copy in copies:
        copy.wait()


def whole_grad(core, half, before=None):
    own = before is None
    far = pl.BlockSpec(memory_space=pl.ANY)
    return pl.pallas_call(
        functools.partial(half_kernel, own),
        in_specs=[pl.BlockSpec(memory_space=pltpu.SMEM), pl.BlockSpec(memory_space=pltpu.VMEM)]
        + ([] if own else [far]),
        out_specs=far,
        out_shape=jax.ShapeDtypeStruct((PLANE, CORES, PIECE, DM), F32),
        scratch_shapes=[pltpu.VMEM((PLANE, PIECE, DM), F32), pltpu.SemaphoreType.DMA((4,))],
        input_output_aliases={} if own else {2: 0},
        compiler_params=pltpu.CompilerParams(vmem_limit_bytes=16 << 20),
        cost_estimate=pl.CostEstimate(flops=1 << 18, bytes_accessed=3 << 20, transcendentals=0),
        name="own_half" if own else "far_half",
    )(core, half, *([] if own else [before]))


def owner_kernel(core, asked, keep, got, out):
    near = asked[:, core[0]].reshape(SLOTS // 2, 128)
    far = asked[:, 1 - core[0]].reshape(SLOTS // 2, 128)
    out[...] = dot_tn(owner_pick(near), keep[...]) + dot_tn(owner_pick(far), got[...])


def owner_sum(core, asked, keep, got):
    whole = pl.BlockSpec(memory_space=pltpu.VMEM)
    return pl.pallas_call(
        owner_kernel,
        in_specs=[pl.BlockSpec(memory_space=pltpu.SMEM)] + [whole] * 3,
        out_specs=whole,
        out_shape=jax.ShapeDtypeStruct((N, DM), F32),
        compiler_params=pltpu.CompilerParams(vmem_limit_bytes=16 << 20),
        cost_estimate=pl.CostEstimate(
            flops=2 * N * DM * SLOTS, bytes_accessed=1 << 20, transcendentals=0
        ),
        name="owner_sum",
    )(core, asked.reshape(PLANE, CORES, CAP, 128), keep, got)


def exchange(rows, axes, count):
    blocks = rows.reshape(count, -1, rows.shape[-1])
    return lax.all_to_all(blocks, axes, split_axis=0, concat_axis=0, tiled=True).reshape(rows.shape)


def plane(x):
    return lax.all_to_all(x, FLAT, split_axis=0, concat_axis=0, tiled=True)


def on_device(
    memory_base,
    messages,
    touched,
    gru_input,
    gru_state,
    attn_weights,
    frequency,
    request_rows,
    event_slots,
    delays,
    upstream,
):
    seg = lax.axis_index("y").reshape(1)
    core = lax.axis_index("core").reshape(1)
    swap = [(0, 1), (1, 0)]
    ids = request_rows.reshape(1, SLOTS)
    written = gru(touched, memory_base, messages[0], gru_input, gru_state)
    r1 = lax.ppermute(written, "y", [(0, 1), (1, 2), (2, 3)])
    r2 = lax.ppermute(written, "y", [(0, 2), (1, 3)])
    r3 = lax.ppermute(written, "y", [(0, 3)])
    written, late, seg, core = lax.optimization_barrier((written, delays[0].T, seg, core))
    chosen_t = event_slots.transpose(2, 0, 1)
    code_t, time_kv, chosen, wanted = time_parts(
        ids, late, frequency.reshape(1, DM), attn_weights, chosen_t
    )
    written, wanted, code_t, time_kv, chosen = lax.optimization_barrier(
        (written, wanted, code_t, time_kv, chosen)
    )
    asked = exchange(wanted, NODE, OWNERS)
    memory, rows = start_rows(seg, memory_base, written, r1, r2, r3, asked)
    slots = exchange(rows, NODE, OWNERS)
    up = upstream[0]
    mine, other, *kept = attend(
        core, slots, chosen, chosen_t, time_kv, code_t, up, attn_weights
    )
    partner = lax.ppermute(other, "core", swap)
    embedded, keep, give = events(core, *kept, up, attn_weights)
    got = lax.ppermute(give, "core", swap)
    part, near, far = plane_sum(plane(pair_sum(mine, partner, keep, got)))
    turns = {s: [(i, (i + s) % SEG) for i in range(SEG)] for s in (1, 2, 3)}
    r2 = lax.ppermute(part, "y", turns[2])
    memory_grad = owner_sum(core, asked, near, far)
    late, memory_grad = lax.optimization_barrier((part, memory_grad))
    r1, r3 = (lax.ppermute(late, "y", turns[s]) for s in (1, 3))
    half = plane(seg_sum(seg, part, r1, r2, r3))
    far = lax.ppermute(half, "core", swap)
    weight_grad = whole_grad(core, far, whole_grad(core, half))
    return embedded[None], memory[None], memory_grad[None], weight_grad.reshape(4, DM, DM)


def solution(mesh):
    fine = Mesh(mesh.devices.reshape(SEG, X, Z, CORES), ("y", "x", "z", "core"))
    both = P("y", NODE, None)
    in_specs = (P(NODE, None), both, P("y", NODE), P(), P(), P(), P(), both, both, both, both)
    out_specs = (both, both, both, P())
    return jax.shard_map(
        on_device, mesh=fine, in_specs=in_specs, out_specs=out_specs, check_vma=False
    )
```

```python
import functools
import math

import jax
import jax.numpy as jnp
from jax import lax
from jax.experimental import pallas as pl
from jax.experimental.pallas import tpu as pltpu
from jax.sharding import Mesh
from jax.sharding import PartitionSpec as P

SEG, X, Z, CORES = 4, 4, 4, 2
OWNERS = X * Z * CORES
PLANE = X * Z
DM = 512
HEADS = 2
HEAD = DM // HEADS
K = 8
E = 256
N = 256
CAP = 8
SLOTS = 256
PIECE = 64
TILE = 128
TILES = E // TILE
ROWS = K * TILE
STEP = 32
ABSENT = 2.0
NODE = ("x", "z", "core")
FLAT = ("x", "z")
BF = jnp.bfloat16
F32 = jnp.float32

COS = (
    0.9999992107823232,
    -19.738980355764145,
    64.92865742103731,
    -85.27162153434116,
    58.79049212030933,
    -21.07110562791079,
)


def dot(a, b):
    return jnp.dot(a, b, preferred_element_type=F32)


def dot_tn(a, b):
    return lax.dot_general(a, b, (((0,), (0,)), ((), ())), preferred_element_type=F32)


def dot_nt(a, b):
    return lax.dot_general(a, b, (((1,), (1,)), ((), ())), preferred_element_type=F32)


def iota(shape, axis):
    return lax.broadcasted_iota(jnp.int32, shape, axis)


def column(row):
    n = row.shape[1]
    square = jnp.where(iota((n, n), 0) == iota((n, n), 1), row.astype(F32), 0.0)
    return jnp.sum(square, axis=1, keepdims=True)


def gru_kernel(touched, state, message, w_input, w_state, out, st, ms, wi, ws, sem):
    moves = ((state, st), (w_state, ws), (message, ms), (w_input, wi))
    copies = [pltpu.make_async_copy(a, b, sem.at[i]) for i, (a, b) in enumerate(moves)]
    for i, copy in enumerate(copies):
        copy.start(priority=i % 2)
    keep = column(touched[...]) > 0.5
    copies[0].wait()
    copies[1].wait()
    s = st[...]
    from_state = [dot(s, ws[:, i * DM : (i + 1) * DM]) for i in range(3)]
    copies[2].wait()
    copies[3].wait()
    m = ms[...]
    update = jax.nn.sigmoid(dot(m, wi[:, :DM]) + from_state[0])
    reset = jax.nn.sigmoid(dot(m, wi[:, DM : 2 * DM]) + from_state[1])
    candidate = jnp.tanh(dot(m, wi[:, 2 * DM :]) + reset * from_state[2])
    fresh = (1.0 - update) * candidate + update * s.astype(F32)
    out[...] = jnp.where(keep, fresh, ABSENT).astype(BF)


def gru(touched, state, message, w_input, w_state):
    whole = pl.BlockSpec(memory_space=pltpu.VMEM)
    far = pl.BlockSpec(memory_space=pl.ANY)
    return pl.pallas_call(
        gru_kernel,
        in_specs=[whole] + [far] * 4,
        out_specs=whole,
        out_shape=jax.ShapeDtypeStruct((N, DM), BF),
        scratch_shapes=[
            pltpu.VMEM((N, DM), BF),
            pltpu.VMEM((N, DM), BF),
            pltpu.VMEM((DM, 3 * DM), BF),
            pltpu.VMEM((DM, 3 * DM), BF),
            pltpu.SemaphoreType.DMA((4,)),
        ],
        compiler_params=pltpu.CompilerParams(vmem_limit_bytes=56 << 20),
        cost_estimate=pl.CostEstimate(
            flops=4 * N * DM * 3 * DM, bytes_accessed=4 << 20, transcendentals=3 * N * DM
        ),
        name="gru",
    )(touched, state, message, w_input, w_state)


def time_kernel(ids, delays, frequency, w, chosen, code_t, time_kv, picked, wanted, code):
    wanted[...] = jnp.broadcast_to(column(ids[...]), (SLOTS, 128)).astype(jnp.int32)
    lane = iota((E, 128), 1)
    columns = jnp.zeros((E, 128), F32)
    for j in range(K + 1):
        columns = jnp.where(lane == j, column(chosen[j]), columns)
    picked[...] = columns.astype(jnp.int32)
    turns = frequency[...] * (1.0 / (2.0 * math.pi))
    for tile in range(TILES):
        for k in range(K):
            delay = column(delays[k : k + 1, tile * TILE : (tile + 1) * TILE])
            angle = delay * turns
            part = angle - jnp.round(angle)
            u = part * part
            wave = jnp.full_like(u, COS[-1])
            for c in COS[-2::-1]:
                wave = wave * u + c
            at = slice(k * TILE, (k + 1) * TILE)
            wave = wave.astype(BF)
            code_t[tile, :, at] = wave.T
            code[tile, at] = wave
        for i in range(2):
            time_kv[tile, :, i * DM : (i + 1) * DM] = dot(code[tile], w[1 + i]).astype(BF)


def time_parts(ids, delays, frequency, weights, chosen):
    whole = pl.BlockSpec(memory_space=pltpu.VMEM)
    return pl.pallas_call(
        time_kernel,
        in_specs=[whole] * 5,
        out_specs=[whole] * 4,
        out_shape=[
            jax.ShapeDtypeStruct((TILES, DM, ROWS), BF),
            jax.ShapeDtypeStruct((TILES, ROWS, 2 * DM), BF),
            jax.ShapeDtypeStruct((E, 128), jnp.int32),
            jax.ShapeDtypeStruct((SLOTS, 128), jnp.int32),
        ],
        scratch_shapes=[pltpu.VMEM((TILES, ROWS, DM), BF)],
        compiler_params=pltpu.CompilerParams(vmem_limit_bytes=24 << 20),
        cost_estimate=pl.CostEstimate(
            flops=4 * K * E * DM * DM, bytes_accessed=8 << 20, transcendentals=K * E * DM
        ),
        name="time_parts",
    )(ids, delays, frequency, weights, chosen)


def owner_pick(asked):
    ids = jnp.concatenate([asked] * (N // 128), axis=1)
    return (ids == iota(ids.shape, 1)).astype(F32).astype(BF)


def start_kernel(seg, state, written, r1, r2, r3, asked, memory, rows):
    start = state[...]
    for back, r in ((3, r3), (2, r2), (1, r1)):
        row = r[...]
        start = jnp.where((row.astype(F32) < 1.5) & (seg[0] >= back), row, start)
    own = written[...]
    memory[...] = jnp.where(own.astype(F32) < 1.5, own, start)
    rows[...] = dot(owner_pick(asked[...]), start).astype(BF)


def start_rows(seg, state, written, r1, r2, r3, asked):
    whole = pl.BlockSpec(memory_space=pltpu.VMEM)
    return pl.pallas_call(
        start_kernel,
        in_specs=[pl.BlockSpec(memory_space=pltpu.SMEM)] + [whole] * 6,
        out_specs=[whole] * 2,
        out_shape=[
            jax.ShapeDtypeStruct((N, DM), BF),
            jax.ShapeDtypeStruct((SLOTS, DM), BF),
        ],
        compiler_params=pltpu.CompilerParams(vmem_limit_bytes=16 << 20),
        cost_estimate=pl.CostEstimate(
            flops=2 * N * DM * SLOTS, bytes_accessed=2 << 20, transcendentals=0
        ),
        name="start_rows",
    )(seg, state, written, r1, r2, r3, asked)


def attend_kernel(
    core, slots, chosen, chosen_t, tkv, tt, up, wq,
    mine, other, att, src, pick_t, s_qkv,
    skv, d_att, qf, both, dkv, dq,
):
    rows = slots[...]
    pick = (chosen[:, 0:1] == iota((E, SLOTS), 1)).astype(F32).astype(BF)
    src[...] = dot(pick, rows).astype(BF)
    skv[:, :DM] = dot(rows, wq[1]).astype(BF)
    skv[:, DM:] = dot(rows, wq[2]).astype(BF)
    qf[...] = dot(pick, dot(rows, wq[0]).astype(BF))
    d_att[...] = dot_nt(up[...], wq[3])

    lane = iota((STEP, 128), 1)
    lane_a = lane < K
    lane_b = (lane >= K) & (lane < 2 * K)
    scale = 1.0 / math.sqrt(HEAD)

    def per_head(x):
        a = jnp.sum(jnp.where(lane_a, x, 0.0), axis=1, keepdims=True)
        b = jnp.sum(jnp.where(lane_b, x, 0.0), axis=1, keepdims=True)
        return jnp.where(lane_a, a, b)

    def gather(i):
        ids = chosen[i * TILE : (i + 1) * TILE, :]
        slot = iota((TILE, SLOTS), 1)
        pick = jnp.concatenate(
            [(ids[:, 1 + k : 2 + k] == slot).astype(F32) for k in range(K)], axis=0
        ).astype(BF)
        both[i] = dot(pick, skv[...])

    def step(i, j):
        at = slice(i * TILE + j * STEP, i * TILE + (j + 1) * STEP)
        scores = jnp.zeros((STEP, 128), F32)
        d_probs = jnp.zeros((STEP, 128), F32)
        for h in range(HEADS):
            part = slice(h * HEAD, (h + 1) * HEAD)
            part_v = slice(DM + h * HEAD, DM + (h + 1) * HEAD)
            query = qf[at, part]
            d_out = d_att[at, part]
            for k in range(K):
                row = slice(k * TILE + j * STEP, k * TILE + (j + 1) * STEP)
                key = both[i, row, part] + tkv[i, row, part].astype(F32)
                value = both[i, row, part_v] + tkv[i, row, part_v].astype(F32)
                both[i, row, part] = key
                both[i, row, part_v] = value
                here = lane == h * K + k
                scores = jnp.where(here, jnp.sum(query * key, axis=1, keepdims=True), scores)
                d_probs = jnp.where(here, jnp.sum(d_out * value, axis=1, keepdims=True), d_probs)
        powered = jnp.exp(scores * scale)
        probs = powered / per_head(powered)
        d_scores = probs * (d_probs - per_head(probs * d_probs)) * scale
        for h in range(HEADS):
            part = slice(h * HEAD, (h + 1) * HEAD)
            part_v = slice(DM + h * HEAD, DM + (h + 1) * HEAD)
            query = qf[at, part]
            d_out = d_att[at, part]
            attended = jnp.zeros((STEP, HEAD), F32)
            d_query = jnp.zeros((STEP, HEAD), F32)
            for k in range(K):
                row = slice(k * TILE + j * STEP, k * TILE + (j + 1) * STEP)
                c = h * K + k
                p = jnp.broadcast_to(probs[:, c : c + 1], (STEP, HEAD))
                d = jnp.broadcast_to(d_scores[:, c : c + 1], (STEP, HEAD))
                attended += p * both[i, row, part_v]
                d_query += d * both[i, row, part]
                dkv[i, row, part] = (d * query).astype(BF)
                dkv[i, row, part_v] = (p * d_out).astype(BF)
            att[at, part] = attended.astype(BF)
            dq[at, part] = d_query.astype(BF)

    for i in range(TILES):
        gather(i)
    sub = iota((SLOTS, TILE), 0)
    s_kv = dot_t = None
    for i in range(TILES):
        for j in range(TILE // STEP):
            step(i, j)
        spread = jnp.concatenate(
            [
                (sub == chosen_t[1 + k, :, i * TILE : (i + 1) * TILE]).astype(F32)
                for k in range(K)
            ],
            axis=1,
        ).astype(BF)
        sums = dot(jnp.concatenate([tt[i], spread], axis=0), dkv[i])
        one, two = sums[DM:], sums[:DM]
        s_kv = one if i == 0 else s_kv + one
        dot_t = two if i == 0 else dot_t + two
    s_kv = s_kv.astype(BF)
    pick_t[...] = (iota((SLOTS, E), 0) == chosen_t[0]).astype(F32).astype(BF)
    s_q = dot(pick_t[...], dq[...]).astype(BF)
    s_qkv[:, :DM] = s_q
    s_qkv[:, DM:] = s_kv
    first = core[0] == 0

    def store(i, value):
        blocks = value.reshape(4, CORES, PIECE, DM)
        at = slice(i * 4, (i + 1) * 4)
        mine[at] = jnp.where(first, blocks[:, 0], blocks[:, 1]).astype(BF)
        other[at] = jnp.where(first, blocks[:, 1], blocks[:, 0]).astype(BF)

    store(0, dot_tn(rows, s_q))
    g_kv = dot_t + dot_tn(rows, s_kv)
    store(1, g_kv[:, :DM])
    store(2, g_kv[:, DM:])
    store(3, dot_tn(att[...], up[...]))


def events_kernel(core, att, src, pick_t, s_qkv, up, w, embedded, keep, give):
    embedded[...] = (dot(att[...], w[3]) + src[...].astype(F32)).astype(BF)
    grads = dot(pick_t[...], up[...])
    for i in range(3):
        grads += dot_nt(s_qkv[:, i * DM : (i + 1) * DM], w[i])
    blocks = grads.reshape(PLANE, CORES, CAP, DM)
    first = core[0] == 0
    low, high = (blocks[:, i].reshape(SLOTS // 2, DM) for i in range(2))
    keep[...] = jnp.where(first, low, high).astype(BF)
    give[...] = jnp.where(first, high, low).astype(BF)


def events(core, att, src, pick_t, s_qkv, up, weights):
    whole = pl.BlockSpec(memory_space=pltpu.VMEM)
    return pl.pallas_call(
        events_kernel,
        in_specs=[pl.BlockSpec(memory_space=pltpu.SMEM)] + [whole] * 6,
        out_specs=[whole] * 3,
        out_shape=[jax.ShapeDtypeStruct((E, DM), BF)]
        + [jax.ShapeDtypeStruct((SLOTS // 2, DM), BF)] * 2,
        compiler_params=pltpu.CompilerParams(vmem_limit_bytes=16 << 20),
        cost_estimate=pl.CostEstimate(flops=1 << 29, bytes_accessed=4 << 20, transcendentals=0),
        name="events",
    )(core, att, src, pick_t, s_qkv, up, weights)


def attend(core, slots, chosen, chosen_t, time_kv, code_t, up, weights):
    whole = pl.BlockSpec(memory_space=pltpu.VMEM)
    return pl.pallas_call(
        attend_kernel,
        in_specs=[pl.BlockSpec(memory_space=pltpu.SMEM)] + [whole] * 7,
        out_specs=[whole] * 6,
        out_shape=[
            jax.ShapeDtypeStruct((PLANE, PIECE, DM), BF),
            jax.ShapeDtypeStruct((PLANE, PIECE, DM), BF),
            jax.ShapeDtypeStruct((E, DM), BF),
            jax.ShapeDtypeStruct((E, DM), BF),
            jax.ShapeDtypeStruct((SLOTS, E), BF),
            jax.ShapeDtypeStruct((SLOTS, 3 * DM), BF),
        ],
        scratch_shapes=[
            pltpu.VMEM((SLOTS, 2 * DM), BF),
            pltpu.VMEM((E, DM), F32),
            pltpu.VMEM((E, DM), F32),
            pltpu.VMEM((TILES, ROWS, 2 * DM), F32),
            pltpu.VMEM((TILES, ROWS, 2 * DM), BF),
            pltpu.VMEM((E, DM), BF),
        ],
        compiler_params=pltpu.CompilerParams(vmem_limit_bytes=40 << 20),
        cost_estimate=pl.CostEstimate(
            flops=6 << 30, bytes_accessed=14 << 20, transcendentals=E * 128
        ),
        name="attend",
    )(core, slots, chosen, chosen_t, time_kv, code_t, up, weights)


def pair_kernel(a, b, keep, got, out):
    out[:, :PIECE] = (a[...].astype(F32) + b[...].astype(F32)).astype(BF)
    near, far = (x[...].astype(F32).reshape(4, CAP, DM) for x in (keep, got))
    out[:, PIECE:] = jnp.concatenate([near, far], axis=1).astype(BF)


def pair_sum(a, b, keep, got):
    spec = pl.BlockSpec((4, PIECE, DM), lambda i: (i, 0, 0))
    rows = pl.BlockSpec((4 * CAP, DM), lambda i: (i, 0))
    return pl.pallas_call(
        pair_kernel,
        grid=(PLANE // 4,),
        in_specs=[spec, spec, rows, rows],
        out_specs=pl.BlockSpec((4, PIECE + 2 * CAP, DM), lambda i: (i, 0, 0)),
        out_shape=jax.ShapeDtypeStruct((PLANE, PIECE + 2 * CAP, DM), BF),
        compiler_params=pltpu.CompilerParams(vmem_limit_bytes=16 << 20),
        cost_estimate=pl.CostEstimate(flops=1 << 19, bytes_accessed=3 << 20, transcendentals=0),
        name="pair_sum",
    )(a, b, keep, got)


def plane_kernel(a, part, near, far):
    total = a[0, :PIECE].astype(F32)
    for i in range(1, PLANE):
        total += a[i, :PIECE].astype(F32)
    part[...] = total.astype(BF)
    grads = a[:, PIECE:].astype(F32)
    near[...] = grads[:, :CAP].reshape(SLOTS // 2, DM).astype(BF)
    far[...] = grads[:, CAP:].reshape(SLOTS // 2, DM).astype(BF)


def plane_sum(a):
    whole = pl.BlockSpec(memory_space=pltpu.VMEM)
    half = jax.ShapeDtypeStruct((SLOTS // 2, DM), BF)
    return pl.pallas_call(
        plane_kernel,
        in_specs=[whole],
        out_specs=[whole] * 3,
        out_shape=[jax.ShapeDtypeStruct((PIECE, DM), BF), half, half],
        compiler_params=pltpu.CompilerParams(vmem_limit_bytes=16 << 20),
        cost_estimate=pl.CostEstimate(flops=1 << 19, bytes_accessed=2 << 20, transcendentals=0),
        name="plane_sum",
    )(a)


def seg_kernel(seg, own, r1, r2, r3, out, parts):
    for back, r in enumerate((own, r1, r2, r3)):
        parts[lax.rem(seg[0] + SEG - back, SEG)] = r[...].astype(F32)
    total = ((parts[0] + parts[1]) + (parts[2] + parts[3])).astype(BF)
    for i in range(PLANE):
        out[i] = total


def seg_sum(seg, own, r1, r2, r3):
    whole = pl.BlockSpec(memory_space=pltpu.VMEM)
    return pl.pallas_call(
        seg_kernel,
        in_specs=[pl.BlockSpec(memory_space=pltpu.SMEM)] + [whole] * 4,
        out_specs=whole,
        out_shape=jax.ShapeDtypeStruct((PLANE, PIECE, DM), BF),
        scratch_shapes=[pltpu.VMEM((SEG, PIECE, DM), F32)],
        compiler_params=pltpu.CompilerParams(vmem_limit_bytes=16 << 20),
        cost_estimate=pl.CostEstimate(flops=1 << 17, bytes_accessed=1 << 20, transcendentals=0),
        name="seg_sum",
    )(seg, own, r1, r2, r3)


def half_kernel(own, core, half, *rest):
    out, wide, sem = rest[-3:]
    place = core[0] if own else 1 - core[0]
    copies = []
    for i in range(4):
        at = pl.ds(i * PLANE // 4, PLANE // 4)
        wide[at] = half[at].astype(F32)
        copies.append(pltpu.make_async_copy(wide.at[at], out.at[at, place], sem.at[i]))
        copies[-1].start(priority=i % 2)
    for copy in copies:
        copy.wait()


def whole_grad(core, half, before=None):
    own = before is None
    far = pl.BlockSpec(memory_space=pl.ANY)
    return pl.pallas_call(
        functools.partial(half_kernel, own),
        in_specs=[pl.BlockSpec(memory_space=pltpu.SMEM), pl.BlockSpec(memory_space=pltpu.VMEM)]
        + ([] if own else [far]),
        out_specs=far,
        out_shape=jax.ShapeDtypeStruct((PLANE, CORES, PIECE, DM), F32),
        scratch_shapes=[pltpu.VMEM((PLANE, PIECE, DM), F32), pltpu.SemaphoreType.DMA((4,))],
        input_output_aliases={} if own else {2: 0},
        compiler_params=pltpu.CompilerParams(vmem_limit_bytes=16 << 20),
        cost_estimate=pl.CostEstimate(flops=1 << 18, bytes_accessed=3 << 20, transcendentals=0),
        name="own_half" if own else "far_half",
    )(core, half, *([] if own else [before]))


def owner_kernel(core, asked, keep, got, out):
    near = asked[:, core[0]].reshape(SLOTS // 2, 128)
    far = asked[:, 1 - core[0]].reshape(SLOTS // 2, 128)
    out[...] = dot_tn(owner_pick(near), keep[...]) + dot_tn(owner_pick(far), got[...])


def owner_sum(core, asked, keep, got):
    whole = pl.BlockSpec(memory_space=pltpu.VMEM)
    return pl.pallas_call(
        owner_kernel,
        in_specs=[pl.BlockSpec(memory_space=pltpu.SMEM)] + [whole] * 3,
        out_specs=whole,
        out_shape=jax.ShapeDtypeStruct((N, DM), F32),
        compiler_params=pltpu.CompilerParams(vmem_limit_bytes=16 << 20),
        cost_estimate=pl.CostEstimate(
            flops=2 * N * DM * SLOTS, bytes_accessed=1 << 20, transcendentals=0
        ),
        name="owner_sum",
    )(core, asked.reshape(PLANE, CORES, CAP, 128), keep, got)


def exchange(rows, axes, count):
    blocks = rows.reshape(count, -1, rows.shape[-1])
    return lax.all_to_all(blocks, axes, split_axis=0, concat_axis=0, tiled=True).reshape(rows.shape)


def plane(x):
    return lax.all_to_all(x, FLAT, split_axis=0, concat_axis=0, tiled=True)


def on_device(
    memory_base,
    messages,
    touched,
    gru_input,
    gru_state,
    attn_weights,
    frequency,
    request_rows,
    event_slots,
    delays,
    upstream,
):
    seg = lax.axis_index("y").reshape(1)
    core = lax.axis_index("core").reshape(1)
    swap = [(0, 1), (1, 0)]
    ids = request_rows.reshape(1, SLOTS)
    written = gru(touched, memory_base, messages[0], gru_input, gru_state)
    r1 = lax.ppermute(written, "y", [(0, 1), (1, 2), (2, 3)])
    r2 = lax.ppermute(written, "y", [(0, 2), (1, 3)])
    r3 = lax.ppermute(written, "y", [(0, 3)])
    written, late, seg, core = lax.optimization_barrier((written, delays[0].T, seg, core))
    chosen_t = event_slots.transpose(2, 0, 1)
    code_t, time_kv, chosen, wanted = time_parts(
        ids, late, frequency.reshape(1, DM), attn_weights, chosen_t
    )
    written, wanted, code_t, time_kv, chosen = lax.optimization_barrier(
        (written, wanted, code_t, time_kv, chosen)
    )
    asked = exchange(wanted, NODE, OWNERS)
    memory, rows = start_rows(seg, memory_base, written, r1, r2, r3, asked)
    slots = exchange(rows, NODE, OWNERS)
    up = upstream[0]
    mine, other, *kept = attend(
        core, slots, chosen, chosen_t, time_kv, code_t, up, attn_weights
    )
    partner = lax.ppermute(other, "core", swap)
    embedded, keep, give = events(core, *kept, up, attn_weights)
    got = lax.ppermute(give, "core", swap)
    part, near, far = plane_sum(plane(pair_sum(mine, partner, keep, got)))
    r2, r3, r1 = (
        lax.ppermute(part, "y", [(i, (i + s) % SEG) for i in range(SEG)]) for s in (2, 3, 1)
    )
    half = plane(seg_sum(seg, part, r1, r2, r3))
    memory_grad = owner_sum(core, asked, near, far)
    far = lax.ppermute(half, "core", swap)
    weight_grad = whole_grad(core, far, whole_grad(core, half))
    return embedded[None], memory[None], memory_grad[None], weight_grad.reshape(4, DM, DM)


def solution(mesh):
    fine = Mesh(mesh.devices.reshape(SEG, X, Z, CORES), ("y", "x", "z", "core"))
    both = P("y", NODE, None)
    in_specs = (P(NODE, None), both, P("y", NODE), P(), P(), P(), P(), both, both, both, both)
    out_specs = (both, both, both, P())
    return jax.shard_map(
        on_device, mesh=fine, in_specs=in_specs, out_specs=out_specs, check_vma=False
    )
```
